512 devices in a mesh: dom: 512 (over x, y, z, core).
Axes of the slice: x: 4, y: 8, z: 8, core: 2. Of those that a mesh axis runs over, the one named last changes fastest.
Arguments:
- positions: float32 [32768, 3, 128], P('dom'), may hold values from -2 to 2, as said below
- moments: float32 [32768, 3, 128], P('dom'), may hold values from -1 to 1
- fwd_cells: int32 [512, 9, 64], P('dom'), may hold values from 0 to 583, as said below
- fwd_leaves: int32 [512, 9, 20], P('dom'), may hold values from 0 to 223, as said below
- fwd_counts: int32 [512, 9, 2], P('dom'), may hold values from 5 to 64, as said below
- cell_list: int32 [32768, 64], P('dom'), may hold values from 0 to 647, as said below
- cell_len: int32 [32768], P('dom'), may hold values from 1 to 64, as said below
- leaf_list: int32 [32768, 8], P('dom'), may hold values from 0 to 243, as said below
- leaf_len: int32 [32768], P('dom'), may hold values from 1 to 8, as said below
Outputs:
- field: float32 [32768, 3, 128], P('dom')
The draws below stay inside these ranges and needn't reach their ends.
Inputs may be any that keep to these rules, and one draw needn't show every extreme that they name: `fwd_cells`: section b entries are slots that already exist in the sender's pool before section b: below 72 + b * 64. `fwd_leaves`: section b entries lie below 64 + b * 20. `fwd_counts`: column 0 counts cells, from 64 // 4 (at least 1) to 64; column 1 counts leaf blocks, from 20 // 4 (at least 1) to 20; every domain sends a full buffer of both at some section. `cell_list`: slots of the final cell pool; some may be empty (zero) slots. `cell_len`: every domain has a leaf with exactly 64 entries; a domain's mean length may be up to three times another's. `leaf_list`: entry 0 of a leaf's list is the leaf itself and entry 1 one of the 8 leaves under its parent cell; the other entries are slots of the final leaf pool, some of which may be empty (zero) slots. `leaf_len`: every domain has a leaf with exactly 8 entries; a domain's mean length may be up to three times another's. `positions`: each leaf's particles scatter around a centre of their own; the centres of a domain's leaves fill a compact region of space.
All inputs are finite; a program needn't handle non-finite values.
Results may differ from the reference program's by a relative error of at most 0.0003.
Values sent between devices are 32-bit elements; how exact they have to be, the bound alone decides.
A program may use at most 128 MiB of HBM per device.

```python
import jax
import jax.numpy as jnp
from jax import lax

LEAF_SIZE = 128
LEAVES = 64
CELL_SENDS = 64
LEAF_SENDS = 20
CELL_SLOTS = 64
LEAF_SLOTS = 8
OWN_CELLS = 72
SECTIONS = 9
LEAF_POOL = 244
CELL_POOL = 648
N_DOM = 512


def draw_positions(key, part):
    key = jax.random.fold_in(key, 12)
    rows = N_DOM * LEAVES
    bits = (rows - 1).bit_length()
    levels = (bits + 2) // 3
    side = 2 ** levels
    index = jnp.arange(rows, dtype=jnp.int32)
    coords = []
    for axis in range(3):
        coord = jnp.zeros((rows,), jnp.int32)
        for level in range(levels):
            bit = jnp.bitwise_and(jnp.right_shift(index, 3 * level + axis), 1)
            coord = coord + jnp.left_shift(bit, level)
        coords.append(coord.astype(jnp.float32))
    step = 4.0 / side
    key_c, key_p = jax.random.split(key)
    jitter = jax.random.uniform(key_c, (rows, 3), jnp.float32, -0.05, 0.05) * step
    center = -2.0 + (jnp.stack(coords, axis=1) + 0.5) * step + jitter
    shape = (rows, 3, LEAF_SIZE)
    offset = jnp.clip(0.5 * jax.random.normal(key_p, shape, jnp.float32), -1.0, 1.0)
    return jnp.clip(center[:, :, None] + offset, -2.0, 2.0)


def draw_moments(key, part):
    key = jax.random.fold_in(key, 11)
    rows = N_DOM * LEAVES
    shape = (rows, 3, LEAF_SIZE)
    place = (jnp.arange(rows, dtype=jnp.int32) // LEAVES).astype(jnp.float32) / (N_DOM - 1)
    noise = 0.02 * jnp.clip(jax.random.normal(key, shape, jnp.float32), -4.0, 4.0)
    ramp = 1.0 + 2.0 * place
    lead = jnp.array([0.0, 0.0, 1.0], jnp.float32)
    return noise + 0.02 * ramp[:, None, None] * lead[None, :, None]


def forward_slots(key, first, sends):
    limit = first + jnp.arange(SECTIONS, dtype=jnp.int32) * sends
    picks = jax.random.randint(key, (N_DOM, SECTIONS, sends), 0, limit[None, :, None])
    slot = jnp.arange(sends, dtype=jnp.int32)[None, None, :]
    section = jnp.arange(SECTIONS, dtype=jnp.int32)[None, :, None]
    picks = jnp.where((section == SECTIONS - 1) & (slot == 0), limit[None, :, None] - 1, picks)
    return jnp.where((section == SECTIONS - 1) & (slot == 1), 0, picks)


def draw_fwd_cells(key, part):
    key = jax.random.fold_in(key, 1)
    return forward_slots(key, OWN_CELLS, CELL_SENDS)


def draw_fwd_leaves(key, part):
    key = jax.random.fold_in(key, 2)
    return forward_slots(key, LEAVES, LEAF_SENDS)


def live_counts(key, sends):
    low = max(1, sends // 4)
    counts = jax.random.randint(key, (N_DOM, SECTIONS), low, sends + 1)
    dom = jnp.arange(N_DOM, dtype=jnp.int32)[:, None]
    section = jnp.arange(SECTIONS, dtype=jnp.int32)[None, :]
    counts = jnp.where(section == dom % SECTIONS, sends, counts)
    return jnp.where(section == (dom + 1) % SECTIONS, low, counts)


def draw_fwd_counts(key, part):
    key = jax.random.fold_in(key, 3)
    key_c, key_l = jax.random.split(key)
    return jnp.stack([live_counts(key_c, CELL_SENDS), live_counts(key_l, LEAF_SENDS)], axis=2)


def ragged_lengths(key, most):
    key_w, key_l, key_p = jax.random.split(key, 3)
    weight = jax.random.randint(key_w, (N_DOM, 1), 1, 4)
    top = jnp.maximum(1, most * weight // 3)
    lengths = jax.random.randint(key_l, (N_DOM, LEAVES), 1, top + 1)
    pick = jax.random.randint(key_p, (N_DOM, 1), 0, LEAVES)
    lengths = jnp.where(jnp.arange(LEAVES, dtype=jnp.int32)[None, :] == pick, most, lengths)
    return lengths.reshape(N_DOM * LEAVES)


def draw_cell_len(key, part):
    key = jax.random.fold_in(key, 4)
    return ragged_lengths(key, CELL_SLOTS)


def draw_leaf_len(key, part):
    key = jax.random.fold_in(key, 5)
    return ragged_lengths(key, LEAF_SLOTS)


def draw_cell_list(key, part):
    key = jax.random.fold_in(key, 6)
    picks = jax.random.randint(key, (N_DOM * LEAVES, CELL_SLOTS), 0, CELL_POOL)
    return picks.at[0, 0].set(CELL_POOL - 1).at[0, 1].set(0)


def draw_leaf_list(key, part):
    key = jax.random.fold_in(key, 7)
    key_r, key_s = jax.random.split(key)
    rows = N_DOM * LEAVES
    picks = jax.random.randint(key_r, (rows, LEAF_SLOTS), 0, LEAF_POOL)
    local = jnp.arange(rows, dtype=jnp.int32) % LEAVES
    sibling = local // 8 * 8 + jax.random.randint(key_s, (rows,), 0, 8)
    picks = picks.at[:, 0].set(local).at[:, 1].set(sibling)
    return picks.at[0, 2].set(LEAF_POOL - 1)


def setup_inputs(seed: int = 0) -> dict:
    keys = jax.random.split(jax.random.key(seed), 10)
    positions = draw_positions(jax.random.fold_in(keys[9], 71), 0)
    moments = draw_moments(jax.random.fold_in(keys[9], 71), 0)
    fwd_cells = draw_fwd_cells(jax.random.fold_in(keys[9], 71), 0)
    fwd_leaves = draw_fwd_leaves(jax.random.fold_in(keys[9], 71), 0)
    fwd_counts = draw_fwd_counts(jax.random.fold_in(keys[9], 71), 0)
    cell_list = draw_cell_list(jax.random.fold_in(keys[9], 71), 0)
    cell_len = draw_cell_len(jax.random.fold_in(keys[9], 71), 0)
    leaf_list = draw_leaf_list(jax.random.fold_in(keys[9], 71), 0)
    leaf_len = draw_leaf_len(jax.random.fold_in(keys[9], 71), 0)
    return {"positions": positions, "moments": moments, "fwd_cells": fwd_cells, "fwd_leaves": fwd_leaves, "fwd_counts": fwd_counts, "cell_list": cell_list, "cell_len": cell_len, "leaf_list": leaf_list, "leaf_len": leaf_len}


SOFT = 1.0
DEMAG = 4.1887902047863905
BLOCK = 16

def leaf_cells(pos, mom):
    center = lax.optimization_barrier(jnp.mean(pos, axis=2))
    offset = pos - center[:, :, None]
    total = lax.optimization_barrier(jnp.sum(mom, axis=2))
    second = lax.optimization_barrier(jnp.sum(offset[:, :, None, :] * mom[:, None, :, :], axis=3))
    return (center, total, second)

def parent_cells(center, total, second):
    kids_c = center.reshape(-1, 8, 3)
    kids_t = total.reshape(-1, 8, 3)
    kids_s = second.reshape(-1, 8, 3, 3)
    pc = lax.optimization_barrier(jnp.mean(kids_c, axis=1))
    pt = lax.optimization_barrier(jnp.sum(kids_t, axis=1))
    shift = kids_c - pc[:, None, :]
    ps = lax.optimization_barrier(jnp.sum(kids_s + shift[:, :, :, None] * kids_t[:, :, None, :], axis=1))
    return (pc, pt, ps)

def pack_rows(center, total, second):
    return jnp.concatenate([center, total, second.reshape(-1, 9)], axis=1)

def pair_field(targets, block):
    src = block[:, 0:3]
    mom = block[:, 3:6]
    sep = targets[:, :, :, None] - src[:, :, None, :]
    quad = lax.optimization_barrier(jnp.sum(sep * sep, axis=1)) + SOFT
    inv = lax.rsqrt(quad)
    inv3 = inv * inv * inv
    inv5 = inv3 / quad
    along = lax.optimization_barrier(jnp.sum(mom[:, :, None, :] * sep, axis=1))
    term = 3.0 * sep * (along * inv5)[:, None] - mom[:, :, None, :] * inv3[:, None]
    return lax.optimization_barrier(jnp.sum(term, axis=3))

def cell_field(targets, cells):
    center = cells[0:3][..., None]
    total = cells[3:6][..., None]
    second = cells[6:15].reshape((3, 3) + cells.shape[1:])[..., None]
    sep = jnp.transpose(targets, (1, 0, 2))[:, :, None, :] - center
    quad = lax.optimization_barrier(jnp.sum(sep * sep, axis=0)) + SOFT
    inv = lax.rsqrt(quad)
    inv3 = inv * inv * inv
    inv5 = inv3 / quad
    inv7 = inv5 / quad
    along = lax.optimization_barrier(jnp.sum(total * sep, axis=0))
    qsep = lax.optimization_barrier(jnp.sum(second * sep[None], axis=1))
    qtsep = lax.optimization_barrier(jnp.sum(second * sep[:, None], axis=0))
    trace = second[0, 0] + second[1, 1] + second[2, 2]
    rqr = lax.optimization_barrier(jnp.sum(sep * qsep, axis=0))
    return 3.0 * sep * (along * inv5) - total * inv3 - 3.0 * inv5 * (qsep + sep * trace + qtsep) + 15.0 * inv7 * sep * rqr

def reference(positions, moments, fwd_cells, fwd_leaves, fwd_counts, cell_list, cell_len, leaf_list, leaf_len):
    blocks_all = jnp.concatenate([positions, moments], axis=1)
    center, total, second = leaf_cells(positions, moments)
    pc, pt, ps = parent_cells(center, total, second)
    leaf_rows = pack_rows(center, total, second).reshape(N_DOM, LEAVES, 15)
    parent_rows = pack_rows(pc, pt, ps).reshape(N_DOM, LEAVES // 8, 15)
    cell_table = jnp.concatenate([leaf_rows, parent_rows], axis=1).reshape(N_DOM * OWN_CELLS, 15)
    dom_ids = jnp.arange(N_DOM, dtype=jnp.int32)
    own_leaf = dom_ids[:, None] * LEAVES + jnp.arange(LEAVES, dtype=jnp.int32)[None, :]
    own_cell = dom_ids[:, None] * OWN_CELLS + jnp.arange(OWN_CELLS, dtype=jnp.int32)[None, :]
    leaf_prov = jnp.concatenate([own_leaf, jnp.full((N_DOM, SECTIONS * LEAF_SENDS), -1, jnp.int32)], axis=1)
    cell_prov = jnp.concatenate([own_cell, jnp.full((N_DOM, SECTIONS * CELL_SENDS), -1, jnp.int32)], axis=1)
    for section in range(SECTIONS):
        partner = jnp.bitwise_xor(dom_ids, 1 << section)
        picked_l = jnp.take_along_axis(leaf_prov[partner], fwd_leaves[partner, section], axis=1)
        live_l = jnp.arange(LEAF_SENDS, dtype=jnp.int32)[None, :] < fwd_counts[partner, section, 1][:, None]
        picked_l = jnp.where(live_l, picked_l, -1)
        picked_c = jnp.take_along_axis(cell_prov[partner], fwd_cells[partner, section], axis=1)
        live_c = jnp.arange(CELL_SENDS, dtype=jnp.int32)[None, :] < fwd_counts[partner, section, 0][:, None]
        picked_c = jnp.where(live_c, picked_c, -1)
        start_l = LEAVES + section * LEAF_SENDS
        start_c = OWN_CELLS + section * CELL_SENDS
        leaf_prov = leaf_prov.at[:, start_l:start_l + LEAF_SENDS].set(picked_l)
        cell_prov = cell_prov.at[:, start_c:start_c + CELL_SENDS].set(picked_c)
    leaf_ids = jnp.take_along_axis(leaf_prov, leaf_list.reshape(N_DOM, LEAVES * LEAF_SLOTS), axis=1)
    leaf_ids = leaf_ids.reshape(N_DOM, LEAVES, LEAF_SLOTS)
    cell_ids = jnp.take_along_axis(cell_prov, cell_list.reshape(N_DOM, LEAVES * CELL_SLOTS), axis=1)
    cell_ids = cell_ids.reshape(N_DOM, LEAVES, CELL_SLOTS)

    def one_domain(items):
        targets, lids, llen, cids, clen = items

        def leaf_step(k, acc):
            ids = lids[:, k]
            blk = jnp.where((ids >= 0)[:, None, None], blocks_all[jnp.maximum(ids, 0)], 0.0)
            return acc + jnp.where((k < llen)[:, None, None], pair_field(targets, blk), 0.0)
        acc = lax.fori_loop(0, LEAF_SLOTS, leaf_step, jnp.zeros(targets.shape, targets.dtype))

        def cell_step(j, acc):
            ids = lax.dynamic_slice_in_dim(cids, j * BLOCK, BLOCK, 1)
            rows = jnp.where((ids >= 0)[:, :, None], cell_table[jnp.maximum(ids, 0)], 0.0)
            part = cell_field(targets, jnp.transpose(rows, (2, 0, 1)))
            slot = j * BLOCK + jnp.arange(BLOCK, dtype=jnp.int32)
            keep = slot[None, :] < clen[:, None]
            summed = lax.optimization_barrier(jnp.sum(jnp.where(keep[None, :, :, None], part, 0.0), axis=2))
            return acc + jnp.transpose(summed, (1, 0, 2))
        return lax.fori_loop(0, CELL_SLOTS // BLOCK, cell_step, acc)
    field = lax.map(one_domain, (positions.reshape(N_DOM, LEAVES, 3, LEAF_SIZE), leaf_ids, leaf_len.reshape(N_DOM, LEAVES), cell_ids, cell_len.reshape(N_DOM, LEAVES)))
    uniform = -DEMAG * lax.optimization_barrier(jnp.sum(moments, axis=(0, 2))) / (N_DOM * LEAVES)
    return (field + uniform[None, None, :, None]).reshape(N_DOM * LEAVES, 3, LEAF_SIZE)
```

```python
import functools

import jax
import jax.numpy as jnp
from jax import lax
from jax.experimental import pallas as pl
from jax.experimental.pallas import tpu as pltpu
from jax.sharding import PartitionSpec as P

F32 = jnp.float32
BF16 = jnp.bfloat16
DEMAG = 4.1887902047863905
LEAVES = 64
PARENTS = 8
OWN = LEAVES + PARENTS
SECTIONS = 9
CELL_SENDS = 64
LEAF_SENDS = 20
LEAF_POOL = LEAVES + SECTIONS * LEAF_SENDS
CELL_POOL = OWN + SECTIONS * CELL_SENDS
LANES = 128
N_DOM = 512
NEAR_UNROLL = 4
FAR_UNROLL = 4


def iota(shape, dim):
    return lax.broadcasted_iota(jnp.int32, shape, dim)


def pieces(x):
    first = x.astype(BF16).astype(F32)
    rest = x - first
    second = rest.astype(BF16).astype(F32)
    return first, second, rest - second


def far_rows(tile):
    row = lambda k, j: tile[6 + 3 * k + j : 7 + 3 * k + j]
    return jnp.concatenate(
        [
            tile[0:6],
            2.0 * row(0, 0),
            2.0 * row(1, 1),
            2.0 * row(2, 2),
            row(0, 1) + row(1, 0),
            row(0, 2) + row(2, 0),
            row(1, 2) + row(2, 1),
            row(0, 0) + row(1, 1) + row(2, 2),
            jnp.zeros((3, LANES), F32),
        ],
        axis=0,
    )


def own_tile(pos_ref, mom_ref):
    pos = [pos_ref[:, k, :] for k in range(3)]
    mom = [mom_ref[:, k, :] for k in range(3)]
    cen = [jnp.sum(p, axis=1, keepdims=True) * (1.0 / LANES) for p in pos]
    tot = [jnp.sum(m, axis=1, keepdims=True) for m in mom]
    off = [pos[k] - cen[k] for k in range(3)]
    sec = [
        [jnp.sum(off[k] * mom[j], axis=1, keepdims=True) for j in range(3)] for k in range(3)
    ]
    full = lambda x: jnp.broadcast_to(x, (LEAVES, LANES)).reshape(PARENTS, 8, LANES)
    fcen = [full(c) for c in cen]
    ftot = [full(c) for c in tot]
    fsec = [[full(sec[k][j]) for j in range(3)] for k in range(3)]
    pcen = [jnp.sum(c, axis=1, keepdims=True) * 0.125 for c in fcen]
    ptot = [jnp.sum(c, axis=1) for c in ftot]
    psec = [
        [jnp.sum(fsec[k][j] + (fcen[k] - pcen[k]) * ftot[j], axis=1) for j in range(3)]
        for k in range(3)
    ]
    leaf = fcen + ftot + [fsec[k][j] for k in range(3) for j in range(3)]
    up = [c[:, 0, :] for c in pcen] + ptot + [psec[k][j] for k in range(3) for j in range(3)]
    lane = iota((LEAVES, LANES), 1)
    lane_p = iota((PARENTS, LANES), 1)
    rows = jnp.zeros((LEAVES, LANES), F32)
    rows_p = jnp.zeros((PARENTS, LANES), F32)
    for i in range(15):
        rows = jnp.where(lane == i, leaf[i].reshape(LEAVES, LANES), rows)
        rows_p = jnp.where(lane_p == i, up[i], rows_p)
    every = jnp.concatenate([rows, rows_p, jnp.zeros((LANES - OWN, LANES), F32)], axis=0)
    sums = [jnp.sum(p, axis=0, keepdims=True) for p in ptot]
    return jnp.transpose(every)[0:16], sums


def exchange_kernel(
    pos_ref, mom_ref, fl_ref, fn_ref, fc_ref,
    pool_ref, cells_ref, unif_ref,
    split, index, send_l, recv_l, send_c, recv_c, sl_sem, rl_sem, sc_sem, rc_sem,
):
    me = lax.axis_index("dom")
    partners = []
    for b in range(SECTIONS):
        stride = 1 << b
        partners.append(me + (1 - 2 * lax.rem(me // stride, 2)) * stride)
    barrier = pltpu.get_barrier_semaphore()
    for other in partners:
        pl.semaphore_signal(
            barrier, inc=1, device_id=(other,), device_id_type=pl.DeviceIdType.MESH
        )
    pool_ref[0:LEAVES, 0:3, :] = pos_ref[...]
    pool_ref[0:LEAVES, 3:6, :] = mom_ref[...]

    lane16 = iota((16, LANES), 1)
    lane = iota((8, LANES), 1)
    sub = iota((8, LANES), 0)
    index[...] = jnp.full((16, LANES), -1, jnp.int32)
    index[0:SECTIONS, 0:CELL_SENDS] = fc_ref[0]
    raw = index[...]
    past = raw - OWN
    index[...] = jnp.where(
        raw < OWN, raw, LANES + (past // CELL_SENDS) * LANES + lax.rem(past, CELL_SENDS)
    )
    pl.semaphore_wait(barrier, SECTIONS)

    def leaf_copy(b):
        return pltpu.make_async_remote_copy(
            src_ref=send_l.at[b], dst_ref=recv_l.at[b],
            send_sem=sl_sem.at[b], recv_sem=rl_sem.at[b],
            device_id=(partners[b],), device_id_type=pl.DeviceIdType.MESH,
        )

    def cell_copy(b):
        return pltpu.make_async_remote_copy(
            src_ref=send_c.at[b], dst_ref=recv_c.at[b],
            send_sem=sc_sem.at[b], recv_sem=rc_sem.at[b],
            device_id=(partners[b],), device_id_type=pl.DeviceIdType.MESH,
        )

    def send_leaves(b):
        live = fn_ref[0, b, 1]
        for s in range(LEAF_SENDS):
            block = pool_ref[fl_ref[0, b, s]][0:6]
            send_l[b, 6 * s : 6 * s + 6, :] = jnp.where(s < live, block, 0.0)
        leaf_copy(b).start()

    def take_tile(tile, t):
        for i, part in enumerate(pieces(tile)):
            split[16 * i : 16 * i + 16, LANES * t : LANES * t + LANES] = part.astype(BF16)

    def send_cells(b, msum):
        depth = (b + 1) * LANES
        wanted = jnp.where(lane[0:1] < fn_ref[0, b, 0], index[b : b + 1, :], -1)
        hot = jnp.where(iota((depth, LANES), 0) == wanted, 1.0, 0.0).astype(BF16)
        got = jnp.dot(split[:, 0:depth], hot, preferred_element_type=F32)
        got = (got[0:16] + got[16:32]) + got[32:48]
        low = jnp.where(sub == 7, msum, got[8:16])
        send_c[b] = jnp.where(lane < CELL_SENDS, got[0:8], pltpu.roll(low, CELL_SENDS, 1))
        cell_copy(b).start()

    def finish_leaves(first, count):
        part = [pool_ref[first : first + count, i, :] for i in range(6)]
        pool_ref[first : first + count, 6, :] = (
            part[0] * part[0] + part[1] * part[1] + part[2] * part[2]
        )
        pool_ref[first : first + count, 7, :] = (
            part[0] * part[3] + part[1] * part[4] + part[2] * part[5]
        )

    def finish_cells(tile, first, count):
        turned = jnp.transpose(
            jnp.concatenate([far_rows(tile), jnp.zeros((LANES - 16, LANES), F32)], axis=0)
        )
        cells_ref[first : first + count, :] = turned[0:count]

    send_leaves(0)
    tile, sums = own_tile(pos_ref, mom_ref)
    msum = jnp.zeros((8, LANES), F32)
    for j in range(3):
        msum = jnp.where((sub == 7) & (lane == j), sums[j], msum)
    take_tile(tile, 0)
    send_cells(0, msum)
    finish_leaves(0, LEAVES)
    finish_cells(tile, 0, OWN)
    for b in range(SECTIONS):
        first = LEAVES + b * LEAF_SENDS
        leaf_copy(b).wait_recv()
        for s in range(LEAF_SENDS):
            pool_ref[first + s, 0:6, :] = recv_l[b, 6 * s : 6 * s + 6, :]
        if b + 1 < SECTIONS:
            send_leaves(b + 1)
        cell_copy(b).wait_recv()
        got = recv_c[b]
        low = jnp.where(lane < CELL_SENDS, pltpu.roll(got, CELL_SENDS, 1), 0.0)
        high = jnp.where(lane < CELL_SENDS, got, 0.0)
        tile = jnp.concatenate([high, low], axis=0)
        msum = msum + jnp.where(sub == 7, low, 0.0)
        if b + 1 < SECTIONS:
            take_tile(tile, b + 1)
            send_cells(b + 1, msum)
        finish_leaves(first, LEAF_SENDS)
        finish_cells(tile, OWN + b * CELL_SENDS, CELL_SENDS)
    scaled = msum * (-DEMAG / (N_DOM * LEAVES))
    unif_ref[...] = jnp.concatenate(
        [jnp.broadcast_to(scaled[7:8, j : j + 1], (1, LANES)) for j in range(3)]
        + [jnp.zeros((5, LANES), F32)],
        axis=0,
    )
    for b in range(SECTIONS):
        leaf_copy(b).wait_send()
        cell_copy(b).wait_send()


def exchange(positions, moments, fwd_leaves, fwd_counts, fwd_cells):
    vmem = pl.BlockSpec(memory_space=pltpu.VMEM)
    smem = pl.BlockSpec(memory_space=pltpu.SMEM)
    dma = pltpu.SemaphoreType.DMA((SECTIONS,))
    return pl.pallas_call(
        exchange_kernel,
        out_shape=(
            jax.ShapeDtypeStruct((LEAF_POOL, 8, LANES), F32),
            jax.ShapeDtypeStruct((CELL_POOL, LANES), F32),
            jax.ShapeDtypeStruct((8, LANES), F32),
        ),
        in_specs=[vmem, vmem, smem, smem, vmem],
        out_specs=(vmem, vmem, vmem),
        scratch_shapes=[
            pltpu.VMEM((48, (SECTIONS + 1) * LANES), BF16),
            pltpu.VMEM((16, LANES), jnp.int32),
            pltpu.VMEM((SECTIONS, 6 * LEAF_SENDS, LANES), F32),
            pltpu.VMEM((SECTIONS, 6 * LEAF_SENDS, LANES), F32),
            pltpu.VMEM((SECTIONS, 8, LANES), F32),
            pltpu.VMEM((SECTIONS, 8, LANES), F32),
            dma, dma, dma, dma,
        ],
        compiler_params=pltpu.CompilerParams(
            collective_id=0, has_side_effects=True, vmem_limit_bytes=40 * 1024 * 1024
        ),
        name="exchange",
    )(positions, moments, fwd_leaves, fwd_counts, fwd_cells)


def target_side(block, sub):
    cut = pieces(block)
    zero = jnp.zeros((8, LANES), F32)
    order = (0, 1, 2, 0, 1, 0)
    lead = (True, False, False, True, False, True)
    quad, along = [], []
    for p, flag in zip(order, lead):
        mark = 1.0 if flag else 0.0
        quad.append(jnp.where(sub < 3, -2.0 * cut[p], jnp.where(sub == 6, mark, 0.0)))
        turned = pltpu.roll(cut[p], 3, 0)
        along.append(
            jnp.where((sub >= 3) & (sub < 6), turned, jnp.where(sub == 7, -mark, 0.0))
        )
    quad.append(
        jnp.where(sub == 6, cut[0], jnp.where(sub == 7, pltpu.roll(cut[1], 1, 0), 0.0))
    )
    quad.append(jnp.where(sub == 6, cut[2], jnp.where(sub == 7, 1.0, 0.0)))
    along += [zero, zero]
    side = jnp.concatenate(
        [
            jnp.transpose(jnp.concatenate(quad, axis=0)),
            jnp.transpose(jnp.concatenate(along, axis=0)),
        ],
        axis=0,
    )
    return side.astype(BF16)


def near_item(side, block, sub):
    cut = pieces(block)
    source = jnp.concatenate(
        [cut[0], cut[0], cut[0], cut[1], cut[1], cut[2], jnp.ones((16, LANES), F32)], axis=0
    ).astype(BF16)
    both = jnp.dot(side, source, preferred_element_type=F32)
    inv = lax.rsqrt(both[0:LANES])
    inv2 = inv * inv
    inv3 = inv2 * inv
    coef = both[LANES:] * (inv3 * inv2)
    weights = jnp.concatenate([coef, inv3], axis=1)
    high = weights.astype(BF16)
    low = (weights - high.astype(F32)).astype(BF16)

    def sums(part, one):
        c_side = jnp.where(sub < 3, part, jnp.where(sub == 6, one, 0.0))
        w_side = jnp.where((sub >= 3) & (sub < 6), part, 0.0)
        return jnp.concatenate([c_side, w_side], axis=1)

    left = jnp.concatenate([sums(cut[0], 1.0), sums(cut[1], 0.0)], axis=0).astype(BF16)
    dims = (((1,), (1,)), ((), ()))
    got = lax.dot_general(left, high, dims, preferred_element_type=F32)
    got = got + lax.dot_general(left, low, dims, preferred_element_type=F32)
    return got[0:8] + got[8:16]


def far_item(x, rows):
    col = lambda p: jnp.broadcast_to(rows[:, p : p + 1], (8, LANES))
    sep = [x[d] - col(d) for d in range(3)]
    tot = [col(3 + d) for d in range(3)]
    xx, yy, zz, xy, xz, yz, trace = [col(6 + i) for i in range(7)]
    quad = sep[0] * sep[0] + sep[1] * sep[1] + sep[2] * sep[2] + 1.0
    inv = lax.rsqrt(quad)
    inv2 = inv * inv
    inv3 = inv2 * inv
    inv5 = 3.0 * (inv3 * inv2)
    inv7 = 2.5 * (inv5 * inv2)
    along = tot[0] * sep[0] + tot[1] * sep[1] + tot[2] * sep[2] - trace
    turn = [
        xx * sep[0] + xy * sep[1] + xz * sep[2],
        xy * sep[0] + yy * sep[1] + yz * sep[2],
        xz * sep[0] + yz * sep[1] + zz * sep[2],
    ]
    bend = sep[0] * turn[0] + sep[1] * turn[1] + sep[2] * turn[2]
    coef = along * inv5 + bend * inv7
    return [sep[d] * coef - tot[d] * inv3 - turn[d] * inv5 for d in range(3)]


def field_kernel(
    pool_ref, cells_ref, unif_ref, clist_ref, clen_ref, llist_ref, llen_ref,
    out_ref, sides, near, far,
):
    sub = iota((8, LANES), 0)

    def prepare(t, carry):
        sides[t] = target_side(pool_ref[t], sub)
        near[t] = jnp.zeros((8, LANES), F32)
        far[t] = jnp.zeros((3, 8, LANES), F32)
        return carry

    lax.fori_loop(0, LEAVES, prepare, 0)
    near[LEAVES] = jnp.zeros((8, LANES), F32)
    far[LEAVES] = jnp.zeros((3, 8, LANES), F32)

    def step(t, k, most):
        more = k + 1 < most
        return jnp.where(more, t, t + 1), jnp.where(more, k + 1, 0)

    def near_body(at):
        t, k = at
        todo = []
        for _ in range(NEAR_UNROLL):
            row = jnp.minimum(t, LEAVES - 1)
            todo.append((jnp.minimum(t, LEAVES), row, llist_ref[row, k]))
            t, k = step(t, k, llen_ref[row])
        parts = [near_item(sides[row], pool_ref[src], sub) for _, row, src in todo]
        for (slot, _, _), part in zip(todo, parts):
            near[slot] += part
        return t, k

    lax.while_loop(lambda at: at[0] < LEAVES, near_body, (jnp.int32(0), jnp.int32(0)))

    def far_body(at):
        t, k = at
        todo = []
        for _ in range(FAR_UNROLL):
            row = jnp.minimum(t, LEAVES - 1)
            most = clen_ref[row]
            todo.append((jnp.minimum(t, LEAVES), row, k, most))
            t, k = step(t, k, (most + 7) // 8)
        parts = []
        for _, row, group, most in todo:
            rows = jnp.concatenate(
                [cells_ref[pl.ds(clist_ref[row, 8 * group + i], 1), :] for i in range(8)], axis=0
            )
            rows = jnp.where(8 * group + sub < most, rows, 0.0)
            block = pool_ref[row]
            x = [jnp.broadcast_to(block[d : d + 1], (8, LANES)) for d in range(3)]
            parts.append(far_item(x, rows))
        for (slot, _, _, _), part in zip(todo, parts):
            for d in range(3):
                far[slot, d] += part[d]
        return t, k

    lax.while_loop(lambda at: at[0] < LEAVES, far_body, (jnp.int32(0), jnp.int32(0)))

    unif = unif_ref[0:3]

    def finish(t, carry):
        got = near[t]
        x = pool_ref[t][0:3]
        close = 3.0 * (x * got[6:7] - got[0:3]) - got[3:6]
        out_ref[t] = close + jnp.sum(far[t], axis=1) + unif
        return carry

    lax.fori_loop(0, LEAVES, finish, 0)


def field(pool, cells, unif, cell_list, cell_len, leaf_list, leaf_len):
    vmem = pl.BlockSpec(memory_space=pltpu.VMEM)
    smem = pl.BlockSpec(memory_space=pltpu.SMEM)
    return pl.pallas_call(
        field_kernel,
        out_shape=jax.ShapeDtypeStruct((LEAVES, 3, LANES), F32),
        in_specs=[vmem, vmem, vmem, smem, smem, smem, smem],
        out_specs=vmem,
        scratch_shapes=[
            pltpu.VMEM((LEAVES, 2 * LANES, 64), BF16),
            pltpu.VMEM((LEAVES + 1, 8, LANES), F32),
            pltpu.VMEM((LEAVES + 1, 3, 8, LANES), F32),
        ],
        compiler_params=pltpu.CompilerParams(vmem_limit_bytes=40 * 1024 * 1024),
        name="field",
    )(pool, cells, unif, cell_list, cell_len, leaf_list, leaf_len)


def per_device(
    positions, moments, fwd_cells, fwd_leaves, fwd_counts, cell_list, cell_len, leaf_list, leaf_len
):
    pool, cells, unif = exchange(positions, moments, fwd_leaves, fwd_counts, fwd_cells)
    return field(pool, cells, unif, cell_list, cell_len, leaf_list, leaf_len)


def solution(mesh):
    row = P("dom", None)
    cube = P("dom", None, None)
    return jax.shard_map(
        per_device,
        mesh=mesh,
        in_specs=(cube, cube, cube, cube, cube, row, P("dom"), row, P("dom")),
        out_specs=cube,
        check_vma=False,
    )
```

```python
import functools

import jax
import jax.numpy as jnp
from jax import lax
from jax.experimental import pallas as pl
from jax.experimental.pallas import tpu as pltpu
from jax.sharding import PartitionSpec as P

F32 = jnp.float32
BF16 = jnp.bfloat16
DEMAG = 4.1887902047863905
LEAVES = 64
PARENTS = 8
OWN = LEAVES + PARENTS
SECTIONS = 9
CELL_SENDS = 64
LEAF_SENDS = 20
LEAF_POOL = LEAVES + SECTIONS * LEAF_SENDS
CELL_POOL = OWN + SECTIONS * CELL_SENDS
LANES = 128
N_DOM = 512
NEAR_UNROLL = 4
FAR_UNROLL = 8


def iota(shape, dim):
    return lax.broadcasted_iota(jnp.int32, shape, dim)


def pieces(x):
    first = x.astype(BF16).astype(F32)
    rest = x - first
    second = rest.astype(BF16).astype(F32)
    return first, second, rest - second


def far_rows(tile):
    row = lambda k, j: tile[6 + 3 * k + j : 7 + 3 * k + j]
    return jnp.concatenate(
        [
            tile[0:6],
            2.0 * row(0, 0),
            2.0 * row(1, 1),
            2.0 * row(2, 2),
            row(0, 1) + row(1, 0),
            row(0, 2) + row(2, 0),
            row(1, 2) + row(2, 1),
            row(0, 0) + row(1, 1) + row(2, 2),
            jnp.zeros((3, LANES), F32),
        ],
        axis=0,
    )


def own_tile(pos_ref, mom_ref):
    pos = [pos_ref[:, k, :] for k in range(3)]
    mom = [mom_ref[:, k, :] for k in range(3)]
    cen = [jnp.sum(p, axis=1, keepdims=True) * (1.0 / LANES) for p in pos]
    tot = [jnp.sum(m, axis=1, keepdims=True) for m in mom]
    off = [pos[k] - cen[k] for k in range(3)]
    sec = [
        [jnp.sum(off[k] * mom[j], axis=1, keepdims=True) for j in range(3)] for k in range(3)
    ]
    full = lambda x: jnp.broadcast_to(x, (LEAVES, LANES)).reshape(PARENTS, 8, LANES)
    fcen = [full(c) for c in cen]
    ftot = [full(c) for c in tot]
    fsec = [[full(sec[k][j]) for j in range(3)] for k in range(3)]
    pcen = [jnp.sum(c, axis=1, keepdims=True) * 0.125 for c in fcen]
    ptot = [jnp.sum(c, axis=1) for c in ftot]
    psec = [
        [jnp.sum(fsec[k][j] + (fcen[k] - pcen[k]) * ftot[j], axis=1) for j in range(3)]
        for k in range(3)
    ]
    leaf = fcen + ftot + [fsec[k][j] for k in range(3) for j in range(3)]
    up = [c[:, 0, :] for c in pcen] + ptot + [psec[k][j] for k in range(3) for j in range(3)]
    lane = iota((LEAVES, LANES), 1)
    lane_p = iota((PARENTS, LANES), 1)
    rows = jnp.zeros((LEAVES, LANES), F32)
    rows_p = jnp.zeros((PARENTS, LANES), F32)
    for i in range(15):
        rows = jnp.where(lane == i, leaf[i].reshape(LEAVES, LANES), rows)
        rows_p = jnp.where(lane_p == i, up[i], rows_p)
    every = jnp.concatenate([rows, rows_p, jnp.zeros((LANES - OWN, LANES), F32)], axis=0)
    sums = [jnp.sum(p, axis=0, keepdims=True) for p in ptot]
    return jnp.transpose(every)[0:16], sums


def exchange_kernel(
    pos_ref, mom_ref, fl_ref, fn_ref, fc_ref,
    pool_ref, cells_ref, unif_ref,
    split, index, send_l, recv_l, send_c, recv_c, sl_sem, rl_sem, sc_sem, rc_sem,
):
    me = lax.axis_index("dom")
    partners = []
    for b in range(SECTIONS):
        stride = 1 << b
        partners.append(me + (1 - 2 * lax.rem(me // stride, 2)) * stride)
    barrier = pltpu.get_barrier_semaphore()
    for other in partners:
        pl.semaphore_signal(
            barrier, inc=1, device_id=(other,), device_id_type=pl.DeviceIdType.MESH
        )
    pool_ref[0:LEAVES, 0:3, :] = pos_ref[...]
    pool_ref[0:LEAVES, 3:6, :] = mom_ref[...]

    lane16 = iota((16, LANES), 1)
    lane = iota((8, LANES), 1)
    sub = iota((8, LANES), 0)
    index[...] = jnp.full((16, LANES), -1, jnp.int32)
    index[0:SECTIONS, 0:CELL_SENDS] = fc_ref[0]
    raw = index[...]
    past = raw - OWN
    index[...] = jnp.where(
        raw < OWN, raw, LANES + (past // CELL_SENDS) * LANES + lax.rem(past, CELL_SENDS)
    )
    pl.semaphore_wait(barrier, SECTIONS)

    def leaf_copy(b):
        return pltpu.make_async_remote_copy(
            src_ref=send_l.at[b], dst_ref=recv_l.at[b],
            send_sem=sl_sem.at[b], recv_sem=rl_sem.at[b],
            device_id=(partners[b],), device_id_type=pl.DeviceIdType.MESH,
        )

    def cell_copy(b):
        return pltpu.make_async_remote_copy(
            src_ref=send_c.at[b], dst_ref=recv_c.at[b],
            send_sem=sc_sem.at[b], recv_sem=rc_sem.at[b],
            device_id=(partners[b],), device_id_type=pl.DeviceIdType.MESH,
        )

    def send_leaves(b):
        live = fn_ref[0, b, 1]
        for s in range(LEAF_SENDS):
            block = pool_ref[fl_ref[0, b, s]][0:6]
            send_l[b, 6 * s : 6 * s + 6, :] = jnp.where(s < live, block, 0.0)
        leaf_copy(b).start()

    def take_tile(tile, t):
        for i, part in enumerate(pieces(tile)):
            split[16 * i : 16 * i + 16, LANES * t : LANES * t + LANES] = part.astype(BF16)

    def send_cells(b, msum):
        depth = (b + 1) * LANES
        wanted = jnp.where(lane[0:1] < fn_ref[0, b, 0], index[b : b + 1, :], -1)
        hot = jnp.where(iota((depth, LANES), 0) == wanted, 1.0, 0.0).astype(BF16)
        got = jnp.dot(split[:, 0:depth], hot, preferred_element_type=F32)
        got = (got[0:16] + got[16:32]) + got[32:48]
        low = jnp.where(sub == 7, msum, got[8:16])
        send_c[b] = jnp.where(lane < CELL_SENDS, got[0:8], pltpu.roll(low, CELL_SENDS, 1))
        cell_copy(b).start()

    def finish_leaves(first, count):
        part = [pool_ref[first : first + count, i, :] for i in range(6)]
        pool_ref[first : first + count, 6, :] = (
            part[0] * part[0] + part[1] * part[1] + part[2] * part[2]
        )
        pool_ref[first : first + count, 7, :] = (
            part[0] * part[3] + part[1] * part[4] + part[2] * part[5]
        )

    def finish_cells(tile, first, count):
        turned = jnp.transpose(
            jnp.concatenate([far_rows(tile), jnp.zeros((LANES - 16, LANES), F32)], axis=0)
        )
        cells_ref[first : first + count, :] = turned[0:count]

    send_leaves(0)
    tile, sums = own_tile(pos_ref, mom_ref)
    msum = jnp.zeros((8, LANES), F32)
    for j in range(3):
        msum = jnp.where((sub == 7) & (lane == j), sums[j], msum)
    take_tile(tile, 0)
    send_cells(0, msum)
    finish_leaves(0, LEAVES)
    finish_cells(tile, 0, OWN)
    for b in range(SECTIONS):
        first = LEAVES + b * LEAF_SENDS
        leaf_copy(b).wait_recv()
        for s in range(LEAF_SENDS):
            pool_ref[first + s, 0:6, :] = recv_l[b, 6 * s : 6 * s + 6, :]
        if b + 1 < SECTIONS:
            send_leaves(b + 1)
        cell_copy(b).wait_recv()
        got = recv_c[b]
        low = jnp.where(lane < CELL_SENDS, pltpu.roll(got, CELL_SENDS, 1), 0.0)
        high = jnp.where(lane < CELL_SENDS, got, 0.0)
        tile = jnp.concatenate([high, low], axis=0)
        msum = msum + jnp.where(sub == 7, low, 0.0)
        if b + 1 < SECTIONS:
            take_tile(tile, b + 1)
            send_cells(b + 1, msum)
        finish_leaves(first, LEAF_SENDS)
        finish_cells(tile, OWN + b * CELL_SENDS, CELL_SENDS)
    scaled = msum * (-DEMAG / (N_DOM * LEAVES))
    unif_ref[...] = jnp.concatenate(
        [jnp.broadcast_to(scaled[7:8, j : j + 1], (1, LANES)) for j in range(3)]
        + [jnp.zeros((5, LANES), F32)],
        axis=0,
    )
    for b in range(SECTIONS):
        leaf_copy(b).wait_send()
        cell_copy(b).wait_send()


def exchange(positions, moments, fwd_leaves, fwd_counts, fwd_cells):
    vmem = pl.BlockSpec(memory_space=pltpu.VMEM)
    smem = pl.BlockSpec(memory_space=pltpu.SMEM)
    dma = pltpu.SemaphoreType.DMA((SECTIONS,))
    return pl.pallas_call(
        exchange_kernel,
        out_shape=(
            jax.ShapeDtypeStruct((LEAF_POOL, 8, LANES), F32),
            jax.ShapeDtypeStruct((CELL_POOL, LANES), F32),
            jax.ShapeDtypeStruct((8, LANES), F32),
        ),
        in_specs=[vmem, vmem, smem, smem, vmem],
        out_specs=(vmem, vmem, vmem),
        scratch_shapes=[
            pltpu.VMEM((48, (SECTIONS + 1) * LANES), BF16),
            pltpu.VMEM((16, LANES), jnp.int32),
            pltpu.VMEM((SECTIONS, 6 * LEAF_SENDS, LANES), F32),
            pltpu.VMEM((SECTIONS, 6 * LEAF_SENDS, LANES), F32),
            pltpu.VMEM((SECTIONS, 8, LANES), F32),
            pltpu.VMEM((SECTIONS, 8, LANES), F32),
            dma, dma, dma, dma,
        ],
        compiler_params=pltpu.CompilerParams(
            collective_id=0, has_side_effects=True, vmem_limit_bytes=40 * 1024 * 1024
        ),
        name="exchange",
    )(positions, moments, fwd_leaves, fwd_counts, fwd_cells)


def target_side(block, sub):
    cut = pieces(block)
    zero = jnp.zeros((16, LANES), F32)
    order = (0, 1, 2, 0, 1, 0)
    lead = (True, False, False, True, False, True)
    quad, along = [], []
    for p, flag in zip(order, lead):
        mark = 1.0 if flag else 0.0
        quad.append(jnp.where(sub < 3, -2.0 * cut[p], jnp.where(sub == 6, mark, 0.0)))
        turned = pltpu.roll(cut[p], 3, 0)
        along.append(
            jnp.where((sub >= 3) & (sub < 6), turned, jnp.where(sub == 7, -mark, 0.0))
        )
    quad.append(
        jnp.where(sub == 6, cut[0], jnp.where(sub == 7, pltpu.roll(cut[1], 1, 0), 0.0))
    )
    quad.append(jnp.where(sub == 6, cut[2], jnp.where(sub == 7, 1.0, 0.0)))
    along.append(zero)
    return jnp.concatenate(
        [jnp.concatenate(quad, axis=0), jnp.concatenate(along, axis=0)], axis=1
    ).astype(BF16)


def near_product(side, block):
    cut = pieces(block)
    source = jnp.concatenate(
        [cut[0], cut[0], cut[0], cut[1], cut[1], cut[2], jnp.ones((16, LANES), F32)], axis=0
    ).astype(BF16)
    return lax.dot_general(
        source, side, (((0,), (0,)), ((), ())), preferred_element_type=F32
    )


def near_sums(both, block, sub):
    parts = [[], [], [], []]
    for c in range(LANES // 16):
        quad = both[16 * c : 16 * c + 16, 0:LANES]
        along = both[16 * c : 16 * c + 16, LANES:]
        inv = lax.rsqrt(quad)
        inv2 = inv * inv
        inv3 = inv2 * inv
        coef = along * (inv3 * inv2)
        for i, weight in enumerate((coef, inv3)):
            high = weight.astype(BF16)
            parts[i].append(high)
            parts[2 + i].append((weight - high.astype(F32)).astype(BF16))
    high = jnp.concatenate(parts[0] + parts[1], axis=0)
    low = jnp.concatenate(parts[2] + parts[3], axis=0)

    def sums(part, one):
        c_side = jnp.where(sub < 3, part, jnp.where(sub == 6, one, 0.0))
        w_side = jnp.where((sub >= 3) & (sub < 6), part, 0.0)
        return jnp.concatenate([c_side, w_side], axis=1)

    cut = pieces(block)
    left = jnp.concatenate([sums(cut[0], 1.0), sums(cut[1], 0.0)], axis=0).astype(BF16)
    got = jnp.dot(left, high, preferred_element_type=F32)
    more = jnp.dot(left, low, preferred_element_type=F32)
    return (got[0:8] + got[8:16]) + more[0:8]


def far_item(x, rows):
    col = lambda p: jnp.broadcast_to(rows[:, p : p + 1], (8, LANES))
    sep = [x[d] - col(d) for d in range(3)]
    tot = [col(3 + d) for d in range(3)]
    xx, yy, zz, xy, xz, yz, trace = [col(6 + i) for i in range(7)]
    quad = sep[0] * sep[0] + sep[1] * sep[1] + sep[2] * sep[2] + 1.0
    inv = lax.rsqrt(quad)
    inv2 = inv * inv
    inv3 = inv2 * inv
    inv5 = 3.0 * (inv3 * inv2)
    inv7 = 2.5 * (inv5 * inv2)
    along = tot[0] * sep[0] + tot[1] * sep[1] + tot[2] * sep[2] - trace
    turn = [
        xx * sep[0] + xy * sep[1] + xz * sep[2],
        xy * sep[0] + yy * sep[1] + yz * sep[2],
        xz * sep[0] + yz * sep[1] + zz * sep[2],
    ]
    bend = sep[0] * turn[0] + sep[1] * turn[1] + sep[2] * turn[2]
    coef = along * inv5 + bend * inv7
    return [sep[d] * coef - tot[d] * inv3 - turn[d] * inv5 for d in range(3)]


def field_kernel(
    pool_ref, cells_ref, unif_ref, clist_ref, clen_ref, llist_ref, llen_ref,
    out_ref, sides, near, far, buf_a, buf_b,
):
    sub = iota((8, LANES), 0)

    def prepare(t, carry):
        sides[t] = target_side(pool_ref[t], sub)
        near[t] = jnp.zeros((8, LANES), F32)
        far[t] = jnp.zeros((3, 8, LANES), F32)
        return carry

    lax.fori_loop(0, LEAVES, prepare, 0)
    near[LEAVES] = jnp.zeros((8, LANES), F32)
    far[LEAVES] = jnp.zeros((3, 8, LANES), F32)

    def step(t, k, most):
        more = k + 1 < most
        return jnp.where(more, t, t + 1), jnp.where(more, k + 1, 0)

    def near_items(at):
        t, k = at
        todo = []
        for _ in range(NEAR_UNROLL):
            row = jnp.minimum(t, LEAVES - 1)
            todo += [jnp.minimum(t, LEAVES), llist_ref[row, k]]
            t, k = step(t, k, llen_ref[row])
        return (t, k), tuple(todo)

    def near_first(todo, buf):
        for i in range(NEAR_UNROLL):
            row = jnp.minimum(todo[2 * i], LEAVES - 1)
            buf[i] = near_product(sides[row], pool_ref[todo[2 * i + 1]])

    def near_last(todo, buf):
        parts = []
        for i in range(NEAR_UNROLL):
            parts.append(near_sums(buf.at[i], pool_ref[todo[2 * i + 1]], sub))
        for i in range(NEAR_UNROLL):
            near[todo[2 * i]] += parts[i]

    def near_body(carry):
        at, now = carry
        at, then = near_items(at)
        near_first(then, buf_b)
        near_last(now, buf_a)
        at, now = near_items(at)
        near_first(now, buf_a)
        near_last(then, buf_b)
        return at, now

    at, now = near_items((jnp.int32(0), jnp.int32(0)))
    near_first(now, buf_a)
    lax.while_loop(lambda carry: carry[1][0] < LEAVES, near_body, (at, now))

    def far_body(at):
        t, k = at
        todo = []
        for _ in range(FAR_UNROLL):
            row = jnp.minimum(t, LEAVES - 1)
            most = clen_ref[row]
            todo.append((jnp.minimum(t, LEAVES), row, k, most))
            t, k = step(t, k, (most + 7) // 8)
        parts = []
        for _, row, group, most in todo:
            rows = jnp.concatenate(
                [cells_ref[pl.ds(clist_ref[row, 8 * group + i], 1), :] for i in range(8)], axis=0
            )
            rows = jnp.where(8 * group + sub < most, rows, 0.0)
            block = pool_ref[row]
            x = [jnp.broadcast_to(block[d : d + 1], (8, LANES)) for d in range(3)]
            parts.append(far_item(x, rows))
        for (slot, _, _, _), part in zip(todo, parts):
            for d in range(3):
                far[slot, d] += part[d]
        return t, k

    lax.while_loop(lambda at: at[0] < LEAVES, far_body, (jnp.int32(0), jnp.int32(0)))

    unif = unif_ref[0:3]

    def finish(t, carry):
        got = near[t]
        x = pool_ref[t][0:3]
        close = 3.0 * (x * got[6:7] - got[0:3]) - got[3:6]
        out_ref[t] = close + jnp.sum(far[t], axis=1) + unif
        return carry

    lax.fori_loop(0, LEAVES, finish, 0)


def field(pool, cells, unif, cell_list, cell_len, leaf_list, leaf_len):
    vmem = pl.BlockSpec(memory_space=pltpu.VMEM)
    smem = pl.BlockSpec(memory_space=pltpu.SMEM)
    return pl.pallas_call(
        field_kernel,
        out_shape=jax.ShapeDtypeStruct((LEAVES, 3, LANES), F32),
        in_specs=[vmem, vmem, vmem, smem, smem, smem, smem],
        out_specs=vmem,
        scratch_shapes=[
            pltpu.VMEM((LEAVES, 64, 2 * LANES), BF16),
            pltpu.VMEM((LEAVES + 1, 8, LANES), F32),
            pltpu.VMEM((LEAVES + 1, 3, 8, LANES), F32),
            pltpu.VMEM((NEAR_UNROLL, LANES, 2 * LANES), F32),
            pltpu.VMEM((NEAR_UNROLL, LANES, 2 * LANES), F32),
        ],
        compiler_params=pltpu.CompilerParams(vmem_limit_bytes=40 * 1024 * 1024),
        name="field",
    )(pool, cells, unif, cell_list, cell_len, leaf_list, leaf_len)


def per_device(
    positions, moments, fwd_cells, fwd_leaves, fwd_counts, cell_list, cell_len, leaf_list, leaf_len
):
    pool, cells, unif = exchange(positions, moments, fwd_leaves, fwd_counts, fwd_cells)
    return field(pool, cells, unif, cell_list, cell_len, leaf_list, leaf_len)


def solution(mesh):
    row = P("dom", None)
    cube = P("dom", None, None)
    return jax.shard_map(
        per_device,
        mesh=mesh,
        in_specs=(cube, cube, cube, cube, cube, row, P("dom"), row, P("dom")),
        out_specs=cube,
        check_vma=False,
    )
```

```python
import functools

import jax
import jax.numpy as jnp
from jax import lax
from jax.experimental import pallas as pl
from jax.experimental.pallas import tpu as pltpu
from jax.sharding import PartitionSpec as P

F32 = jnp.float32
BF16 = jnp.bfloat16
DEMAG = 4.1887902047863905
LEAVES = 64
PARENTS = 8
OWN = LEAVES + PARENTS
SECTIONS = 9
CELL_SENDS = 64
LEAF_SENDS = 20
LEAF_POOL = LEAVES + SECTIONS * LEAF_SENDS
WIDE = 128 + SECTIONS * CELL_SENDS
LANES = 128
N_DOM = 512
NEAR_UNROLL = 4
FAR_UNROLL = 2


def iota(shape, dim):
    return lax.broadcasted_iota(jnp.int32, shape, dim)


def pieces(x):
    first = x.astype(BF16).astype(F32)
    rest = x - first
    second = rest.astype(BF16).astype(F32)
    return first, second, rest - second


def cell_features(tile):
    row = lambda i: tile[i : i + 1]
    sec = lambda k, j: row(6 + 3 * k + j)
    c = [row(d) for d in range(3)]
    tot = [row(3 + d) for d in range(3)]
    xx, yy, zz = [2.0 * sec(d, d) for d in range(3)]
    xy, xz, yz = sec(0, 1) + sec(1, 0), sec(0, 2) + sec(2, 0), sec(1, 2) + sec(2, 1)
    turn = [
        xx * c[0] + xy * c[1] + xz * c[2],
        xy * c[0] + yy * c[1] + yz * c[2],
        xz * c[0] + yz * c[1] + zz * c[2],
    ]
    main = jnp.concatenate(
        [tile[0:6], xx, yy, zz, xy, xz, yz] + turn + [jnp.ones((1, LANES), F32)], axis=0
    )
    rest = jnp.concatenate(
        [
            c[0] * c[0] + c[1] * c[1] + c[2] * c[2] + 1.0,
            -(tot[0] * c[0] + tot[1] * c[1] + tot[2] * c[2])
            - (sec(0, 0) + sec(1, 1) + sec(2, 2)),
            c[0] * turn[0] + c[1] * turn[1] + c[2] * turn[2],
        ],
        axis=0,
    )
    blocks = list(pieces(main)) + list(pieces(rest)) + [jnp.zeros((7, LANES), F32)]
    return jnp.concatenate(blocks, axis=0).astype(BF16)


def far_side(block):
    x = [block[d : d + 1] for d in range(3)]
    none = lambda n: jnp.zeros((n, LANES), F32)
    x3 = block[0:3]
    quad = jnp.concatenate([-2.0 * x3, none(12), block[6:7]], axis=0)
    along = jnp.concatenate([none(3), x3, none(10)], axis=0)
    bend = jnp.concatenate(
        [
            none(6), x[0] * x[0], x[1] * x[1], x[2] * x[2],
            2.0 * (x[0] * x[1]), 2.0 * (x[0] * x[2]), 2.0 * (x[1] * x[2]),
            -2.0 * x3, none(1),
        ],
        axis=0,
    )
    sub = iota((16, LANES), 0)
    cols = []
    for i, part in enumerate((quad, along, bend)):
        p0, p1, p2 = pieces(part)
        ones = jnp.where((sub < 9) & (lax.rem(sub, 3) == i), 1.0, 0.0)
        cols.append(jnp.concatenate([p0, p1, p2, p0, p1, p0, ones], axis=0).astype(BF16))
    return jnp.concatenate(cols, axis=1)


def far_product(side, picked):
    a0, a1, a2, rest = picked[0:16], picked[16:32], picked[32:48], picked[48:64]
    stack = jnp.concatenate([a0, a0, a0, a1, a1, a2, rest], axis=0).astype(BF16)
    return lax.dot_general(stack, side, (((0,), (0,)), ((), ())), preferred_element_type=F32)


def far_sums(both, picked, block):
    quad = jnp.maximum(both[:, 0:LANES], 1.0)
    inv = lax.rsqrt(quad)
    inv2 = inv * inv
    inv3 = inv2 * inv
    inv5 = 3.0 * (inv3 * inv2)
    inv7 = 2.5 * (inv5 * inv2)
    coef = both[:, LANES : 2 * LANES] * inv5 + both[:, 2 * LANES :] * inv7
    sub = iota((16, 64), 0)

    def lefts(part, one):
        first = jnp.where(sub < 3, part, jnp.where(sub == 3, one, 0.0))
        second = jnp.where(sub < 3, pltpu.roll(part, 13, 0), 0.0)
        third = jnp.where(
            sub < 3,
            -pltpu.roll(part, 4, 0),
            jnp.where((sub >= 4) & (sub < 10), pltpu.roll(part, 14, 0), 0.0),
        )
        return first, second, third

    total = None
    for weight, high_l, low_l in zip(
        (coef, inv3, inv5), lefts(picked[0:16], 1.0), lefts(picked[16:32], 0.0)
    ):
        high = weight.astype(BF16)
        low = (weight - high.astype(F32)).astype(BF16)
        left = jnp.concatenate([high_l, low_l], axis=0).astype(BF16)
        part = jnp.dot(
            left, jnp.concatenate([high, low], axis=1), preferred_element_type=F32
        )
        total = part if total is None else total + part
    got = (total[0:16, 0:LANES] + total[16:32, 0:LANES]) + total[0:16, LANES:]
    x = [block[d : d + 1] for d in range(3)]
    q = [got[4 + i : 5 + i] for i in range(6)]
    turn = [
        q[0] * x[0] + q[3] * x[1] + q[4] * x[2],
        q[3] * x[0] + q[1] * x[1] + q[5] * x[2],
        q[4] * x[0] + q[5] * x[1] + q[2] * x[2],
    ]
    return [x[d] * got[3:4] - got[d : d + 1] - turn[d] for d in range(3)]


def own_tile(pos_ref, mom_ref):
    pos = [pos_ref[:, k, :] for k in range(3)]
    mom = [mom_ref[:, k, :] for k in range(3)]
    cen = [jnp.sum(p, axis=1, keepdims=True) * (1.0 / LANES) for p in pos]
    tot = [jnp.sum(m, axis=1, keepdims=True) for m in mom]
    off = [pos[k] - cen[k] for k in range(3)]
    sec = [
        [jnp.sum(off[k] * mom[j], axis=1, keepdims=True) for j in range(3)] for k in range(3)
    ]
    full = lambda x: jnp.broadcast_to(x, (LEAVES, LANES)).reshape(PARENTS, 8, LANES)
    fcen = [full(c) for c in cen]
    ftot = [full(c) for c in tot]
    fsec = [[full(sec[k][j]) for j in range(3)] for k in range(3)]
    pcen = [jnp.sum(c, axis=1, keepdims=True) * 0.125 for c in fcen]
    ptot = [jnp.sum(c, axis=1) for c in ftot]
    psec = [
        [jnp.sum(fsec[k][j] + (fcen[k] - pcen[k]) * ftot[j], axis=1) for j in range(3)]
        for k in range(3)
    ]
    leaf = fcen + ftot + [fsec[k][j] for k in range(3) for j in range(3)]
    up = [c[:, 0, :] for c in pcen] + ptot + [psec[k][j] for k in range(3) for j in range(3)]
    lane = iota((LEAVES, LANES), 1)
    lane_p = iota((PARENTS, LANES), 1)
    rows = jnp.zeros((LEAVES, LANES), F32)
    rows_p = jnp.zeros((PARENTS, LANES), F32)
    for i in range(15):
        rows = jnp.where(lane == i, leaf[i].reshape(LEAVES, LANES), rows)
        rows_p = jnp.where(lane_p == i, up[i], rows_p)
    every = jnp.concatenate([rows, rows_p, jnp.zeros((LANES - OWN, LANES), F32)], axis=0)
    sums = [jnp.sum(p, axis=0, keepdims=True) for p in ptot]
    return jnp.transpose(every)[0:16], sums


def target_side(block, sub):
    cut = pieces(block)
    zero = jnp.zeros((16, LANES), F32)
    order = (0, 1, 2, 0, 1, 0)
    lead = (True, False, False, True, False, True)
    quad, along = [], []
    for p, flag in zip(order, lead):
        mark = 1.0 if flag else 0.0
        quad.append(jnp.where(sub < 3, -2.0 * cut[p], jnp.where(sub == 6, mark, 0.0)))
        turned = pltpu.roll(cut[p], 3, 0)
        along.append(
            jnp.where((sub >= 3) & (sub < 6), turned, jnp.where(sub == 7, -mark, 0.0))
        )
    quad.append(
        jnp.where(sub == 6, cut[0], jnp.where(sub == 7, pltpu.roll(cut[1], 1, 0), 0.0))
    )
    quad.append(jnp.where(sub == 6, cut[2], jnp.where(sub == 7, 1.0, 0.0)))
    along.append(zero)
    return jnp.concatenate(
        [jnp.concatenate(quad, axis=0), jnp.concatenate(along, axis=0)], axis=1
    ).astype(BF16)


def near_product(side, block):
    cut = pieces(block)
    source = jnp.concatenate(
        [cut[0], cut[0], cut[0], cut[1], cut[1], cut[2], jnp.ones((16, LANES), F32)], axis=0
    ).astype(BF16)
    return lax.dot_general(
        source, side, (((0,), (0,)), ((), ())), preferred_element_type=F32
    )


def near_sums(both, block, sub):
    parts = [[], [], [], []]
    for c in range(LANES // 16):
        quad = both[16 * c : 16 * c + 16, 0:LANES]
        along = both[16 * c : 16 * c + 16, LANES:]
        inv = lax.rsqrt(quad)
        inv2 = inv * inv
        inv3 = inv2 * inv
        coef = along * (inv3 * inv2)
        for i, weight in enumerate((coef, inv3)):
            high = weight.astype(BF16)
            parts[i].append(high)
            parts[2 + i].append((weight - high.astype(F32)).astype(BF16))
    high = jnp.concatenate(parts[0] + parts[1], axis=0)
    low = jnp.concatenate(parts[2] + parts[3], axis=0)

    def sums(part, one):
        c_side = jnp.where(sub < 3, part, jnp.where(sub == 6, one, 0.0))
        w_side = jnp.where((sub >= 3) & (sub < 6), part, 0.0)
        return jnp.concatenate([c_side, w_side], axis=1)

    cut = pieces(block)
    left = jnp.concatenate([sums(cut[0], 1.0), sums(cut[1], 0.0)], axis=0).astype(BF16)
    got = jnp.dot(left, high, preferred_element_type=F32)
    more = jnp.dot(left, low, preferred_element_type=F32)
    return (got[0:8] + got[8:16]) + more[0:8]


def near_pass(count, first, last, buf_a, buf_b):
    first(0, buf_a)

    def body(i, carry):
        g = 2 * i
        first(g + 1, buf_b)
        last(g, buf_a)
        first(jnp.minimum(g + 2, count - 1), buf_a)
        last(g + 1, buf_b)
        return carry

    lax.fori_loop(0, count // 2, body, 0)


def exchange_kernel(
    pos_ref, mom_ref, fl_ref, fn_ref, fc_ref, llist_ref, llen_ref, clist_ref, clen_ref,
    pool_ref, sides, near, far_ref,
    split, feats, index, cindex, gath, pick, fsides, buf_a, buf_b, far_a, far_b,
    send_l, recv_l, send_c, recv_c, sl_sem, rl_sem, sc_sem, rc_sem,
):
    me = lax.axis_index("dom")
    partners = []
    for b in range(SECTIONS):
        stride = 1 << b
        partners.append(me + (1 - 2 * lax.rem(me // stride, 2)) * stride)
    barrier = pltpu.get_barrier_semaphore()
    for other in partners:
        pl.semaphore_signal(
            barrier, inc=1, device_id=(other,), device_id_type=pl.DeviceIdType.MESH
        )
    pool_ref[0:LEAVES, 0:3, :] = pos_ref[...]
    pool_ref[0:LEAVES, 3:6, :] = mom_ref[...]

    lane = iota((8, LANES), 1)
    sub = iota((8, LANES), 0)
    index[...] = jnp.full((16, LANES), -1, jnp.int32)
    index[0:SECTIONS, 0:CELL_SENDS] = fc_ref[0]
    raw = index[...]
    index[...] = jnp.where(raw < OWN, raw, raw + (LANES - OWN))
    for half in range(2):
        rows = clist_ref[half * 32 : half * 32 + 32, :]
        cindex[:, half * 64 : half * 64 + 64] = jnp.where(
            rows < OWN, rows, rows + (LANES - OWN)
        )
    pl.semaphore_wait(barrier, SECTIONS)

    def leaf_copy(b):
        return pltpu.make_async_remote_copy(
            src_ref=send_l.at[b], dst_ref=recv_l.at[b],
            send_sem=sl_sem.at[b], recv_sem=rl_sem.at[b],
            device_id=(partners[b],), device_id_type=pl.DeviceIdType.MESH,
        )

    def cell_copy(b):
        return pltpu.make_async_remote_copy(
            src_ref=send_c.at[b], dst_ref=recv_c.at[b],
            send_sem=sc_sem.at[b], recv_sem=rc_sem.at[b],
            device_id=(partners[b],), device_id_type=pl.DeviceIdType.MESH,
        )

    def send_leaves(b):
        live = fn_ref[0, b, 1]
        for s in range(LEAF_SENDS):
            block = pool_ref[fl_ref[0, b, s]][0:6]
            send_l[b, 6 * s : 6 * s + 6, :] = jnp.where(s < live, block, 0.0)
        leaf_copy(b).start()

    def take_tile(tile, at, ref, rows):
        if at % 2:
            kept = ref[:, at // 2 * LANES : at // 2 * LANES + LANES]
            turned = pltpu.roll(rows.astype(F32), CELL_SENDS, 1).astype(BF16)
            wide = iota(rows.shape, 1)
            rows = jnp.where(wide < CELL_SENDS, kept.astype(F32), turned.astype(F32)).astype(BF16)
        ref[:, at // 2 * LANES : at // 2 * LANES + LANES] = rows

    def take_split(tile, at):
        take_tile(tile, at, split, jnp.concatenate(pieces(tile), axis=0).astype(BF16))

    def take_features(tile, at):
        take_tile(tile, at, feats, cell_features(tile))

    def send_cells(b, msum):
        depth = LANES * ((b + 3) // 2)
        wanted = jnp.where(lane[0:1] < fn_ref[0, b, 0], index[b : b + 1, :], -1)
        hot = jnp.where(iota((depth, LANES), 0) == wanted, 1.0, 0.0).astype(BF16)
        got = jnp.dot(split[:, 0:depth], hot, preferred_element_type=F32)
        got = (got[0:16] + got[16:32]) + got[32:48]
        low = jnp.where(sub == 7, msum, got[8:16])
        send_c[b] = jnp.where(lane < CELL_SENDS, got[0:8], pltpu.roll(low, CELL_SENDS, 1))
        cell_copy(b).start()

    def finish_leaves(first, count):
        part = [pool_ref[first : first + count, i, :] for i in range(6)]
        pool_ref[first : first + count, 6, :] = (
            part[0] * part[0] + part[1] * part[1] + part[2] * part[2]
        )
        pool_ref[first : first + count, 7, :] = (
            part[0] * part[3] + part[1] * part[4] + part[2] * part[5]
        )

    def prepare(t, carry):
        block = pool_ref[t]
        sides[t] = target_side(block, sub)
        fsides[t] = far_side(block)
        return carry

    def near_source(t, k):
        if k == 0:
            return pool_ref[t]
        return jnp.where(llen_ref[t] > 1, pool_ref[llist_ref[t, 1]], 0.0)

    def near_steps(t0, count):
        def first(g, buf):
            for i in range(4):
                t = t0 + 2 * g + i // 2
                buf[i] = near_product(sides[t], near_source(t, i % 2))

        def last(g, buf):
            for i in range(2):
                t = t0 + 2 * g + i
                near[t] = near_sums(buf.at[2 * i], near_source(t, 0), sub) + near_sums(
                    buf.at[2 * i + 1], near_source(t, 1), sub
                )

        near_pass(count // 2, first, last, buf_a, buf_b)

    def wanted_cells(i):
        row = cindex[pl.ds(i, 1), :]
        k = jnp.where(lane[0:1] < 64, lane[0:1], lane[0:1] - 64)
        most = jnp.where(lane[0:1] < 64, clen_ref[i], clen_ref[i + 32])
        return jnp.where(k < most, row, -1)

    old = LANES + (SECTIONS - 1) * CELL_SENDS

    def gather_old(g, carry):
        for j in range(2):
            i = 2 * g + j
            hot = jnp.where(iota((old, LANES), 0) == wanted_cells(i), 1.0, 0.0).astype(BF16)
            gath[i] = jnp.dot(feats[:, 0:old], hot, preferred_element_type=F32)
        return carry

    def far_first(g, buf):
        for j in range(FAR_UNROLL):
            i = FAR_UNROLL * g + j
            hot = jnp.where(
                iota((LANES, LANES), 0) + old == wanted_cells(i), 1.0, 0.0
            ).astype(BF16)
            picked = gath[i] + jnp.dot(
                feats[:, old : old + LANES], hot, preferred_element_type=F32
            )
            pick[i] = picked
            buf[2 * j] = far_product(fsides[i], picked[:, 0:64])
            buf[2 * j + 1] = far_product(fsides[i + 32], pltpu.roll(picked, 64, 1)[:, 0:64])

    def far_last(g, buf, unif):
        for j in range(FAR_UNROLL):
            i = FAR_UNROLL * g + j
            for half in range(2):
                picked = pick[i, 0:32]
                if half:
                    picked = pltpu.roll(picked, 64, 1)
                t = i + 32 * half
                parts = far_sums(buf[2 * j + half], picked[:, 0:64], pool_ref[t])
                for d in range(3):
                    far_ref[t, d : d + 1, :] = parts[d] + unif[d]

    def beside(b):
        if b == 0:
            finish_leaves(0, LEAVES)
            lax.fori_loop(0, LEAVES, prepare, 0)
        elif b < 5:
            near_steps(16 * (b - 1), 16)
        elif b == SECTIONS - 1:
            lax.fori_loop(0, 16, gather_old, 0)

    send_leaves(0)
    tile, sums = own_tile(pos_ref, mom_ref)
    msum = jnp.zeros((8, LANES), F32)
    for j in range(3):
        msum = jnp.where((sub == 7) & (lane == j), sums[j], msum)
    take_split(tile, 0)
    send_cells(0, msum)
    take_features(tile, 0)
    beside(0)
    for b in range(SECTIONS):
        first = LEAVES + b * LEAF_SENDS
        leaf_copy(b).wait_recv()
        for s in range(LEAF_SENDS):
            pool_ref[first + s, 0:6, :] = recv_l[b, 6 * s : 6 * s + 6, :]
        if b + 1 < SECTIONS:
            send_leaves(b + 1)
        cell_copy(b).wait_recv()
        got = recv_c[b]
        low = jnp.where(lane < CELL_SENDS, pltpu.roll(got, CELL_SENDS, 1), 0.0)
        high = jnp.where(lane < CELL_SENDS, got, 0.0)
        tile = jnp.concatenate([high, low], axis=0)
        msum = msum + jnp.where(sub == 7, low, 0.0)
        if b + 1 < SECTIONS:
            take_split(tile, b + 2)
            send_cells(b + 1, msum)
        take_features(tile, b + 2)
        finish_leaves(first, LEAF_SENDS)
        if b + 1 < SECTIONS:
            beside(b + 1)
    scaled = msum * (-DEMAG / (N_DOM * LEAVES))
    unif = [jnp.broadcast_to(scaled[7:8, j : j + 1], (1, LANES)) for j in range(3)]
    near_pass(
        32 // FAR_UNROLL, far_first, lambda g, buf: far_last(g, buf, unif), far_a, far_b
    )
    for b in range(SECTIONS):
        leaf_copy(b).wait_send()
        cell_copy(b).wait_send()


def exchange(
    positions, moments, fwd_leaves, fwd_counts, fwd_cells, leaf_list, leaf_len, cell_list, cell_len
):
    vmem = pl.BlockSpec(memory_space=pltpu.VMEM)
    smem = pl.BlockSpec(memory_space=pltpu.SMEM)
    dma = pltpu.SemaphoreType.DMA((SECTIONS,))
    return pl.pallas_call(
        exchange_kernel,
        out_shape=(
            jax.ShapeDtypeStruct((LEAF_POOL, 8, LANES), F32),
            jax.ShapeDtypeStruct((LEAVES, 64, 2 * LANES), BF16),
            jax.ShapeDtypeStruct((LEAVES, 8, LANES), F32),
            jax.ShapeDtypeStruct((LEAVES, 3, LANES), F32),
        ),
        in_specs=[vmem, vmem, smem, smem, vmem, smem, smem, vmem, smem],
        out_specs=(vmem, vmem, vmem, vmem),
        scratch_shapes=[
            pltpu.VMEM((48, WIDE + 64), BF16),
            pltpu.VMEM((64, WIDE + 64), BF16),
            pltpu.VMEM((16, LANES), jnp.int32),
            pltpu.VMEM((32, LANES), jnp.int32),
            pltpu.VMEM((32, 64, LANES), F32),
            pltpu.VMEM((32, 64, LANES), F32),
            pltpu.VMEM((LEAVES, 112, 3 * LANES), BF16),
            pltpu.VMEM((4, LANES, 2 * LANES), F32),
            pltpu.VMEM((4, LANES, 2 * LANES), F32),
            pltpu.VMEM((2 * FAR_UNROLL, 64, 3 * LANES), F32),
            pltpu.VMEM((2 * FAR_UNROLL, 64, 3 * LANES), F32),
            pltpu.VMEM((SECTIONS, 6 * LEAF_SENDS, LANES), F32),
            pltpu.VMEM((SECTIONS, 6 * LEAF_SENDS, LANES), F32),
            pltpu.VMEM((SECTIONS, 8, LANES), F32),
            pltpu.VMEM((SECTIONS, 8, LANES), F32),
            dma, dma, dma, dma,
        ],
        compiler_params=pltpu.CompilerParams(
            collective_id=0, has_side_effects=True, vmem_limit_bytes=40 * 1024 * 1024
        ),
        name="exchange",
    )(
        positions, moments, fwd_leaves, fwd_counts, fwd_cells,
        leaf_list, leaf_len, cell_list, cell_len,
    )


def field_kernel(
    pool_ref, sides, near0, far_ref, llist_ref, llen_ref, out_ref, near, todo_ref, buf_a, buf_b
):
    sub = iota((8, LANES), 0)

    def collect(t, count):
        todo_ref[count] = t
        return jnp.where(llen_ref[t] > 2, count + 1, count)

    busy = lax.fori_loop(0, LEAVES, collect, 0)
    near[0:LEAVES] = near0[...]
    near[LEAVES] = jnp.zeros((8, LANES), F32)

    def near_items(at):
        n, k = at
        todo = []
        for _ in range(NEAR_UNROLL):
            t = todo_ref[jnp.minimum(n, LEAVES - 1)]
            t = jnp.where(n < busy, t, 0)
            todo += [jnp.where(n < busy, t, LEAVES), t, llist_ref[t, k]]
            more = k + 1 < llen_ref[t]
            n, k = jnp.where(more, n, n + 1), jnp.where(more, k + 1, 2)
        return (n, k), tuple(todo)

    def near_first(todo, buf):
        for i in range(NEAR_UNROLL):
            buf[i] = near_product(sides[todo[3 * i + 1]], pool_ref[todo[3 * i + 2]])

    def near_last(todo, buf):
        parts = []
        for i in range(NEAR_UNROLL):
            parts.append(near_sums(buf.at[i], pool_ref[todo[3 * i + 2]], sub))
        for i in range(NEAR_UNROLL):
            near[todo[3 * i]] += parts[i]

    def near_body(carry):
        at, now = carry
        at, then = near_items(at)
        near_first(then, buf_b)
        near_last(now, buf_a)
        at, now = near_items(at)
        near_first(now, buf_a)
        near_last(then, buf_b)
        return at, now

    at, now = near_items((jnp.int32(0), jnp.int32(2)))
    near_first(now, buf_a)
    lax.while_loop(lambda carry: carry[1][0] < LEAVES, near_body, (at, now))

    def finish(g, carry):
        for i in range(4):
            t = 4 * g + i
            got = near[t]
            x = pool_ref[t][0:3]
            out_ref[t] = (3.0 * (x * got[6:7] - got[0:3]) - got[3:6]) + far_ref[t]
        return carry

    lax.fori_loop(0, LEAVES // 4, finish, 0)


def field(pool, sides, near, far, leaf_list, leaf_len):
    vmem = pl.BlockSpec(memory_space=pltpu.VMEM)
    smem = pl.BlockSpec(memory_space=pltpu.SMEM)
    return pl.pallas_call(
        field_kernel,
        out_shape=jax.ShapeDtypeStruct((LEAVES, 3, LANES), F32),
        in_specs=[vmem, vmem, vmem, vmem, smem, smem],
        out_specs=vmem,
        scratch_shapes=[
            pltpu.VMEM((LEAVES + 1, 8, LANES), F32),
            pltpu.SMEM((LEAVES + 8,), jnp.int32),
            pltpu.VMEM((NEAR_UNROLL, LANES, 2 * LANES), F32),
            pltpu.VMEM((NEAR_UNROLL, LANES, 2 * LANES), F32),
        ],
        compiler_params=pltpu.CompilerParams(vmem_limit_bytes=16 * 1024 * 1024),
        name="field",
    )(pool, sides, near, far, leaf_list, leaf_len)


def per_device(
    positions, moments, fwd_cells, fwd_leaves, fwd_counts, cell_list, cell_len, leaf_list, leaf_len
):
    pool, sides, near, far = exchange(
        positions, moments, fwd_leaves, fwd_counts, fwd_cells,
        leaf_list, leaf_len, cell_list, cell_len,
    )
    return field(pool, sides, near, far, leaf_list, leaf_len)


def solution(mesh):
    row = P("dom", None)
    cube = P("dom", None, None)
    return jax.shard_map(
        per_device,
        mesh=mesh,
        in_specs=(cube, cube, cube, cube, cube, row, P("dom"), row, P("dom")),
        out_specs=cube,
        check_vma=False,
    )
```

```python
import functools

import jax
import jax.numpy as jnp
from jax import lax
from jax.experimental import pallas as pl
from jax.experimental.pallas import tpu as pltpu
from jax.sharding import PartitionSpec as P

F32 = jnp.float32
BF16 = jnp.bfloat16
DEMAG = 4.1887902047863905
LEAVES = 64
PARENTS = 8
OWN = LEAVES + PARENTS
SECTIONS = 9
CELL_SENDS = 64
LEAF_SENDS = 20
LEAF_POOL = LEAVES + SECTIONS * LEAF_SENDS
WIDE = 128 + SECTIONS * CELL_SENDS
LANES = 128
N_DOM = 512
NEAR_UNROLL = 8
FAR_UNROLL = 4


def iota(shape, dim):
    return lax.broadcasted_iota(jnp.int32, shape, dim)


def pieces(x):
    first = x.astype(BF16).astype(F32)
    rest = x - first
    second = rest.astype(BF16).astype(F32)
    return first, second, rest - second


def cell_features(tile):
    row = lambda i: tile[i : i + 1]
    sec = lambda k, j: row(6 + 3 * k + j)
    c = [row(d) for d in range(3)]
    tot = [row(3 + d) for d in range(3)]
    xx, yy, zz = [2.0 * sec(d, d) for d in range(3)]
    xy, xz, yz = sec(0, 1) + sec(1, 0), sec(0, 2) + sec(2, 0), sec(1, 2) + sec(2, 1)
    turn = [
        xx * c[0] + xy * c[1] + xz * c[2],
        xy * c[0] + yy * c[1] + yz * c[2],
        xz * c[0] + yz * c[1] + zz * c[2],
    ]
    main = jnp.concatenate(
        [tile[0:6], xx, yy, zz, xy, xz, yz] + turn + [jnp.ones((1, LANES), F32)], axis=0
    )
    rest = jnp.concatenate(
        [
            c[0] * c[0] + c[1] * c[1] + c[2] * c[2] + 1.0,
            -(tot[0] * c[0] + tot[1] * c[1] + tot[2] * c[2])
            - (sec(0, 0) + sec(1, 1) + sec(2, 2)),
            c[0] * turn[0] + c[1] * turn[1] + c[2] * turn[2],
        ],
        axis=0,
    )
    blocks = list(pieces(main)) + list(pieces(rest)) + [jnp.zeros((7, LANES), F32)]
    return jnp.concatenate(blocks, axis=0).astype(BF16)


def far_side(block):
    x = [block[d : d + 1] for d in range(3)]
    none = lambda n: jnp.zeros((n, LANES), F32)
    x3 = block[0:3]
    quad = jnp.concatenate([-2.0 * x3, none(12), block[6:7]], axis=0)
    along = jnp.concatenate([none(3), x3, none(10)], axis=0)
    bend = jnp.concatenate(
        [
            none(6), x[0] * x[0], x[1] * x[1], x[2] * x[2],
            2.0 * (x[0] * x[1]), 2.0 * (x[0] * x[2]), 2.0 * (x[1] * x[2]),
            -2.0 * x3, none(1),
        ],
        axis=0,
    )
    sub = iota((16, LANES), 0)
    cols = []
    for i, part in enumerate((quad, along, bend)):
        p0, p1, p2 = pieces(part)
        ones = jnp.where((sub < 9) & (lax.rem(sub, 3) == i), 1.0, 0.0)
        cols.append(jnp.concatenate([p0, p1, p2, p0, p1, p0, ones], axis=0).astype(BF16))
    return jnp.concatenate(cols, axis=1)


def far_product(side, picked):
    a0, a1, a2, rest = picked[0:16], picked[16:32], picked[32:48], picked[48:64]
    stack = jnp.concatenate([a0, a0, a0, a1, a1, a2, rest], axis=0).astype(BF16)
    return lax.dot_general(stack, side, (((0,), (0,)), ((), ())), preferred_element_type=F32)


def far_sums(both, picked, block):
    quad = jnp.maximum(both[:, 0:LANES], 1.0)
    inv = lax.rsqrt(quad)
    inv2 = inv * inv
    inv3 = inv2 * inv
    inv5 = 3.0 * (inv3 * inv2)
    inv7 = 2.5 * (inv5 * inv2)
    coef = both[:, LANES : 2 * LANES] * inv5 + both[:, 2 * LANES :] * inv7
    sub = iota((16, 64), 0)

    def lefts(part, one):
        first = jnp.where(sub < 3, part, jnp.where(sub == 3, one, 0.0))
        second = jnp.where(sub < 3, pltpu.roll(part, 13, 0), 0.0)
        third = jnp.where(
            sub < 3,
            -pltpu.roll(part, 4, 0),
            jnp.where((sub >= 4) & (sub < 10), pltpu.roll(part, 14, 0), 0.0),
        )
        return first, second, third

    total = None
    for weight, high_l, low_l in zip(
        (coef, inv3, inv5), lefts(picked[0:16], 1.0), lefts(picked[16:32], 0.0)
    ):
        high = weight.astype(BF16)
        low = (weight - high.astype(F32)).astype(BF16)
        left = jnp.concatenate([high_l, low_l], axis=0).astype(BF16)
        part = jnp.dot(
            left, jnp.concatenate([high, low], axis=1), preferred_element_type=F32
        )
        total = part if total is None else total + part
    got = (total[0:16, 0:LANES] + total[16:32, 0:LANES]) + total[0:16, LANES:]
    x = [block[d : d + 1] for d in range(3)]
    q = [got[4 + i : 5 + i] for i in range(6)]
    turn = [
        q[0] * x[0] + q[3] * x[1] + q[4] * x[2],
        q[3] * x[0] + q[1] * x[1] + q[5] * x[2],
        q[4] * x[0] + q[5] * x[1] + q[2] * x[2],
    ]
    return [x[d] * got[3:4] - got[d : d + 1] - turn[d] for d in range(3)]


def own_tile(pos_ref, mom_ref):
    pos = [pos_ref[k] for k in range(3)]
    mom = [mom_ref[k] for k in range(3)]
    cen = [jnp.sum(p, axis=1, keepdims=True) * (1.0 / LANES) for p in pos]
    tot = [jnp.sum(m, axis=1, keepdims=True) for m in mom]
    off = [pos[k] - cen[k] for k in range(3)]
    sec = [
        [jnp.sum(off[k] * mom[j], axis=1, keepdims=True) for j in range(3)] for k in range(3)
    ]
    full = lambda x: jnp.broadcast_to(x, (LEAVES, LANES)).reshape(PARENTS, 8, LANES)
    fcen = [full(c) for c in cen]
    ftot = [full(c) for c in tot]
    fsec = [[full(sec[k][j]) for j in range(3)] for k in range(3)]
    pcen = [jnp.sum(c, axis=1, keepdims=True) * 0.125 for c in fcen]
    ptot = [jnp.sum(c, axis=1) for c in ftot]
    psec = [
        [jnp.sum(fsec[k][j] + (fcen[k] - pcen[k]) * ftot[j], axis=1) for j in range(3)]
        for k in range(3)
    ]
    leaf = fcen + ftot + [fsec[k][j] for k in range(3) for j in range(3)]
    up = [c[:, 0, :] for c in pcen] + ptot + [psec[k][j] for k in range(3) for j in range(3)]
    lane = iota((LEAVES, LANES), 1)
    lane_p = iota((PARENTS, LANES), 1)
    rows = jnp.zeros((LEAVES, LANES), F32)
    rows_p = jnp.zeros((PARENTS, LANES), F32)
    for i in range(15):
        rows = jnp.where(lane == i, leaf[i].reshape(LEAVES, LANES), rows)
        rows_p = jnp.where(lane_p == i, up[i], rows_p)
    every = jnp.concatenate([rows, rows_p, jnp.zeros((LANES - OWN, LANES), F32)], axis=0)
    sums = [jnp.sum(p, axis=0, keepdims=True) for p in ptot]
    return jnp.transpose(every)[0:16], sums


def target_side(block, sub):
    cut = pieces(block)
    zero = jnp.zeros((16, LANES), F32)
    order = (0, 1, 2, 0, 1, 0)
    lead = (True, False, False, True, False, True)
    quad, along = [], []
    for p, flag in zip(order, lead):
        mark = 1.0 if flag else 0.0
        quad.append(jnp.where(sub < 3, -2.0 * cut[p], jnp.where(sub == 6, mark, 0.0)))
        turned = pltpu.roll(cut[p], 3, 0)
        along.append(
            jnp.where((sub >= 3) & (sub < 6), turned, jnp.where(sub == 7, -mark, 0.0))
        )
    quad.append(
        jnp.where(sub == 6, cut[0], jnp.where(sub == 7, pltpu.roll(cut[1], 1, 0), 0.0))
    )
    quad.append(jnp.where(sub == 6, cut[2], jnp.where(sub == 7, 1.0, 0.0)))
    along.append(zero)
    return jnp.concatenate(
        [jnp.concatenate(quad, axis=0), jnp.concatenate(along, axis=0)], axis=1
    ).astype(BF16)


def near_product(side, block):
    cut = pieces(block)
    source = jnp.concatenate(
        [cut[0], cut[0], cut[0], cut[1], cut[1], cut[2], jnp.ones((16, LANES), F32)], axis=0
    ).astype(BF16)
    return lax.dot_general(
        source, side, (((0,), (0,)), ((), ())), preferred_element_type=F32
    )


def near_sums(both, block, sub):
    parts = [[], [], [], []]
    for c in range(LANES // 16):
        quad = both[16 * c : 16 * c + 16, 0:LANES]
        along = both[16 * c : 16 * c + 16, LANES:]
        inv = lax.rsqrt(quad)
        inv2 = inv * inv
        inv3 = inv2 * inv
        coef = along * (inv3 * inv2)
        for i, weight in enumerate((coef, inv3)):
            high = weight.astype(BF16)
            parts[i].append(high)
            parts[2 + i].append((weight - high.astype(F32)).astype(BF16))
    high = jnp.concatenate(parts[0] + parts[1], axis=0)
    low = jnp.concatenate(parts[2] + parts[3], axis=0)

    def sums(part, one):
        c_side = jnp.where(sub < 3, part, jnp.where(sub == 6, one, 0.0))
        w_side = jnp.where((sub >= 3) & (sub < 6), part, 0.0)
        return jnp.concatenate([c_side, w_side], axis=1)

    cut = pieces(block)
    left = jnp.concatenate([sums(cut[0], 1.0), sums(cut[1], 0.0)], axis=0).astype(BF16)
    got = jnp.dot(left, high, preferred_element_type=F32)
    more = jnp.dot(left, low, preferred_element_type=F32)
    return (got[0:8] + got[8:16]) + more[0:8]


def near_pass(steps, width, first, last, store, buf_a, buf_b):
    def both(then, now, write, read):
        parts = []
        for i in range(width):
            write[i] = first(then, i)
            parts.append(last(now, i, read))
        store(now, parts)

    for i in range(width):
        buf_a[i] = first(0, i)

    def body(i, carry):
        both(2 * i + 1, 2 * i, buf_b, buf_a)
        both(jnp.minimum(2 * i + 2, steps - 1), 2 * i + 1, buf_a, buf_b)
        return carry

    lax.fori_loop(0, steps // 2, body, 0)


def exchange_kernel(
    pos_in, mom_in, fl_in, fn_in, fc_in, llist_in, llen_in, clist_in, clen_in,
    pool_ref, sides, near, far_ref, llist_out, llen_out,
    pos_ref, mom_ref, fl_ref, fn_ref, fc_ref, llist_ref, llen_ref, clist_ref, clen_ref, in_sem,
    split, feats, index, cindex, gath, pick, fsides, buf_a, buf_b, far_a, far_b,
    send_l, recv_l, send_c, recv_c, sl_sem, rl_sem, sc_sem, rc_sem,
):
    loads = [
        pltpu.make_async_copy(src, dst, in_sem.at[i])
        for i, (src, dst) in enumerate(
            (
                (pos_in, pos_ref), (mom_in, mom_ref), (fl_in, fl_ref), (fn_in, fn_ref),
                (fc_in, fc_ref), (llist_in, llist_ref), (llen_in, llen_ref),
                (clist_in, clist_ref), (clen_in, clen_ref),
                (llist_in, llist_out), (llen_in, llen_out),
            )
        )
    ]
    for load in loads:
        load.start()
    me = lax.axis_index("dom")
    partners = []
    for b in range(SECTIONS):
        stride = 1 << b
        partners.append(me + (1 - 2 * lax.rem(me // stride, 2)) * stride)
    barrier = pltpu.get_barrier_semaphore()
    for other in partners:
        pl.semaphore_signal(
            barrier, inc=1, device_id=(other,), device_id_type=pl.DeviceIdType.MESH
        )
    for load in loads:
        load.wait()
    for d in range(3):
        pool_ref[0:LEAVES, d, :] = pos_ref[d]
        pool_ref[0:LEAVES, 3 + d, :] = mom_ref[d]

    lane = iota((8, LANES), 1)
    sub = iota((8, LANES), 0)
    index[...] = jnp.full((16, LANES), -1, jnp.int32)
    for b in range(SECTIONS):
        index[b : b + 1, 0:CELL_SENDS] = fc_ref[b]
    raw = index[...]
    index[...] = jnp.where(raw < OWN, raw, raw + (LANES - OWN))
    for half in range(2):
        rows = clist_ref[half * 32 : half * 32 + 32, :]
        cindex[:, half * 64 : half * 64 + 64] = jnp.where(
            rows < OWN, rows, rows + (LANES - OWN)
        )

    def leaf_copy(b):
        return pltpu.make_async_remote_copy(
            src_ref=send_l.at[b], dst_ref=recv_l.at[b],
            send_sem=sl_sem.at[b], recv_sem=rl_sem.at[b],
            device_id=(partners[b],), device_id_type=pl.DeviceIdType.MESH,
        )

    def cell_copy(b):
        return pltpu.make_async_remote_copy(
            src_ref=send_c.at[b], dst_ref=recv_c.at[b],
            send_sem=sc_sem.at[b], recv_sem=rc_sem.at[b],
            device_id=(partners[b],), device_id_type=pl.DeviceIdType.MESH,
        )

    def send_leaves(b):
        live = fn_ref[0, 1, b]
        for s in range(LEAF_SENDS):
            block = pool_ref[fl_ref[b, 0, s]][0:6]
            send_l[b, 6 * s : 6 * s + 6, :] = jnp.where(s < live, block, 0.0)
        leaf_copy(b).start()

    def take_tile(tile, at, ref, rows):
        if at % 2:
            kept = ref[:, at // 2 * LANES : at // 2 * LANES + LANES]
            turned = pltpu.roll(rows.astype(F32), CELL_SENDS, 1).astype(BF16)
            wide = iota(rows.shape, 1)
            rows = jnp.where(wide < CELL_SENDS, kept.astype(F32), turned.astype(F32)).astype(BF16)
        ref[:, at // 2 * LANES : at // 2 * LANES + LANES] = rows

    def take_split(tile, at):
        take_tile(tile, at, split, jnp.concatenate(pieces(tile), axis=0).astype(BF16))

    def take_features(tile, at):
        take_tile(tile, at, feats, cell_features(tile))

    def send_cells(b, msum):
        depth = LANES * ((b + 3) // 2)
        wanted = jnp.where(lane[0:1] < fn_ref[0, 0, b], index[b : b + 1, :], -1)
        hot = jnp.where(iota((depth, LANES), 0) == wanted, 1.0, 0.0).astype(BF16)
        got = jnp.dot(split[:, 0:depth], hot, preferred_element_type=F32)
        got = (got[0:16] + got[16:32]) + got[32:48]
        low = jnp.where(sub == 7, msum, got[8:16])
        send_c[b] = jnp.where(lane < CELL_SENDS, got[0:8], pltpu.roll(low, CELL_SENDS, 1))
        cell_copy(b).start()

    def finish_leaves(first, count):
        part = [pool_ref[first : first + count, i, :] for i in range(6)]
        pool_ref[first : first + count, 6, :] = (
            part[0] * part[0] + part[1] * part[1] + part[2] * part[2]
        )
        pool_ref[first : first + count, 7, :] = (
            part[0] * part[3] + part[1] * part[4] + part[2] * part[5]
        )

    def prepare_near(g, carry):
        for i in range(2):
            t = 2 * g + i
            sides[t] = target_side(pool_ref[t], sub)
        return carry

    def prepare_far(g, carry):
        for i in range(2):
            t = 2 * g + i
            fsides[t] = far_side(pool_ref[t])
        return carry

    def near_source(t, k):
        if k == 0:
            return pool_ref[t]
        return jnp.where(llen_ref[t] > 1, pool_ref[llist_ref[1, t]], 0.0)

    def near_steps(t0, leaves):
        def first(g, i):
            t = t0 + 4 * g + i // 2
            return near_product(sides[t], near_source(t, i % 2))

        def last(g, i, buf):
            return near_sums(buf.at[i], near_source(t0 + 4 * g + i // 2, i % 2), sub)

        def store(g, parts):
            for i in range(4):
                near[t0 + 4 * g + i] = parts[2 * i] + parts[2 * i + 1]

        near_pass(leaves // 4, 8, first, last, store, buf_a, buf_b)

    def wanted_cells(i):
        row = cindex[pl.ds(i, 1), :]
        k = jnp.where(lane[0:1] < 64, lane[0:1], lane[0:1] - 64)
        most = jnp.where(lane[0:1] < 64, clen_ref[i], clen_ref[i + 32])
        return jnp.where(k < most, row, -1)

    old = LANES + (SECTIONS - 1) * CELL_SENDS

    def gather(low, high):
        def body(g, carry):
            for j in range(4):
                i = 4 * g + j
                spot = iota((high - low, LANES), 0) + low
                hot = jnp.where(spot == wanted_cells(i), 1.0, 0.0).astype(BF16)
                got = jnp.dot(feats[:, low:high], hot, preferred_element_type=F32)
                gath[i] = got if low == 0 else gath[i] + got
            return carry

        lax.fori_loop(0, 8, body, 0)

    def far_first(g, j):
        i = FAR_UNROLL * g + j
        hot = jnp.where(iota((64, LANES), 0) + old == wanted_cells(i), 1.0, 0.0).astype(BF16)
        picked = gath[i] + jnp.dot(feats[:, old : old + 64], hot, preferred_element_type=F32)
        pick[i] = picked
        return jnp.concatenate(
            [
                far_product(fsides[i], picked[:, 0:64]),
                far_product(fsides[i + 32], pltpu.roll(picked, 64, 1)[:, 0:64]),
            ],
            axis=0,
        )

    def far_last(g, j, buf):
        i = FAR_UNROLL * g + j
        parts = []
        for half in range(2):
            picked = pick[i, 0:32]
            if half:
                picked = pltpu.roll(picked, 64, 1)
            parts.append(
                far_sums(
                    buf[j, 64 * half : 64 * half + 64], picked[:, 0:64], pool_ref[i + 32 * half]
                )
            )
        return parts

    def far_store(g, parts, unif):
        for j in range(FAR_UNROLL):
            for half in range(2):
                t = FAR_UNROLL * g + j + 32 * half
                for d in range(3):
                    far_ref[d, pl.ds(t, 1), :] = parts[j][half][d] + unif[d]

    def beside(b):
        if b == 0:
            lax.fori_loop(0, LEAVES // 2, prepare_near, 0)
        elif b == 1:
            near_steps(0, 16)
        elif b == 2:
            near_steps(16, 16)
        elif b == 3:
            near_steps(32, 32)
        elif b == 4:
            lax.fori_loop(0, LEAVES // 2, prepare_far, 0)
        elif b == 5:
            gather(0, 384)
        elif b == SECTIONS - 1:
            gather(384, old)

    tile, sums = own_tile(pos_ref, mom_ref)
    msum = jnp.zeros((8, LANES), F32)
    for j in range(3):
        msum = jnp.where((sub == 7) & (lane == j), sums[j], msum)
    take_split(tile, 0)
    finish_leaves(0, LEAVES)
    take_features(tile, 0)
    pl.semaphore_wait(barrier, SECTIONS)
    send_leaves(0)
    send_cells(0, msum)
    beside(0)
    for b in range(SECTIONS):
        first = LEAVES + b * LEAF_SENDS
        leaf_copy(b).wait_recv()
        for s in range(LEAF_SENDS):
            pool_ref[first + s, 0:6, :] = recv_l[b, 6 * s : 6 * s + 6, :]
        if b + 1 < SECTIONS:
            send_leaves(b + 1)
        cell_copy(b).wait_recv()
        got = recv_c[b]
        low = jnp.where(lane < CELL_SENDS, pltpu.roll(got, CELL_SENDS, 1), 0.0)
        high = jnp.where(lane < CELL_SENDS, got, 0.0)
        tile = jnp.concatenate([high, low], axis=0)
        msum = msum + jnp.where(sub == 7, low, 0.0)
        if b + 1 < SECTIONS:
            take_split(tile, b + 2)
            send_cells(b + 1, msum)
        take_features(tile, b + 2)
        finish_leaves(first, LEAF_SENDS)
        if b + 1 < SECTIONS:
            beside(b + 1)
    scaled = msum * (-DEMAG / (N_DOM * LEAVES))
    unif = [jnp.broadcast_to(scaled[7:8, j : j + 1], (1, LANES)) for j in range(3)]
    near_pass(
        32 // FAR_UNROLL, FAR_UNROLL, far_first, far_last,
        lambda g, parts: far_store(g, parts, unif), far_a, far_b,
    )
    for b in range(SECTIONS):
        leaf_copy(b).wait_send()
        cell_copy(b).wait_send()


def exchange(
    positions, moments, fwd_leaves, fwd_counts, fwd_cells, leaf_list, leaf_len, cell_list, cell_len
):
    vmem = pl.BlockSpec(memory_space=pltpu.VMEM)
    hbm = pl.BlockSpec(memory_space=pltpu.MemorySpace.HBM)
    dma = pltpu.SemaphoreType.DMA((SECTIONS,))
    return pl.pallas_call(
        exchange_kernel,
        out_shape=(
            jax.ShapeDtypeStruct((LEAF_POOL, 8, LANES), F32),
            jax.ShapeDtypeStruct((LEAVES, 64, 2 * LANES), BF16),
            jax.ShapeDtypeStruct((LEAVES, 8, LANES), F32),
            jax.ShapeDtypeStruct((3, LEAVES, LANES), F32),
            jax.ShapeDtypeStruct((8, LEAVES), jnp.int32),
            jax.ShapeDtypeStruct((LEAVES,), jnp.int32),
        ),
        in_specs=[hbm] * 9,
        out_specs=(vmem,) * 6,
        scratch_shapes=[
            pltpu.VMEM((3, LEAVES, LANES), F32),
            pltpu.VMEM((3, LEAVES, LANES), F32),
            pltpu.SMEM((SECTIONS, 1, LEAF_SENDS), jnp.int32),
            pltpu.SMEM((1, 2, SECTIONS), jnp.int32),
            pltpu.VMEM((SECTIONS, 1, CELL_SENDS), jnp.int32),
            pltpu.SMEM((8, LEAVES), jnp.int32),
            pltpu.SMEM((LEAVES,), jnp.int32),
            pltpu.VMEM((LEAVES, 64), jnp.int32),
            pltpu.SMEM((LEAVES,), jnp.int32),
            pltpu.SemaphoreType.DMA((11,)),
            pltpu.VMEM((48, WIDE + 64), BF16),
            pltpu.VMEM((64, WIDE + 64), BF16),
            pltpu.VMEM((16, LANES), jnp.int32),
            pltpu.VMEM((32, LANES), jnp.int32),
            pltpu.VMEM((32, 64, LANES), F32),
            pltpu.VMEM((32, 64, LANES), F32),
            pltpu.VMEM((LEAVES, 112, 3 * LANES), BF16),
            pltpu.VMEM((8, LANES, 2 * LANES), F32),
            pltpu.VMEM((8, LANES, 2 * LANES), F32),
            pltpu.VMEM((FAR_UNROLL, LANES, 3 * LANES), F32),
            pltpu.VMEM((FAR_UNROLL, LANES, 3 * LANES), F32),
            pltpu.VMEM((SECTIONS, 6 * LEAF_SENDS, LANES), F32),
            pltpu.VMEM((SECTIONS, 6 * LEAF_SENDS, LANES), F32),
            pltpu.VMEM((SECTIONS, 8, LANES), F32),
            pltpu.VMEM((SECTIONS, 8, LANES), F32),
            dma, dma, dma, dma,
        ],
        compiler_params=pltpu.CompilerParams(
            collective_id=0, has_side_effects=True, vmem_limit_bytes=40 * 1024 * 1024
        ),
        name="exchange",
    )(
        *(
            pltpu.with_memory_space_constraint(x, pltpu.MemorySpace.HBM)
            for x in (
                positions, moments, fwd_leaves, fwd_counts, fwd_cells,
                leaf_list, leaf_len, cell_list, cell_len,
            )
        )
    )


def field_kernel(
    pool_ref, sides, near0, far_ref, llist_ref, llen_ref, out_ref, near, todo_ref, buf_a, buf_b
):
    sub = iota((8, LANES), 0)

    def collect(t, count):
        todo_ref[count] = t
        return jnp.where(llen_ref[t] > 2, count + 1, count)

    busy = lax.fori_loop(0, LEAVES, collect, 0)
    near[0:LEAVES] = near0[...]

    def near_items(at):
        n, k = at
        todo = []
        for _ in range(NEAR_UNROLL):
            t = todo_ref[jnp.minimum(n, LEAVES - 1)]
            t = jnp.where(n < busy, t, 0)
            todo += [jnp.where(n < busy, t, LEAVES), t, llist_ref[k, t], k]
            more = k + 1 < llen_ref[t]
            n, k = jnp.where(more, n, n + 1), jnp.where(more, k + 1, 2)
        return (n, k), tuple(todo)

    def near_both(then, now, write, read, acc):
        parts = []
        for i in range(NEAR_UNROLL):
            write[i] = near_product(sides[then[4 * i + 1]], pool_ref[then[4 * i + 2]])
            parts.append(near_sums(read.at[i], pool_ref[now[4 * i + 2]], sub))
        for i in range(NEAR_UNROLL):
            acc = jnp.where(now[4 * i + 3] == 2, near0[now[4 * i + 1]], acc) + parts[i]
            near[now[4 * i]] = acc
        return acc

    def near_body(carry):
        at, now, then, acc = carry
        at, later = near_items(at)
        acc = near_both(then, now, buf_b, buf_a, acc)
        at, last = near_items(at)
        acc = near_both(later, then, buf_a, buf_b, acc)
        return at, later, last, acc

    at, now = near_items((jnp.int32(0), jnp.int32(2)))
    at, then = near_items(at)
    for i in range(NEAR_UNROLL):
        buf_a[i] = near_product(sides[now[4 * i + 1]], pool_ref[now[4 * i + 2]])
    lax.while_loop(
        lambda carry: carry[1][0] < LEAVES,
        near_body,
        (at, now, then, jnp.zeros((8, LANES), F32)),
    )

    for d in range(3):
        got = near[0:LEAVES, d, :]
        x = pool_ref[0:LEAVES, d, :]
        out_ref[d] = (
            3.0 * (x * near[0:LEAVES, 6, :] - got) - near[0:LEAVES, 3 + d, :] + far_ref[d]
        )


def field(pool, sides, near, far, leaf_list, leaf_len):
    vmem = pl.BlockSpec(memory_space=pltpu.VMEM)
    smem = pl.BlockSpec(memory_space=pltpu.SMEM)
    return pl.pallas_call(
        field_kernel,
        out_shape=jax.ShapeDtypeStruct((3, LEAVES, LANES), F32),
        in_specs=[vmem, vmem, vmem, vmem, smem, smem],
        out_specs=vmem,
        scratch_shapes=[
            pltpu.VMEM((LEAVES + 1, 8, LANES), F32),
            pltpu.SMEM((LEAVES + 8,), jnp.int32),
            pltpu.VMEM((NEAR_UNROLL, LANES, 2 * LANES), F32),
            pltpu.VMEM((NEAR_UNROLL, LANES, 2 * LANES), F32),
        ],
        compiler_params=pltpu.CompilerParams(vmem_limit_bytes=16 * 1024 * 1024),
        name="field",
    )(pool, sides, near, far, leaf_list, leaf_len)


def per_device(
    positions, moments, fwd_cells, fwd_leaves, fwd_counts, cell_list, cell_len, leaf_list, leaf_len
):
    swap = lambda x: jnp.transpose(x, (1, 0, 2))
    pool, sides, near, far, lists, lens = exchange(
        swap(positions), swap(moments), swap(fwd_leaves), jnp.transpose(fwd_counts, (0, 2, 1)),
        swap(fwd_cells), leaf_list.T, leaf_len, cell_list, cell_len,
    )
    return swap(field(pool, sides, near, far, lists, lens))


def solution(mesh):
    row = P("dom", None)
    cube = P("dom", None, None)
    return jax.shard_map(
        per_device,
        mesh=mesh,
        in_specs=(cube, cube, cube, cube, cube, row, P("dom"), row, P("dom")),
        out_specs=cube,
        check_vma=False,
    )
```

```python
import functools

import jax
import jax.numpy as jnp
from jax import lax
from jax.experimental import pallas as pl
from jax.experimental.pallas import tpu as pltpu
from jax.sharding import PartitionSpec as P

F32 = jnp.float32
BF16 = jnp.bfloat16
DEMAG = 4.1887902047863905
LEAVES = 64
PARENTS = 8
OWN = LEAVES + PARENTS
SECTIONS = 9
CELL_SENDS = 64
LEAF_SENDS = 20
LEAF_POOL = LEAVES + SECTIONS * LEAF_SENDS
WIDE = 128 + SECTIONS * CELL_SENDS
LANES = 128
N_DOM = 512
NEAR_UNROLL = 8
LEAD = 3
HELD = (LEAVES + 6 * LEAF_SENDS, LEAVES + 7 * LEAF_SENDS)
FAR_UNROLL = 4


def iota(shape, dim):
    return lax.broadcasted_iota(jnp.int32, shape, dim)


def pieces(x):
    first = x.astype(BF16).astype(F32)
    rest = x - first
    second = rest.astype(BF16).astype(F32)
    return first, second, rest - second


def cell_features(tile):
    row = lambda i: tile[i : i + 1]
    sec = lambda k, j: row(6 + 3 * k + j)
    c = [row(d) for d in range(3)]
    tot = [row(3 + d) for d in range(3)]
    xx, yy, zz = [2.0 * sec(d, d) for d in range(3)]
    xy, xz, yz = sec(0, 1) + sec(1, 0), sec(0, 2) + sec(2, 0), sec(1, 2) + sec(2, 1)
    turn = [
        xx * c[0] + xy * c[1] + xz * c[2],
        xy * c[0] + yy * c[1] + yz * c[2],
        xz * c[0] + yz * c[1] + zz * c[2],
    ]
    main = jnp.concatenate(
        [tile[0:6], xx, yy, zz, xy, xz, yz] + turn + [jnp.ones((1, LANES), F32)], axis=0
    )
    rest = jnp.concatenate(
        [
            c[0] * c[0] + c[1] * c[1] + c[2] * c[2],
            -(tot[0] * c[0] + tot[1] * c[1] + tot[2] * c[2])
            - (sec(0, 0) + sec(1, 1) + sec(2, 2)),
            2.5 * (c[0] * turn[0] + c[1] * turn[1] + c[2] * turn[2]),
        ],
        axis=0,
    )
    blocks = list(pieces(main)) + list(pieces(rest)) + [jnp.zeros((7, LANES), F32)]
    return jnp.concatenate(blocks, axis=0).astype(BF16)


def far_side(block):
    x = [block[d : d + 1] for d in range(3)]
    none = lambda n: jnp.zeros((n, LANES), F32)
    x3 = block[0:3]
    quad = jnp.concatenate([-2.0 * x3, none(12), block[6:7]], axis=0)
    along = jnp.concatenate([none(3), x3, none(10)], axis=0)
    bend = jnp.concatenate(
        [
            none(6), 2.5 * (x[0] * x[0]), 2.5 * (x[1] * x[1]), 2.5 * (x[2] * x[2]),
            5.0 * (x[0] * x[1]), 5.0 * (x[0] * x[2]), 5.0 * (x[1] * x[2]),
            -5.0 * x3, none(1),
        ],
        axis=0,
    )
    sub = iota((16, LANES), 0)
    cols = []
    for i, part in enumerate((quad, along, bend)):
        p0, p1, p2 = pieces(part)
        ones = jnp.where((sub < 9 + (i == 0)) & (lax.rem(sub, 3) == i), 1.0, 0.0)
        cols.append(jnp.concatenate([p0, p1, p2, p0, p1, p0, ones], axis=0).astype(BF16))
    return jnp.concatenate(cols, axis=1)


def far_product(side, picked):
    a0, a1, a2, rest = picked[0:16], picked[16:32], picked[32:48], picked[48:64]
    rest = jnp.where(iota((16, 64), 0) == 9, 1.0, rest)
    stack = jnp.concatenate([a0, a0, a0, a1, a1, a2, rest], axis=0).astype(BF16)
    return lax.dot_general(stack, side, (((0,), (0,)), ((), ())), preferred_element_type=F32)


def far_sums(both, picked, block):
    weights = [[], [], []]
    for c in range(4):
        rows = slice(16 * c, 16 * c + 16)
        inv = lax.rsqrt(both[rows, 0:LANES])
        inv2 = inv * inv
        inv3 = inv2 * inv
        inv5 = inv3 * inv2
        coef = (both[rows, LANES : 2 * LANES] + both[rows, 2 * LANES :] * inv2) * inv5
        for out, weight in zip(weights, (coef, inv3, inv5)):
            high = weight.astype(BF16)
            low = (weight - high.astype(F32)).astype(BF16)
            out.append(jnp.concatenate([high, low], axis=1))
    sub = iota((16, 64), 0)

    def lefts(part, one):
        first = jnp.where(sub < 3, part, jnp.where(sub == 3, one, 0.0))
        second = jnp.where((sub >= 10) & (sub < 13), pltpu.roll(part, 7, 0), 0.0)
        third = jnp.where(
            sub < 3,
            -pltpu.roll(part, 4, 0),
            jnp.where((sub >= 4) & (sub < 10), pltpu.roll(part, 14, 0), 0.0),
        )
        return first, second, third

    total = None
    for weight, high_l, low_l in zip(weights, lefts(picked[0:16], 1.0), lefts(picked[16:32], 0.0)):
        left = jnp.concatenate([high_l, low_l], axis=0).astype(BF16)
        part = jnp.dot(left, jnp.concatenate(weight, axis=0), preferred_element_type=F32)
        total = part if total is None else total + part
    got = (total[0:16, 0:LANES] + total[16:32, 0:LANES]) + total[0:16, LANES:]
    x = [block[d : d + 1] for d in range(3)]
    q = [got[4 + i : 5 + i] for i in range(6)]
    turn = [
        q[0] * x[0] + q[3] * x[1] + q[4] * x[2],
        q[3] * x[0] + q[1] * x[1] + q[5] * x[2],
        q[4] * x[0] + q[5] * x[1] + q[2] * x[2],
    ]
    return [
        3.0 * (x[d] * got[3:4] - got[d : d + 1] - turn[d]) - got[10 + d : 11 + d]
        for d in range(3)
    ]


def own_tile(pos_ref, mom_ref):
    pos = [pos_ref[k] for k in range(3)]
    mom = [mom_ref[k] for k in range(3)]
    cen = [jnp.sum(p, axis=1, keepdims=True) * (1.0 / LANES) for p in pos]
    tot = [jnp.sum(m, axis=1, keepdims=True) for m in mom]
    off = [pos[k] - cen[k] for k in range(3)]
    sec = [
        [jnp.sum(off[k] * mom[j], axis=1, keepdims=True) for j in range(3)] for k in range(3)
    ]
    full = lambda x: jnp.broadcast_to(x, (LEAVES, LANES)).reshape(PARENTS, 8, LANES)
    fcen = [full(c) for c in cen]
    ftot = [full(c) for c in tot]
    fsec = [[full(sec[k][j]) for j in range(3)] for k in range(3)]
    pcen = [jnp.sum(c, axis=1, keepdims=True) * 0.125 for c in fcen]
    ptot = [jnp.sum(c, axis=1) for c in ftot]
    psec = [
        [jnp.sum(fsec[k][j] + (fcen[k] - pcen[k]) * ftot[j], axis=1) for j in range(3)]
        for k in range(3)
    ]
    leaf = fcen + ftot + [fsec[k][j] for k in range(3) for j in range(3)]
    up = [c[:, 0, :] for c in pcen] + ptot + [psec[k][j] for k in range(3) for j in range(3)]
    lane = iota((LEAVES, LANES), 1)
    lane_p = iota((PARENTS, LANES), 1)
    rows = jnp.zeros((LEAVES, LANES), F32)
    rows_p = jnp.zeros((PARENTS, LANES), F32)
    for i in range(15):
        rows = jnp.where(lane == i, leaf[i].reshape(LEAVES, LANES), rows)
        rows_p = jnp.where(lane_p == i, up[i], rows_p)
    every = jnp.concatenate([rows, rows_p, jnp.zeros((LANES - OWN, LANES), F32)], axis=0)
    sums = [jnp.sum(p, axis=0, keepdims=True) for p in ptot]
    return jnp.transpose(every)[0:16], sums


def target_side(block, sub):
    cut = pieces(block)
    zero = jnp.zeros((16, LANES), F32)
    order = (0, 1, 2, 0, 1, 0)
    lead = (True, False, False, True, False, True)
    quad, along = [], []
    for p, flag in zip(order, lead):
        mark = 1.0 if flag else 0.0
        quad.append(jnp.where(sub < 3, -2.0 * cut[p], jnp.where(sub == 6, mark, 0.0)))
        turned = pltpu.roll(cut[p], 3, 0)
        along.append(
            jnp.where((sub >= 3) & (sub < 6), turned, jnp.where(sub == 7, -mark, 0.0))
        )
    quad.append(
        jnp.where(sub == 6, cut[0], jnp.where(sub == 7, pltpu.roll(cut[1], 1, 0), 0.0))
    )
    quad.append(jnp.where(sub == 6, cut[2], jnp.where(sub == 7, 1.0, 0.0)))
    along.append(zero)
    return jnp.concatenate(
        [jnp.concatenate(quad, axis=0), jnp.concatenate(along, axis=0)], axis=1
    ).astype(BF16)


def near_product(side, block):
    cut = pieces(block)
    source = jnp.concatenate(
        [cut[0], cut[0], cut[0], cut[1], cut[1], cut[2], jnp.ones((16, LANES), F32)], axis=0
    ).astype(BF16)
    return lax.dot_general(
        source, side, (((0,), (0,)), ((), ())), preferred_element_type=F32
    )


def near_sums(both, block, sub):
    parts = [[], [], [], []]
    for c in range(LANES // 16):
        quad = both[16 * c : 16 * c + 16, 0:LANES]
        along = both[16 * c : 16 * c + 16, LANES:]
        inv = lax.rsqrt(quad)
        inv2 = inv * inv
        inv3 = inv2 * inv
        coef = along * (inv3 * inv2)
        for i, weight in enumerate((coef, inv3)):
            high = weight.astype(BF16)
            parts[i].append(high)
            parts[2 + i].append((weight - high.astype(F32)).astype(BF16))
    high = jnp.concatenate(parts[0] + parts[1], axis=0)
    low = jnp.concatenate(parts[2] + parts[3], axis=0)

    def sums(part, one):
        c_side = jnp.where(sub < 3, part, jnp.where(sub == 6, one, 0.0))
        w_side = jnp.where((sub >= 3) & (sub < 6), part, 0.0)
        return jnp.concatenate([c_side, w_side], axis=1)

    cut = pieces(block)
    left = jnp.concatenate([sums(cut[0], 1.0), sums(cut[1], 0.0)], axis=0).astype(BF16)
    got = jnp.dot(left, high, preferred_element_type=F32)
    more = jnp.dot(left, low, preferred_element_type=F32)
    return (got[0:8] + got[8:16]) + more[0:8]


def near_pass(steps, width, first, last, store, buf_a, buf_b):
    def both(then, now, write, read):
        parts = []
        for i in range(width + LEAD):
            if i < width:
                first(then, i, write)
            if i >= LEAD:
                parts.append(last(now, i - LEAD, read))
        store(now, parts)

    for i in range(width):
        first(0, i, buf_a)

    def body(i, carry):
        both(2 * i + 1, 2 * i, buf_b, buf_a)
        both(jnp.minimum(2 * i + 2, steps - 1), 2 * i + 1, buf_a, buf_b)
        return carry

    lax.fori_loop(0, steps // 2, body, 0)


def exchange_kernel(
    pos_in, mom_in, fl_in, fn_in, fc_in, llist_in, llen_in, clist_in, clen_in,
    pool_ref, sides, near, far_ref, llist_out, llen_out,
    pos_ref, mom_ref, fl_ref, fn_ref, fc_ref, llist_ref, llen_ref, clist_ref, clen_ref, in_sem,
    split, feats, index, cindex, gath, fsides, buf_a, buf_b, far_a, far_b, pick_a, pick_b, kept_a, kept_b,
    send_l, recv_l, send_c, recv_c, sl_sem, rl_sem, sc_sem, rc_sem,
):
    loads = [
        pltpu.make_async_copy(src, dst, in_sem.at[i])
        for i, (src, dst) in enumerate(
            (
                (pos_in, pos_ref), (mom_in, mom_ref), (fl_in, fl_ref), (fn_in, fn_ref),
                (fc_in, fc_ref), (llist_in, llist_ref), (llen_in, llen_ref),
                (clist_in, clist_ref), (clen_in, clen_ref),
                (llist_in, llist_out), (llen_in, llen_out),
            )
        )
    ]
    for load in loads:
        load.start()
    me = lax.axis_index("dom")
    partners = []
    for b in range(SECTIONS):
        stride = 1 << b
        partners.append(me + (1 - 2 * lax.rem(me // stride, 2)) * stride)
    barrier = pltpu.get_barrier_semaphore()
    for other in partners:
        pl.semaphore_signal(
            barrier, inc=1, device_id=(other,), device_id_type=pl.DeviceIdType.MESH
        )
    for load in loads:
        load.wait()
    for d in range(3):
        pool_ref[0:LEAVES, d, :] = pos_ref[d]
        pool_ref[0:LEAVES, 3 + d, :] = mom_ref[d]

    lane = iota((8, LANES), 1)
    sub = iota((8, LANES), 0)
    index[...] = jnp.full((16, LANES), -1, jnp.int32)
    for b in range(SECTIONS):
        index[b : b + 1, 0:CELL_SENDS] = fc_ref[b]
    raw = index[...]
    index[...] = jnp.where(raw < OWN, raw, raw + (LANES - OWN))
    for half in range(2):
        rows = clist_ref[half * 32 : half * 32 + 32, :]
        cindex[:, half * 64 : half * 64 + 64] = jnp.where(
            rows < OWN, rows, rows + (LANES - OWN)
        )

    def leaf_copy(b):
        return pltpu.make_async_remote_copy(
            src_ref=send_l.at[b], dst_ref=recv_l.at[b],
            send_sem=sl_sem.at[b], recv_sem=rl_sem.at[b],
            device_id=(partners[b],), device_id_type=pl.DeviceIdType.MESH,
        )

    def cell_copy(b):
        return pltpu.make_async_remote_copy(
            src_ref=send_c.at[b], dst_ref=recv_c.at[b],
            send_sem=sc_sem.at[b], recv_sem=rc_sem.at[b],
            device_id=(partners[b],), device_id_type=pl.DeviceIdType.MESH,
        )

    def send_leaves(b):
        live = fn_ref[0, 1, b]
        for s in range(LEAF_SENDS):
            block = pool_ref[fl_ref[b, 0, s]][0:6]
            send_l[b, 6 * s : 6 * s + 6, :] = jnp.where(s < live, block, 0.0)
        leaf_copy(b).start()

    def take_tile(tile, at, ref, rows):
        if at % 2:
            kept = ref[:, at // 2 * LANES : at // 2 * LANES + LANES]
            turned = pltpu.roll(rows.astype(F32), CELL_SENDS, 1).astype(BF16)
            wide = iota(rows.shape, 1)
            rows = jnp.where(wide < CELL_SENDS, kept.astype(F32), turned.astype(F32)).astype(BF16)
        ref[:, at // 2 * LANES : at // 2 * LANES + LANES] = rows

    def take_split(tile, at):
        take_tile(tile, at, split, jnp.concatenate(pieces(tile), axis=0).astype(BF16))

    def take_features(tile, at):
        take_tile(tile, at, feats, cell_features(tile))

    def send_cells(b, msum):
        depth = LANES * ((b + 3) // 2)
        wanted = jnp.where(lane[0:1] < fn_ref[0, 0, b], index[b : b + 1, :], -1)
        hot = jnp.where(iota((depth, LANES), 0) == wanted, 1.0, 0.0).astype(BF16)
        got = jnp.dot(split[:, 0:depth], hot, preferred_element_type=F32)
        got = (got[0:16] + got[16:32]) + got[32:48]
        low = jnp.where(sub == 7, msum, got[8:16])
        send_c[b] = jnp.where(lane < CELL_SENDS, got[0:8], pltpu.roll(low, CELL_SENDS, 1))
        cell_copy(b).start()

    def finish_leaves(first, count):
        part = [pool_ref[first : first + count, i, :] for i in range(6)]
        pool_ref[first : first + count, 6, :] = (
            part[0] * part[0] + part[1] * part[1] + part[2] * part[2]
        )
        pool_ref[first : first + count, 7, :] = (
            part[0] * part[3] + part[1] * part[4] + part[2] * part[5]
        )

    def prepare_near(g, carry):
        for i in range(2):
            t = 2 * g + i
            sides[t] = target_side(pool_ref[t], sub)
        return carry

    def prepare_far(g, carry):
        for i in range(2):
            t = 2 * g + i
            fsides[t] = far_side(pool_ref[t])
        return carry

    def near_source(t, k, held):
        if k == 0:
            return pool_ref[t]
        src = llist_ref[k, t]
        use = llen_ref[t] > k
        if k > 1:
            use = use & (src < held)
        return jnp.where(use, pool_ref[src], 0.0)

    def near_steps(t0, leaves, places, held=0):
        n = len(places)

        def spot(g, i):
            return t0 + 8 // n * g + i // n, places[i % n]

        def first(g, i, buf):
            t, k = spot(g, i)
            buf[i] = near_product(sides[t], near_source(t, k, held))

        def last(g, i, buf):
            t, k = spot(g, i)
            return near_sums(buf.at[i], near_source(t, k, held), sub)

        def store(g, parts):
            for i in range(0, 8, n):
                t, k = spot(g, i)
                got = parts[i] if n == 1 else parts[i] + parts[i + 1]
                near[t] = got if k == 0 else near[t] + got

        near_pass(leaves * n // 8, 8, first, last, store, buf_a, buf_b)

    def wanted_cells(i):
        row = cindex[pl.ds(i, 1), :]
        k = jnp.where(lane[0:1] < 64, lane[0:1], lane[0:1] - 64)
        most = jnp.where(lane[0:1] < 64, clen_ref[i], clen_ref[i + 32])
        return jnp.where(k < most, row, -1)

    old = LANES + (SECTIONS - 1) * CELL_SENDS

    def gather(low, high):
        def body(g, carry):
            for j in range(4):
                i = 4 * g + j
                spot = iota((high - low, LANES), 0) + low
                hot = jnp.where(spot == wanted_cells(i), 1.0, 0.0).astype(BF16)
                got = jnp.dot(feats[:, low:high], hot, preferred_element_type=F32)
                gath[i] = got if low == 0 else gath[i] + got
            return carry

        lax.fori_loop(0, 8, body, 0)

    def far_pick(g, j, buf):
        i = FAR_UNROLL * g + j
        hot = jnp.where(iota((64, LANES), 0) + old == wanted_cells(i), 1.0, 0.0).astype(BF16)
        picked = gath[i] + jnp.dot(feats[:, old : old + 64], hot, preferred_element_type=F32)
        buf[2 * j] = picked
        buf[2 * j + 1] = pltpu.roll(picked, 64, 1)

    def far_middle(g, j, read, buf):
        both, kept = buf
        for h in range(2):
            part = read[2 * j + h]
            kept[2 * j + h] = part[0:32]
            both[2 * j + h] = far_product(fsides[FAR_UNROLL * g + j + 32 * h], part[:, 0:64])

    def far_last(g, j, buf):
        i = FAR_UNROLL * g + j
        both, kept = buf
        return [
            far_sums(both.at[2 * j + h], kept[2 * j + h][:, 0:64], pool_ref[i + 32 * h])
            for h in range(2)
        ]

    def far_store(g, parts, unif):
        for j in range(FAR_UNROLL):
            for half in range(2):
                t = FAR_UNROLL * g + j + 32 * half
                for d in range(3):
                    far_ref[d, pl.ds(t, 1), :] = parts[j][half][d] + unif[d]

    def beside(b):
        if b == 0:
            lax.fori_loop(0, LEAVES // 2, prepare_near, 0)
        elif b == 1:
            near_steps(0, 16, (0, 1))
        elif b == 2:
            near_steps(16, 16, (0, 1))
        elif b == 3:
            near_steps(32, 32, (0, 1))
        elif b == 4:
            lax.fori_loop(0, LEAVES // 2, prepare_far, 0)
        elif b == 5:
            gather(0, 384)
        elif b == 6:
            near_steps(0, LEAVES, (2,), HELD[0])
        elif b == 7:
            near_steps(0, 32, (3,), HELD[1])
        elif b == 8:
            near_steps(32, 32, (3,), HELD[1])
            gather(384, old)

    pl.semaphore_wait(barrier, SECTIONS)
    send_leaves(0)
    tile, sums = own_tile(pos_ref, mom_ref)
    msum = jnp.zeros((8, LANES), F32)
    for j in range(3):
        msum = jnp.where((sub == 7) & (lane == j), sums[j], msum)
    take_split(tile, 0)
    send_cells(0, msum)
    finish_leaves(0, LEAVES)
    take_features(tile, 0)
    beside(0)
    for b in range(SECTIONS):
        first = LEAVES + b * LEAF_SENDS
        leaf_copy(b).wait_recv()
        for s in range(LEAF_SENDS):
            pool_ref[first + s, 0:6, :] = recv_l[b, 6 * s : 6 * s + 6, :]
        if b + 1 < SECTIONS:
            send_leaves(b + 1)
        cell_copy(b).wait_recv()
        got = recv_c[b]
        low = jnp.where(lane < CELL_SENDS, pltpu.roll(got, CELL_SENDS, 1), 0.0)
        high = jnp.where(lane < CELL_SENDS, got, 0.0)
        tile = jnp.concatenate([high, low], axis=0)
        msum = msum + jnp.where(sub == 7, low, 0.0)
        if b + 1 < SECTIONS:
            take_split(tile, b + 2)
            send_cells(b + 1, msum)
        take_features(tile, b + 2)
        finish_leaves(first, LEAF_SENDS)
        if b + 1 < SECTIONS:
            beside(b + 1)
    scaled = msum * (-DEMAG / (N_DOM * LEAVES))
    unif = [jnp.broadcast_to(scaled[7:8, j : j + 1], (1, LANES)) for j in range(3)]
    steps = 32 // FAR_UNROLL
    capped = lambda g: jnp.minimum(g, steps - 1)

    def far_round(g, pick_w, pick_r, far_w, far_r):
        parts = []
        for j in range(FAR_UNROLL):
            far_pick(capped(g + 2), j, pick_w)
            far_middle(capped(g + 1), j, pick_r, far_w)
            parts.append(far_last(g, j, far_r))
        far_store(g, parts, unif)

    for j in range(FAR_UNROLL):
        far_pick(0, j, pick_a)
        far_pick(1, j, pick_b)
    for j in range(FAR_UNROLL):
        far_middle(0, j, pick_a, (far_a, kept_a))

    def far_body(i, carry):
        far_round(2 * i, pick_a, pick_b, (far_b, kept_b), (far_a, kept_a))
        far_round(2 * i + 1, pick_b, pick_a, (far_a, kept_a), (far_b, kept_b))
        return carry

    lax.fori_loop(0, steps // 2, far_body, 0)
    for b in range(SECTIONS):
        leaf_copy(b).wait_send()
        cell_copy(b).wait_send()


def exchange(
    positions, moments, fwd_leaves, fwd_counts, fwd_cells, leaf_list, leaf_len, cell_list, cell_len
):
    vmem = pl.BlockSpec(memory_space=pltpu.VMEM)
    hbm = pl.BlockSpec(memory_space=pltpu.MemorySpace.HBM)
    dma = pltpu.SemaphoreType.DMA((SECTIONS,))
    return pl.pallas_call(
        exchange_kernel,
        out_shape=(
            jax.ShapeDtypeStruct((LEAF_POOL, 8, LANES), F32),
            jax.ShapeDtypeStruct((LEAVES, 64, 2 * LANES), BF16),
            jax.ShapeDtypeStruct((LEAVES, 8, LANES), F32),
            jax.ShapeDtypeStruct((3, LEAVES, LANES), F32),
            jax.ShapeDtypeStruct((8, LEAVES), jnp.int32),
            jax.ShapeDtypeStruct((LEAVES,), jnp.int32),
        ),
        in_specs=[hbm] * 9,
        out_specs=(vmem,) * 6,
        scratch_shapes=[
            pltpu.VMEM((3, LEAVES, LANES), F32),
            pltpu.VMEM((3, LEAVES, LANES), F32),
            pltpu.SMEM((SECTIONS, 1, LEAF_SENDS), jnp.int32),
            pltpu.SMEM((1, 2, SECTIONS), jnp.int32),
            pltpu.VMEM((SECTIONS, 1, CELL_SENDS), jnp.int32),
            pltpu.SMEM((8, LEAVES), jnp.int32),
            pltpu.SMEM((LEAVES,), jnp.int32),
            pltpu.VMEM((LEAVES, 64), jnp.int32),
            pltpu.SMEM((LEAVES,), jnp.int32),
            pltpu.SemaphoreType.DMA((11,)),
            pltpu.VMEM((48, WIDE + 64), BF16),
            pltpu.VMEM((64, WIDE + 64), BF16),
            pltpu.VMEM((16, LANES), jnp.int32),
            pltpu.VMEM((32, LANES), jnp.int32),
            pltpu.VMEM((32, 64, LANES), F32),
            pltpu.VMEM((LEAVES, 112, 3 * LANES), BF16),
            pltpu.VMEM((8, LANES, 2 * LANES), F32),
            pltpu.VMEM((8, LANES, 2 * LANES), F32),
            pltpu.VMEM((2 * FAR_UNROLL, 64, 3 * LANES), F32),
            pltpu.VMEM((2 * FAR_UNROLL, 64, 3 * LANES), F32),
            pltpu.VMEM((2 * FAR_UNROLL, 64, LANES), F32),
            pltpu.VMEM((2 * FAR_UNROLL, 64, LANES), F32),
            pltpu.VMEM((2 * FAR_UNROLL, 32, LANES), F32),
            pltpu.VMEM((2 * FAR_UNROLL, 32, LANES), F32),
            pltpu.VMEM((SECTIONS, 6 * LEAF_SENDS, LANES), F32),
            pltpu.VMEM((SECTIONS, 6 * LEAF_SENDS, LANES), F32),
            pltpu.VMEM((SECTIONS, 8, LANES), F32),
            pltpu.VMEM((SECTIONS, 8, LANES), F32),
            dma, dma, dma, dma,
        ],
        compiler_params=pltpu.CompilerParams(
            collective_id=0, has_side_effects=True, vmem_limit_bytes=40 * 1024 * 1024
        ),
        name="exchange",
    )(
        *(
            pltpu.with_memory_space_constraint(x, pltpu.MemorySpace.HBM)
            for x in (
                positions, moments, fwd_leaves, fwd_counts, fwd_cells,
                leaf_list, leaf_len, cell_list, cell_len,
            )
        )
    )


def field_kernel(
    pool_ref, sides, near0, far_ref, llist_ref, llen_ref, out_ref, near, todo_ref, from_ref,
    buf_a, buf_b
):
    sub = iota((8, LANES), 0)

    busy = jnp.int32(0)
    for t in range(LEAVES):
        size = llen_ref[t]
        late = (size > 2) & (llist_ref[2, t] >= HELD[0])
        again = (size > 3) & (llist_ref[3, t] >= HELD[1])
        start = jnp.where(late, 2, jnp.where(again, 3, 4))
        todo_ref[busy] = t
        from_ref[busy] = start
        busy = busy + (start < size).astype(jnp.int32)
    near[0:LEAVES] = near0[...]

    def near_items(at):
        n, k = at
        todo = []
        for _ in range(NEAR_UNROLL):
            here = jnp.minimum(n, LEAVES - 1)
            t = jnp.where(n < busy, todo_ref[here], 0)
            start = from_ref[here]
            k = jnp.where(k < 0, jnp.where(n < busy, start, 2), k)
            src = llist_ref[k, t]
            used = (k != 3) | (src >= HELD[1])
            todo += [
                jnp.where(n < busy, t, LEAVES), t, src,
                (k == start).astype(jnp.int32), used.astype(jnp.int32),
            ]
            more = k + 1 < llen_ref[t]
            n, k = jnp.where(more, n, n + 1), jnp.where(more, k + 1, -1)
        return (n, k), tuple(todo)

    def source(todo, i):
        return jnp.where(todo[5 * i + 4] > 0, pool_ref[todo[5 * i + 2]], 0.0)

    def near_both(then, now, write, read, acc):
        parts = []
        for i in range(NEAR_UNROLL):
            write[i] = near_product(sides[then[5 * i + 1]], source(then, i))
            parts.append(near_sums(read.at[i], source(now, i), sub))
        for i in range(NEAR_UNROLL):
            acc = jnp.where(now[5 * i + 3] > 0, near0[now[5 * i + 1]], acc) + parts[i]
            near[now[5 * i]] = acc
        return acc

    def near_body(carry):
        at, now, then, acc = carry
        at, later = near_items(at)
        acc = near_both(then, now, buf_b, buf_a, acc)
        at, last = near_items(at)
        acc = near_both(later, then, buf_a, buf_b, acc)
        return at, later, last, acc

    at, now = near_items((jnp.int32(0), jnp.int32(-1)))
    at, then = near_items(at)
    for i in range(NEAR_UNROLL):
        buf_a[i] = near_product(sides[now[5 * i + 1]], source(now, i))
    lax.while_loop(
        lambda carry: carry[1][0] < LEAVES,
        near_body,
        (at, now, then, jnp.zeros((8, LANES), F32)),
    )

    for d in range(3):
        got = near[0:LEAVES, d, :]
        x = pool_ref[0:LEAVES, d, :]
        out_ref[d] = (
            3.0 * (x * near[0:LEAVES, 6, :] - got) - near[0:LEAVES, 3 + d, :] + far_ref[d]
        )


def field(pool, sides, near, far, leaf_list, leaf_len):
    vmem = pl.BlockSpec(memory_space=pltpu.VMEM)
    smem = pl.BlockSpec(memory_space=pltpu.SMEM)
    return pl.pallas_call(
        field_kernel,
        out_shape=jax.ShapeDtypeStruct((3, LEAVES, LANES), F32),
        in_specs=[vmem, vmem, vmem, vmem, smem, smem],
        out_specs=vmem,
        scratch_shapes=[
            pltpu.VMEM((LEAVES + 1, 8, LANES), F32),
            pltpu.SMEM((LEAVES,), jnp.int32),
            pltpu.SMEM((LEAVES,), jnp.int32),
            pltpu.VMEM((NEAR_UNROLL, LANES, 2 * LANES), F32),
            pltpu.VMEM((NEAR_UNROLL, LANES, 2 * LANES), F32),
        ],
        compiler_params=pltpu.CompilerParams(vmem_limit_bytes=16 * 1024 * 1024),
        name="field",
    )(pool, sides, near, far, leaf_list, leaf_len)


def per_device(
    positions, moments, fwd_cells, fwd_leaves, fwd_counts, cell_list, cell_len, leaf_list, leaf_len
):
    swap = lambda x: jnp.transpose(x, (1, 0, 2))
    pool, sides, near, far, lists, lens = exchange(
        swap(positions), swap(moments), swap(fwd_leaves), jnp.transpose(fwd_counts, (0, 2, 1)),
        swap(fwd_cells), leaf_list.T, leaf_len, cell_list, cell_len,
    )
    return swap(field(pool, sides, near, far, lists, lens))


def solution(mesh):
    row = P("dom", None)
    cube = P("dom", None, None)
    return jax.shard_map(
        per_device,
        mesh=mesh,
        in_specs=(cube, cube, cube, cube, cube, row, P("dom"), row, P("dom")),
        out_specs=cube,
        check_vma=False,
    )
```

```python
import functools

import jax
import jax.numpy as jnp
from jax import lax
from jax.experimental import pallas as pl
from jax.experimental.pallas import tpu as pltpu
from jax.sharding import PartitionSpec as P

F32 = jnp.float32
BF16 = jnp.bfloat16
DEMAG = 4.1887902047863905
LEAVES = 64
PARENTS = 8
OWN = LEAVES + PARENTS
SECTIONS = 9
CELL_SENDS = 64
LEAF_SENDS = 20
LEAF_POOL = LEAVES + SECTIONS * LEAF_SENDS
WIDE = 128 + SECTIONS * CELL_SENDS
LANES = 128
N_DOM = 512
NEAR_UNROLL = 8
LEAD = 3
ENTRIES = 6 * LEAVES
STAGES = ((0, 64, 6), (64, 32, 7), (96, 32, 8))
DONE = STAGES[-1][0] + STAGES[-1][1]


def held(b):
    return LEAVES + b * LEAF_SENDS
FAR_UNROLL = 4


def iota(shape, dim):
    return lax.broadcasted_iota(jnp.int32, shape, dim)


def pieces(x):
    first = x.astype(BF16).astype(F32)
    rest = x - first
    second = rest.astype(BF16).astype(F32)
    return first, second, rest - second


def cell_features(tile):
    row = lambda i: tile[i : i + 1]
    sec = lambda k, j: row(6 + 3 * k + j)
    c = [row(d) for d in range(3)]
    tot = [row(3 + d) for d in range(3)]
    xx, yy, zz = [2.0 * sec(d, d) for d in range(3)]
    xy, xz, yz = sec(0, 1) + sec(1, 0), sec(0, 2) + sec(2, 0), sec(1, 2) + sec(2, 1)
    turn = [
        xx * c[0] + xy * c[1] + xz * c[2],
        xy * c[0] + yy * c[1] + yz * c[2],
        xz * c[0] + yz * c[1] + zz * c[2],
    ]
    main = jnp.concatenate(
        [tile[0:6], xx, yy, zz, xy, xz, yz] + turn + [jnp.ones((1, LANES), F32)], axis=0
    )
    rest = jnp.concatenate(
        [
            c[0] * c[0] + c[1] * c[1] + c[2] * c[2],
            -(tot[0] * c[0] + tot[1] * c[1] + tot[2] * c[2])
            - (sec(0, 0) + sec(1, 1) + sec(2, 2)),
            2.5 * (c[0] * turn[0] + c[1] * turn[1] + c[2] * turn[2]),
        ],
        axis=0,
    )
    blocks = list(pieces(main)) + list(pieces(rest)) + [jnp.zeros((7, LANES), F32)]
    return jnp.concatenate(blocks, axis=0).astype(BF16)


def far_side(block):
    x = [block[d : d + 1] for d in range(3)]
    none = lambda n: jnp.zeros((n, LANES), F32)
    x3 = block[0:3]
    quad = jnp.concatenate([-2.0 * x3, none(12), block[6:7]], axis=0)
    along = jnp.concatenate([none(3), x3, none(10)], axis=0)
    bend = jnp.concatenate(
        [
            none(6), 2.5 * (x[0] * x[0]), 2.5 * (x[1] * x[1]), 2.5 * (x[2] * x[2]),
            5.0 * (x[0] * x[1]), 5.0 * (x[0] * x[2]), 5.0 * (x[1] * x[2]),
            -5.0 * x3, none(1),
        ],
        axis=0,
    )
    sub = iota((16, LANES), 0)
    cols = []
    for i, part in enumerate((quad, along, bend)):
        p0, p1, p2 = pieces(part)
        ones = jnp.where((sub < 9 + (i == 0)) & (lax.rem(sub, 3) == i), 1.0, 0.0)
        cols.append(jnp.concatenate([p0, p1, p2, p0, p1, p0, ones], axis=0).astype(BF16))
    return jnp.concatenate(cols, axis=1)


def far_product(side, picked):
    a0, a1, a2, rest = picked[0:16], picked[16:32], picked[32:48], picked[48:64]
    rest = jnp.where(iota((16, 64), 0) == 9, 1.0, rest)
    stack = jnp.concatenate([a0, a0, a0, a1, a1, a2, rest], axis=0).astype(BF16)
    return lax.dot_general(stack, side, (((0,), (0,)), ((), ())), preferred_element_type=F32)


def far_sums(both, picked, block):
    weights = [[], [], []]
    for c in range(4):
        rows = slice(16 * c, 16 * c + 16)
        inv = lax.rsqrt(both[rows, 0:LANES])
        inv2 = inv * inv
        inv3 = inv2 * inv
        inv5 = inv3 * inv2
        coef = (both[rows, LANES : 2 * LANES] + both[rows, 2 * LANES :] * inv2) * inv5
        for out, weight in zip(weights, (coef, inv3, inv5)):
            high = weight.astype(BF16)
            low = (weight - high.astype(F32)).astype(BF16)
            out.append(jnp.concatenate([high, low], axis=1))
    sub = iota((16, 64), 0)

    def lefts(part, one):
        first = jnp.where(sub < 3, part, jnp.where(sub == 3, one, 0.0))
        second = jnp.where((sub >= 10) & (sub < 13), pltpu.roll(part, 7, 0), 0.0)
        third = jnp.where(
            sub < 3,
            -pltpu.roll(part, 4, 0),
            jnp.where((sub >= 4) & (sub < 10), pltpu.roll(part, 14, 0), 0.0),
        )
        return first, second, third

    total = None
    for weight, high_l, low_l in zip(weights, lefts(picked[0:16], 1.0), lefts(picked[16:32], 0.0)):
        left = jnp.concatenate([high_l, low_l], axis=0).astype(BF16)
        part = jnp.dot(left, jnp.concatenate(weight, axis=0), preferred_element_type=F32)
        total = part if total is None else total + part
    got = (total[0:16, 0:LANES] + total[16:32, 0:LANES]) + total[0:16, LANES:]
    x = [block[d : d + 1] for d in range(3)]
    q = [got[4 + i : 5 + i] for i in range(6)]
    turn = [
        q[0] * x[0] + q[3] * x[1] + q[4] * x[2],
        q[3] * x[0] + q[1] * x[1] + q[5] * x[2],
        q[4] * x[0] + q[5] * x[1] + q[2] * x[2],
    ]
    return [
        3.0 * (x[d] * got[3:4] - got[d : d + 1] - turn[d]) - got[10 + d : 11 + d]
        for d in range(3)
    ]


def own_tile(pos_ref, mom_ref):
    pos = [pos_ref[k] for k in range(3)]
    mom = [mom_ref[k] for k in range(3)]
    cen = [jnp.sum(p, axis=1, keepdims=True) * (1.0 / LANES) for p in pos]
    tot = [jnp.sum(m, axis=1, keepdims=True) for m in mom]
    off = [pos[k] - cen[k] for k in range(3)]
    sec = [
        [jnp.sum(off[k] * mom[j], axis=1, keepdims=True) for j in range(3)] for k in range(3)
    ]
    full = lambda x: jnp.broadcast_to(x, (LEAVES, LANES)).reshape(PARENTS, 8, LANES)
    fcen = [full(c) for c in cen]
    ftot = [full(c) for c in tot]
    fsec = [[full(sec[k][j]) for j in range(3)] for k in range(3)]
    pcen = [jnp.sum(c, axis=1, keepdims=True) * 0.125 for c in fcen]
    ptot = [jnp.sum(c, axis=1) for c in ftot]
    psec = [
        [jnp.sum(fsec[k][j] + (fcen[k] - pcen[k]) * ftot[j], axis=1) for j in range(3)]
        for k in range(3)
    ]
    leaf = fcen + ftot + [fsec[k][j] for k in range(3) for j in range(3)]
    up = [c[:, 0, :] for c in pcen] + ptot + [psec[k][j] for k in range(3) for j in range(3)]
    lane = iota((LEAVES, LANES), 1)
    lane_p = iota((PARENTS, LANES), 1)
    rows = jnp.zeros((LEAVES, LANES), F32)
    rows_p = jnp.zeros((PARENTS, LANES), F32)
    for i in range(15):
        rows = jnp.where(lane == i, leaf[i].reshape(LEAVES, LANES), rows)
        rows_p = jnp.where(lane_p == i, up[i], rows_p)
    every = jnp.concatenate([rows, rows_p, jnp.zeros((LANES - OWN, LANES), F32)], axis=0)
    sums = [jnp.sum(p, axis=0, keepdims=True) for p in ptot]
    return jnp.transpose(every)[0:16], sums


def target_side(block, sub):
    cut = pieces(block)
    zero = jnp.zeros((16, LANES), F32)
    order = (0, 1, 2, 0, 1, 0)
    lead = (True, False, False, True, False, True)
    quad, along = [], []
    for p, flag in zip(order, lead):
        mark = 1.0 if flag else 0.0
        quad.append(jnp.where(sub < 3, -2.0 * cut[p], jnp.where(sub == 6, mark, 0.0)))
        turned = pltpu.roll(cut[p], 3, 0)
        along.append(
            jnp.where((sub >= 3) & (sub < 6), turned, jnp.where(sub == 7, -mark, 0.0))
        )
    quad.append(
        jnp.where(sub == 6, cut[0], jnp.where(sub == 7, pltpu.roll(cut[1], 1, 0), 0.0))
    )
    quad.append(jnp.where(sub == 6, cut[2], jnp.where(sub == 7, 1.0, 0.0)))
    along.append(zero)
    return jnp.concatenate(
        [jnp.concatenate(quad, axis=0), jnp.concatenate(along, axis=0)], axis=1
    ).astype(BF16)


def near_product(side, block):
    cut = pieces(block)
    source = jnp.concatenate(
        [cut[0], cut[0], cut[0], cut[1], cut[1], cut[2], jnp.ones((16, LANES), F32)], axis=0
    ).astype(BF16)
    return lax.dot_general(
        source, side, (((0,), (0,)), ((), ())), preferred_element_type=F32
    )


def near_sums(both, block, sub):
    parts = [[], [], [], []]
    for c in range(LANES // 16):
        quad = both[16 * c : 16 * c + 16, 0:LANES]
        along = both[16 * c : 16 * c + 16, LANES:]
        inv = lax.rsqrt(quad)
        inv2 = inv * inv
        inv3 = inv2 * inv
        coef = along * (inv3 * inv2)
        for i, weight in enumerate((coef, inv3)):
            high = weight.astype(BF16)
            parts[i].append(high)
            parts[2 + i].append((weight - high.astype(F32)).astype(BF16))
    high = jnp.concatenate(parts[0] + parts[1], axis=0)
    low = jnp.concatenate(parts[2] + parts[3], axis=0)

    def sums(part, one):
        c_side = jnp.where(sub < 3, part, jnp.where(sub == 6, one, 0.0))
        w_side = jnp.where((sub >= 3) & (sub < 6), part, 0.0)
        return jnp.concatenate([c_side, w_side], axis=1)

    cut = pieces(block)
    left = jnp.concatenate([sums(cut[0], 1.0), sums(cut[1], 0.0)], axis=0).astype(BF16)
    got = jnp.dot(left, high, preferred_element_type=F32)
    more = jnp.dot(left, low, preferred_element_type=F32)
    return (got[0:8] + got[8:16]) + more[0:8]


def near_pass(steps, width, first, last, store, buf_a, buf_b):
    def both(then, now, write, read):
        parts = []
        for i in range(width + LEAD):
            if i < width:
                first(then, i, write)
            if i >= LEAD:
                parts.append(last(now, i - LEAD, read))
        store(now, parts)

    for i in range(width):
        first(0, i, buf_a)

    def body(i, carry):
        both(2 * i + 1, 2 * i, buf_b, buf_a)
        both(jnp.minimum(2 * i + 2, steps - 1), 2 * i + 1, buf_a, buf_b)
        return carry

    lax.fori_loop(0, steps // 2, body, 0)


def exchange_kernel(
    pos_in, mom_in, fl_in, fn_in, fc_in, llist_in, llen_in, clist_in, clen_in, lens_in,
    pool_ref, sides, near, far_ref, parts_ref, list_out,
    pos_ref, mom_ref, fl_ref, fn_ref, fc_ref, llist_ref, llen_ref, clist_ref, clen_ref, in_sem,
    list_vec, lens_vec, key_rows, list_ref, list_sem,
    split, feats, index, cindex, gath, fsides, buf_a, buf_b, far_a, far_b, pick_a, pick_b, kept_a, kept_b,
    send_l, recv_l, send_c, recv_c, sl_sem, rl_sem, sc_sem, rc_sem,
):
    loads = [
        pltpu.make_async_copy(src, dst, in_sem.at[i])
        for i, (src, dst) in enumerate(
            (
                (pos_in, pos_ref), (mom_in, mom_ref), (fl_in, fl_ref), (fn_in, fn_ref),
                (fc_in, fc_ref), (llist_in, llist_ref), (llen_in, llen_ref),
                (clist_in, clist_ref), (clen_in, clen_ref),
                (llist_in, list_vec), (lens_in, lens_vec),
            )
        )
    ]
    for load in loads:
        load.start()
    me = lax.axis_index("dom")
    partners = []
    for b in range(SECTIONS):
        stride = 1 << b
        partners.append(me + (1 - 2 * lax.rem(me // stride, 2)) * stride)
    barrier = pltpu.get_barrier_semaphore()
    for other in partners:
        pl.semaphore_signal(
            barrier, inc=1, device_id=(other,), device_id_type=pl.DeviceIdType.MESH
        )
    for load in loads:
        load.wait()
    for d in range(3):
        pool_ref[0:LEAVES, d, :] = pos_ref[d]
        pool_ref[0:LEAVES, 3 + d, :] = mom_ref[d]

    lane = iota((8, LANES), 1)
    sub = iota((8, LANES), 0)
    index[...] = jnp.full((16, LANES), -1, jnp.int32)
    for b in range(SECTIONS):
        index[b : b + 1, 0:CELL_SENDS] = fc_ref[b]
    raw = index[...]
    index[...] = jnp.where(raw < OWN, raw, raw + (LANES - OWN))
    for half in range(2):
        rows = clist_ref[half * 32 : half * 32 + 32, :]
        cindex[:, half * 64 : half * 64 + 64] = jnp.where(
            rows < OWN, rows, rows + (LANES - OWN)
        )

    def leaf_copy(b):
        return pltpu.make_async_remote_copy(
            src_ref=send_l.at[b], dst_ref=recv_l.at[b],
            send_sem=sl_sem.at[b], recv_sem=rl_sem.at[b],
            device_id=(partners[b],), device_id_type=pl.DeviceIdType.MESH,
        )

    def cell_copy(b):
        return pltpu.make_async_remote_copy(
            src_ref=send_c.at[b], dst_ref=recv_c.at[b],
            send_sem=sc_sem.at[b], recv_sem=rc_sem.at[b],
            device_id=(partners[b],), device_id_type=pl.DeviceIdType.MESH,
        )

    def send_leaves(b):
        live = fn_ref[0, 1, b]
        for s in range(LEAF_SENDS):
            block = pool_ref[fl_ref[b, 0, s]][0:6]
            send_l[b, 6 * s : 6 * s + 6, :] = jnp.where(s < live, block, 0.0)
        leaf_copy(b).start()

    def take_tile(tile, at, ref, rows):
        if at % 2:
            kept = ref[:, at // 2 * LANES : at // 2 * LANES + LANES]
            turned = pltpu.roll(rows.astype(F32), CELL_SENDS, 1).astype(BF16)
            wide = iota(rows.shape, 1)
            rows = jnp.where(wide < CELL_SENDS, kept.astype(F32), turned.astype(F32)).astype(BF16)
        ref[:, at // 2 * LANES : at // 2 * LANES + LANES] = rows

    def take_split(tile, at):
        take_tile(tile, at, split, jnp.concatenate(pieces(tile), axis=0).astype(BF16))

    def take_features(tile, at):
        take_tile(tile, at, feats, cell_features(tile))

    def send_cells(b, msum):
        depth = LANES * ((b + 3) // 2)
        wanted = jnp.where(lane[0:1] < fn_ref[0, 0, b], index[b : b + 1, :], -1)
        hot = jnp.where(iota((depth, LANES), 0) == wanted, 1.0, 0.0).astype(BF16)
        got = jnp.dot(split[:, 0:depth], hot, preferred_element_type=F32)
        got = (got[0:16] + got[16:32]) + got[32:48]
        low = jnp.where(sub == 7, msum, got[8:16])
        send_c[b] = jnp.where(lane < CELL_SENDS, got[0:8], pltpu.roll(low, CELL_SENDS, 1))
        cell_copy(b).start()

    def finish_leaves(first, count):
        part = [pool_ref[first : first + count, i, :] for i in range(6)]
        pool_ref[first : first + count, 6, :] = (
            part[0] * part[0] + part[1] * part[1] + part[2] * part[2]
        )
        pool_ref[first : first + count, 7, :] = (
            part[0] * part[3] + part[1] * part[4] + part[2] * part[5]
        )

    def prepare_near(g, carry):
        for i in range(2):
            t = 2 * g + i
            sides[t] = target_side(pool_ref[t], sub)
        return carry

    def prepare_far(g, carry):
        for i in range(2):
            t = 2 * g + i
            fsides[t] = far_side(pool_ref[t])
        return carry

    def sort_list():
        slots = list_vec[...]
        place = iota((8, LEAVES), 0)
        leaf = iota((8, LEAVES), 1)
        live = (place >= 2) & (lens_vec[...] > place)
        section = jnp.zeros((8, LEAVES), jnp.int32)
        for b in range(SECTIONS):
            section = section + jnp.where(slots >= held(b), 1, 0)
        key = jnp.where(live, section, 16) * 512 + place * LEAVES + leaf
        key = key.astype(F32)
        for i in range(3):
            key_rows[i : i + 1, 0:LEAVES] = key[2 + i : 3 + i]
            key_rows[i : i + 1, LEAVES:] = key[5 + i : 6 + i]
        source = jnp.where(live, slots + 1, 0).astype(F32)
        both = jnp.concatenate([key, source], axis=0)
        both = jnp.concatenate([both, jnp.zeros((16, LANES - LEAVES), F32)], axis=1)
        turned = jnp.transpose(jnp.concatenate([both, jnp.zeros((LANES - 16, LANES), F32)], axis=0))
        own = iota((LEAVES, LANES), 0).astype(F32)
        spot = iota((LEAVES, LANES), 1).astype(F32)
        got_t = [jnp.zeros((LEAVES, LANES), F32) for _ in range(3)]
        got_s = [jnp.zeros((LEAVES, LANES), F32) for _ in range(3)]
        for k in range(2, 8):
            mine = jnp.broadcast_to(turned[0:LEAVES, k : k + 1], (LEAVES, LANES))
            src = jnp.broadcast_to(turned[0:LEAVES, 8 + k : 9 + k], (LEAVES, LANES))
            below = jnp.zeros((LEAVES, LANES), F32)
            for i in range(3):
                below = below + jnp.where(key_rows[i : i + 1, :] < mine, 1.0, 0.0)
            rank = jnp.sum(below, axis=1, keepdims=True)
            for m in range(3):
                here = rank == spot + float(LANES * m)
                got_t[m] = got_t[m] + jnp.where(here, own, 0.0)
                got_s[m] = got_s[m] + jnp.where(here, src, 0.0)
        counts = jnp.zeros((1, LANES), F32)
        for i, b in enumerate([stage[2] for stage in STAGES] + [SECTIONS]):
            ready = jnp.where(live & (slots < held(b)), 1.0, 0.0)
            number = jnp.sum(jnp.sum(ready, axis=1, keepdims=True), axis=0, keepdims=True)
            counts = jnp.where(lane[0:1] == i, number, counts)
        list_out[...] = jnp.zeros((8, ENTRIES), jnp.int32)
        for m in range(3):
            cols = slice(LANES * m, LANES * m + LANES)
            list_out[0:1, cols] = jnp.sum(got_t[m], axis=0, keepdims=True).astype(jnp.int32)
            list_out[1:2, cols] = jnp.sum(got_s[m], axis=0, keepdims=True).astype(jnp.int32)
        list_out[2:3, 0:LANES] = counts.astype(jnp.int32)

    list_copy = pltpu.make_async_copy(list_out, list_ref, list_sem)

    def near_source(t, k):
        if k == 0:
            return pool_ref[t]
        return jnp.where(llen_ref[t] > 1, pool_ref[llist_ref[1, t]], 0.0)

    def near_steps(t0, leaves):
        def spot(g, i):
            return t0 + 4 * g + i // 2, i % 2

        def first(g, i, buf):
            t, k = spot(g, i)
            buf[i] = near_product(sides[t], near_source(t, k))

        def last(g, i, buf):
            return near_sums(buf.at[i], near_source(*spot(g, i)), sub)

        def store(g, parts):
            for i in range(4):
                near[t0 + 4 * g + i] = parts[2 * i] + parts[2 * i + 1]

        near_pass(leaves // 4, 8, first, last, store, buf_a, buf_b)

    def near_listed(n0, count, b):
        def block(g, i):
            src = list_ref[1, n0 + 8 * g + i]
            use = (src > 0) & (src <= held(b))
            return jnp.where(use, pool_ref[jnp.clip(src - 1, 0, LEAF_POOL - 1)], 0.0)

        def first(g, i, buf):
            t = jnp.clip(list_ref[0, n0 + 8 * g + i], 0, LEAVES - 1)
            buf[i] = near_product(sides[t], block(g, i))

        def last(g, i, buf):
            return near_sums(buf.at[i], block(g, i), sub)

        def store(g, parts):
            for i in range(8):
                parts_ref[n0 + 8 * g + i] = parts[i]

        near_pass(count // 8, 8, first, last, store, buf_a, buf_b)

    def wanted_cells(i):
        row = cindex[pl.ds(i, 1), :]
        k = jnp.where(lane[0:1] < 64, lane[0:1], lane[0:1] - 64)
        most = jnp.where(lane[0:1] < 64, clen_ref[i], clen_ref[i + 32])
        return jnp.where(k < most, row, -1)

    old = LANES + (SECTIONS - 1) * CELL_SENDS

    def gather(low, high):
        def body(g, carry):
            for j in range(4):
                i = 4 * g + j
                spot = iota((high - low, LANES), 0) + low
                hot = jnp.where(spot == wanted_cells(i), 1.0, 0.0).astype(BF16)
                got = jnp.dot(feats[:, low:high], hot, preferred_element_type=F32)
                gath[i] = got if low == 0 else gath[i] + got
            return carry

        lax.fori_loop(0, 8, body, 0)

    def far_pick(g, j, buf):
        i = FAR_UNROLL * g + j
        hot = jnp.where(iota((64, LANES), 0) + old == wanted_cells(i), 1.0, 0.0).astype(BF16)
        picked = gath[i] + jnp.dot(feats[:, old : old + 64], hot, preferred_element_type=F32)
        buf[2 * j] = picked
        buf[2 * j + 1] = pltpu.roll(picked, 64, 1)

    def far_middle(g, j, read, buf):
        both, kept = buf
        for h in range(2):
            part = read[2 * j + h]
            kept[2 * j + h] = part[0:32]
            both[2 * j + h] = far_product(fsides[FAR_UNROLL * g + j + 32 * h], part[:, 0:64])

    def far_last(g, j, buf):
        i = FAR_UNROLL * g + j
        both, kept = buf
        return [
            far_sums(both.at[2 * j + h], kept[2 * j + h][:, 0:64], pool_ref[i + 32 * h])
            for h in range(2)
        ]

    def far_store(g, parts, unif):
        for j in range(FAR_UNROLL):
            for half in range(2):
                t = FAR_UNROLL * g + j + 32 * half
                for d in range(3):
                    far_ref[d, pl.ds(t, 1), :] = parts[j][half][d] + unif[d]

    def beside(b):
        if b == 0:
            sort_list()
            list_copy.start()
            lax.fori_loop(0, LEAVES // 2, prepare_near, 0)
            list_copy.wait()
        elif b == 1:
            near_steps(0, 16)
        elif b == 2:
            near_steps(16, 16)
        elif b == 3:
            near_steps(32, 32)
        elif b == 4:
            lax.fori_loop(0, LEAVES // 2, prepare_far, 0)
        elif b == 5:
            gather(0, 384)
        for n0, count, when in STAGES:
            if b == when:
                near_listed(n0, count, b)
        if b == SECTIONS - 1:
            gather(384, old)

    pl.semaphore_wait(barrier, SECTIONS)
    send_leaves(0)
    tile, sums = own_tile(pos_ref, mom_ref)
    msum = jnp.zeros((8, LANES), F32)
    for j in range(3):
        msum = jnp.where((sub == 7) & (lane == j), sums[j], msum)
    take_split(tile, 0)
    send_cells(0, msum)
    finish_leaves(0, LEAVES)
    take_features(tile, 0)
    beside(0)
    for b in range(SECTIONS):
        first = LEAVES + b * LEAF_SENDS
        leaf_copy(b).wait_recv()
        for s in range(LEAF_SENDS):
            pool_ref[first + s, 0:6, :] = recv_l[b, 6 * s : 6 * s + 6, :]
        if b + 1 < SECTIONS:
            send_leaves(b + 1)
        cell_copy(b).wait_recv()
        got = recv_c[b]
        low = jnp.where(lane < CELL_SENDS, pltpu.roll(got, CELL_SENDS, 1), 0.0)
        high = jnp.where(lane < CELL_SENDS, got, 0.0)
        tile = jnp.concatenate([high, low], axis=0)
        msum = msum + jnp.where(sub == 7, low, 0.0)
        if b + 1 < SECTIONS:
            take_split(tile, b + 2)
            send_cells(b + 1, msum)
        take_features(tile, b + 2)
        finish_leaves(first, LEAF_SENDS)
        if b + 1 < SECTIONS:
            beside(b + 1)
    scaled = msum * (-DEMAG / (N_DOM * LEAVES))
    unif = [jnp.broadcast_to(scaled[7:8, j : j + 1], (1, LANES)) for j in range(3)]
    steps = 32 // FAR_UNROLL
    capped = lambda g: jnp.minimum(g, steps - 1)

    def far_round(g, pick_w, pick_r, far_w, far_r):
        parts = []
        for j in range(FAR_UNROLL):
            far_pick(capped(g + 2), j, pick_w)
            far_middle(capped(g + 1), j, pick_r, far_w)
            parts.append(far_last(g, j, far_r))
        far_store(g, parts, unif)

    for j in range(FAR_UNROLL):
        far_pick(0, j, pick_a)
        far_pick(1, j, pick_b)
    for j in range(FAR_UNROLL):
        far_middle(0, j, pick_a, (far_a, kept_a))

    def far_body(i, carry):
        far_round(2 * i, pick_a, pick_b, (far_b, kept_b), (far_a, kept_a))
        far_round(2 * i + 1, pick_b, pick_a, (far_a, kept_a), (far_b, kept_b))
        return carry

    lax.fori_loop(0, steps // 2, far_body, 0)
    for b in range(SECTIONS):
        leaf_copy(b).wait_send()
        cell_copy(b).wait_send()


def exchange(
    positions, moments, fwd_leaves, fwd_counts, fwd_cells, leaf_list, leaf_len, cell_list, cell_len
):
    vmem = pl.BlockSpec(memory_space=pltpu.VMEM)
    hbm = pl.BlockSpec(memory_space=pltpu.MemorySpace.HBM)
    dma = pltpu.SemaphoreType.DMA((SECTIONS,))
    return pl.pallas_call(
        exchange_kernel,
        out_shape=(
            jax.ShapeDtypeStruct((LEAF_POOL, 8, LANES), F32),
            jax.ShapeDtypeStruct((LEAVES, 64, 2 * LANES), BF16),
            jax.ShapeDtypeStruct((LEAVES, 8, LANES), F32),
            jax.ShapeDtypeStruct((3, LEAVES, LANES), F32),
            jax.ShapeDtypeStruct((DONE, 8, LANES), F32),
            jax.ShapeDtypeStruct((8, ENTRIES), jnp.int32),
        ),
        in_specs=[hbm] * 10,
        out_specs=(vmem,) * 6,
        scratch_shapes=[
            pltpu.VMEM((3, LEAVES, LANES), F32),
            pltpu.VMEM((3, LEAVES, LANES), F32),
            pltpu.SMEM((SECTIONS, 1, LEAF_SENDS), jnp.int32),
            pltpu.SMEM((1, 2, SECTIONS), jnp.int32),
            pltpu.VMEM((SECTIONS, 1, CELL_SENDS), jnp.int32),
            pltpu.SMEM((8, LEAVES), jnp.int32),
            pltpu.SMEM((LEAVES,), jnp.int32),
            pltpu.VMEM((LEAVES, 64), jnp.int32),
            pltpu.SMEM((LEAVES,), jnp.int32),
            pltpu.SemaphoreType.DMA((11,)),
            pltpu.VMEM((8, LEAVES), jnp.int32),
            pltpu.VMEM((1, LEAVES), jnp.int32),
            pltpu.VMEM((8, LANES), F32),
            pltpu.SMEM((8, ENTRIES), jnp.int32),
            pltpu.SemaphoreType.DMA,
            pltpu.VMEM((48, WIDE + 64), BF16),
            pltpu.VMEM((64, WIDE + 64), BF16),
            pltpu.VMEM((16, LANES), jnp.int32),
            pltpu.VMEM((32, LANES), jnp.int32),
            pltpu.VMEM((32, 64, LANES), F32),
            pltpu.VMEM((LEAVES, 112, 3 * LANES), BF16),
            pltpu.VMEM((8, LANES, 2 * LANES), F32),
            pltpu.VMEM((8, LANES, 2 * LANES), F32),
            pltpu.VMEM((2 * FAR_UNROLL, 64, 3 * LANES), F32),
            pltpu.VMEM((2 * FAR_UNROLL, 64, 3 * LANES), F32),
            pltpu.VMEM((2 * FAR_UNROLL, 64, LANES), F32),
            pltpu.VMEM((2 * FAR_UNROLL, 64, LANES), F32),
            pltpu.VMEM((2 * FAR_UNROLL, 32, LANES), F32),
            pltpu.VMEM((2 * FAR_UNROLL, 32, LANES), F32),
            pltpu.VMEM((SECTIONS, 6 * LEAF_SENDS, LANES), F32),
            pltpu.VMEM((SECTIONS, 6 * LEAF_SENDS, LANES), F32),
            pltpu.VMEM((SECTIONS, 8, LANES), F32),
            pltpu.VMEM((SECTIONS, 8, LANES), F32),
            dma, dma, dma, dma,
        ],
        compiler_params=pltpu.CompilerParams(
            collective_id=0, has_side_effects=True, vmem_limit_bytes=40 * 1024 * 1024
        ),
        name="exchange",
    )(
        *(
            pltpu.with_memory_space_constraint(x, pltpu.MemorySpace.HBM)
            for x in (
                positions, moments, fwd_leaves, fwd_counts, fwd_cells,
                leaf_list, leaf_len, cell_list, cell_len, leaf_len.reshape(1, LEAVES),
            )
        )
    )


def field_kernel(
    pool_ref, sides, near0, far_ref, parts_ref, list_ref, out_ref, near, more, buf_a, buf_b
):
    sub = iota((8, LANES), 0)
    total = list_ref[2, len(STAGES)]
    more[...] = jnp.zeros_like(more)

    def add_parts(g, carry):
        for i in range(4):
            more[i, jnp.clip(list_ref[0, 4 * g + i], 0, LEAVES - 1)] += parts_ref[4 * g + i]
        return carry

    lax.fori_loop(0, (jnp.clip(total, 0, DONE) + 3) // 4, add_parts, 0)
    near[0:LEAVES] = near0[...] + ((more[0] + more[1]) + (more[2] + more[3]))

    def settle(n):
        for i, (n0, count, _) in enumerate(STAGES):
            ready = jnp.clip(list_ref[2, i] - n0, 0, count)
            n = jnp.where(n == n0, n0 + ready, n)
        return n

    def near_items(n):
        todo = []
        for _ in range(NEAR_UNROLL):
            here = jnp.clip(n, 0, ENTRIES - 1)
            t = jnp.clip(list_ref[0, here], 0, LEAVES - 1)
            live = n < total
            src = jnp.clip(list_ref[1, here] - 1, 0, LEAF_POOL - 1)
            todo += [jnp.where(live, t, LEAVES), t, src]
            n = settle(n + 1)
        return n, tuple(todo)

    def near_both(then, now, write, read):
        parts = []
        for i in range(NEAR_UNROLL):
            write[i] = near_product(sides[then[3 * i + 1]], pool_ref[then[3 * i + 2]])
            parts.append(near_sums(read.at[i], pool_ref[now[3 * i + 2]], sub))
        for i in range(NEAR_UNROLL):
            near[now[3 * i]] += parts[i]

    def near_body(carry):
        n, now, then = carry
        n, later = near_items(n)
        near_both(then, now, buf_b, buf_a)
        n, last = near_items(n)
        near_both(later, then, buf_a, buf_b)
        return n, later, last

    n, now = near_items(settle(jnp.int32(0)))
    n, then = near_items(n)

    @pl.when(now[0] < LEAVES)
    def _():
        for i in range(NEAR_UNROLL):
            buf_a[i] = near_product(sides[now[3 * i + 1]], pool_ref[now[3 * i + 2]])
        lax.while_loop(lambda carry: carry[1][0] < LEAVES, near_body, (n, now, then))

    for d in range(3):
        close = pool_ref[0:LEAVES, d, :] * near[0:LEAVES, 6, :] - near[0:LEAVES, d, :]
        out_ref[d] = 3.0 * close - near[0:LEAVES, 3 + d, :] + far_ref[d]


def field(pool, sides, near, far, parts, lists):
    vmem = pl.BlockSpec(memory_space=pltpu.VMEM)
    smem = pl.BlockSpec(memory_space=pltpu.SMEM)
    return pl.pallas_call(
        field_kernel,
        out_shape=jax.ShapeDtypeStruct((3, LEAVES, LANES), F32),
        in_specs=[vmem, vmem, vmem, vmem, vmem, smem],
        out_specs=vmem,
        scratch_shapes=[
            pltpu.VMEM((LEAVES + 1, 8, LANES), F32),
            pltpu.VMEM((4, LEAVES, 8, LANES), F32),
            pltpu.VMEM((NEAR_UNROLL, LANES, 2 * LANES), F32),
            pltpu.VMEM((NEAR_UNROLL, LANES, 2 * LANES), F32),
        ],
        compiler_params=pltpu.CompilerParams(vmem_limit_bytes=16 * 1024 * 1024),
        name="field",
    )(pool, sides, near, far, parts, lists)


def per_device(
    positions, moments, fwd_cells, fwd_leaves, fwd_counts, cell_list, cell_len, leaf_list, leaf_len
):
    swap = lambda x: jnp.transpose(x, (1, 0, 2))
    pool, sides, near, far, parts, lists = exchange(
        swap(positions), swap(moments), swap(fwd_leaves), jnp.transpose(fwd_counts, (0, 2, 1)),
        swap(fwd_cells), leaf_list.T, leaf_len, cell_list, cell_len,
    )
    return swap(field(pool, sides, near, far, parts, lists))


def solution(mesh):
    row = P("dom", None)
    cube = P("dom", None, None)
    return jax.shard_map(
        per_device,
        mesh=mesh,
        in_specs=(cube, cube, cube, cube, cube, row, P("dom"), row, P("dom")),
        out_specs=cube,
        check_vma=False,
    )
```

```python
import functools

import jax
import jax.numpy as jnp
from jax import lax
from jax.experimental import pallas as pl
from jax.experimental.pallas import tpu as pltpu
from jax.sharding import PartitionSpec as P

F32 = jnp.float32
BF16 = jnp.bfloat16
DEMAG = 4.1887902047863905
LEAVES = 64
PARENTS = 8
OWN = LEAVES + PARENTS
SECTIONS = 9
CELL_SENDS = 64
LEAF_SENDS = 20
LEAF_POOL = LEAVES + SECTIONS * LEAF_SENDS
WIDE = 128 + SECTIONS * CELL_SENDS
LANES = 128
N_DOM = 512
NEAR_UNROLL = 8
LEAD = 3
ENTRIES = 6 * LEAVES
EARLY = ((0, 32, 1), (32, 32, 2))
EARLY_DONE = 64
STAGES = ((0, 64, 6), (64, 32, 7), (96, 32, 8))
DONE = STAGES[-1][0] + STAGES[-1][1] + EARLY_DONE


def held(b):
    return LEAVES + b * LEAF_SENDS
FAR_UNROLL = 4


def iota(shape, dim):
    return lax.broadcasted_iota(jnp.int32, shape, dim)


def pieces(x):
    first = x.astype(BF16).astype(F32)
    rest = x - first
    second = rest.astype(BF16).astype(F32)
    return first, second, rest - second


def cell_features(tile):
    row = lambda i: tile[i : i + 1]
    sec = lambda k, j: row(6 + 3 * k + j)
    c = [row(d) for d in range(3)]
    tot = [row(3 + d) for d in range(3)]
    xx, yy, zz = [2.0 * sec(d, d) for d in range(3)]
    xy, xz, yz = sec(0, 1) + sec(1, 0), sec(0, 2) + sec(2, 0), sec(1, 2) + sec(2, 1)
    turn = [
        xx * c[0] + xy * c[1] + xz * c[2],
        xy * c[0] + yy * c[1] + yz * c[2],
        xz * c[0] + yz * c[1] + zz * c[2],
    ]
    main = jnp.concatenate(
        [tile[0:6], xx, yy, zz, xy, xz, yz] + turn + [jnp.ones((1, LANES), F32)], axis=0
    )
    rest = jnp.concatenate(
        [
            c[0] * c[0] + c[1] * c[1] + c[2] * c[2],
            -(tot[0] * c[0] + tot[1] * c[1] + tot[2] * c[2])
            - (sec(0, 0) + sec(1, 1) + sec(2, 2)),
            2.5 * (c[0] * turn[0] + c[1] * turn[1] + c[2] * turn[2]),
        ],
        axis=0,
    )
    blocks = list(pieces(main)) + list(pieces(rest)) + [jnp.zeros((7, LANES), F32)]
    return jnp.concatenate(blocks, axis=0).astype(BF16)


def far_side(block):
    x = [block[d : d + 1] for d in range(3)]
    none = lambda n: jnp.zeros((n, LANES), F32)
    x3 = block[0:3]
    quad = jnp.concatenate([-2.0 * x3, none(12), block[6:7]], axis=0)
    along = jnp.concatenate([none(3), x3, none(10)], axis=0)
    bend = jnp.concatenate(
        [
            none(6), 2.5 * (x[0] * x[0]), 2.5 * (x[1] * x[1]), 2.5 * (x[2] * x[2]),
            5.0 * (x[0] * x[1]), 5.0 * (x[0] * x[2]), 5.0 * (x[1] * x[2]),
            -5.0 * x3, none(1),
        ],
        axis=0,
    )
    sub = iota((16, LANES), 0)
    cols = []
    for i, part in enumerate((quad, along, bend)):
        p0, p1, p2 = pieces(part)
        ones = jnp.where((sub < 9 + (i == 0)) & (lax.rem(sub, 3) == i), 1.0, 0.0)
        cols.append(jnp.concatenate([p0, p1, p2, p0, p1, p0, ones], axis=0).astype(BF16))
    return jnp.concatenate(cols, axis=1)


def far_product(side, picked):
    a0, a1, a2, rest = picked[0:16], picked[16:32], picked[32:48], picked[48:64]
    rest = jnp.where(iota((16, 64), 0) == 9, 1.0, rest)
    stack = jnp.concatenate([a0, a0, a0, a1, a1, a2, rest], axis=0).astype(BF16)
    return lax.dot_general(stack, side, (((0,), (0,)), ((), ())), preferred_element_type=F32)


def far_sums(both, picked, block):
    weights = [[], [], []]
    for c in range(4):
        rows = slice(16 * c, 16 * c + 16)
        inv = lax.rsqrt(both[rows, 0:LANES])
        inv2 = inv * inv
        inv3 = inv2 * inv
        inv5 = inv3 * inv2
        coef = (both[rows, LANES : 2 * LANES] + both[rows, 2 * LANES :] * inv2) * inv5
        for out, weight in zip(weights, (coef, inv3, inv5)):
            high = weight.astype(BF16)
            low = (weight - high.astype(F32)).astype(BF16)
            out.append(jnp.concatenate([high, low], axis=1))
    sub = iota((16, 64), 0)

    def lefts(part, one):
        first = jnp.where(sub < 3, part, jnp.where(sub == 3, one, 0.0))
        second = jnp.where((sub >= 10) & (sub < 13), pltpu.roll(part, 7, 0), 0.0)
        third = jnp.where(
            sub < 3,
            -pltpu.roll(part, 4, 0),
            jnp.where((sub >= 4) & (sub < 10), pltpu.roll(part, 14, 0), 0.0),
        )
        return first, second, third

    total = None
    for weight, high_l, low_l in zip(weights, lefts(picked[0:16], 1.0), lefts(picked[16:32], 0.0)):
        left = jnp.concatenate([high_l, low_l], axis=0).astype(BF16)
        part = jnp.dot(left, jnp.concatenate(weight, axis=0), preferred_element_type=F32)
        total = part if total is None else total + part
    got = (total[0:16, 0:LANES] + total[16:32, 0:LANES]) + total[0:16, LANES:]
    x = [block[d : d + 1] for d in range(3)]
    q = [got[4 + i : 5 + i] for i in range(6)]
    turn = [
        q[0] * x[0] + q[3] * x[1] + q[4] * x[2],
        q[3] * x[0] + q[1] * x[1] + q[5] * x[2],
        q[4] * x[0] + q[5] * x[1] + q[2] * x[2],
    ]
    return [
        3.0 * (x[d] * got[3:4] - got[d : d + 1] - turn[d]) - got[10 + d : 11 + d]
        for d in range(3)
    ]


def own_tile(pos_ref, mom_ref):
    pos = [pos_ref[k] for k in range(3)]
    mom = [mom_ref[k] for k in range(3)]
    cen = [jnp.sum(p, axis=1, keepdims=True) * (1.0 / LANES) for p in pos]
    tot = [jnp.sum(m, axis=1, keepdims=True) for m in mom]
    off = [pos[k] - cen[k] for k in range(3)]
    sec = [
        [jnp.sum(off[k] * mom[j], axis=1, keepdims=True) for j in range(3)] for k in range(3)
    ]
    full = lambda x: jnp.broadcast_to(x, (LEAVES, LANES)).reshape(PARENTS, 8, LANES)
    fcen = [full(c) for c in cen]
    ftot = [full(c) for c in tot]
    fsec = [[full(sec[k][j]) for j in range(3)] for k in range(3)]
    pcen = [jnp.sum(c, axis=1, keepdims=True) * 0.125 for c in fcen]
    ptot = [jnp.sum(c, axis=1) for c in ftot]
    psec = [
        [jnp.sum(fsec[k][j] + (fcen[k] - pcen[k]) * ftot[j], axis=1) for j in range(3)]
        for k in range(3)
    ]
    leaf = fcen + ftot + [fsec[k][j] for k in range(3) for j in range(3)]
    up = [c[:, 0, :] for c in pcen] + ptot + [psec[k][j] for k in range(3) for j in range(3)]
    lane = iota((LEAVES, LANES), 1)
    lane_p = iota((PARENTS, LANES), 1)
    rows = jnp.zeros((LEAVES, LANES), F32)
    rows_p = jnp.zeros((PARENTS, LANES), F32)
    for i in range(15):
        rows = jnp.where(lane == i, leaf[i].reshape(LEAVES, LANES), rows)
        rows_p = jnp.where(lane_p == i, up[i], rows_p)
    every = jnp.concatenate([rows, rows_p, jnp.zeros((LANES - OWN, LANES), F32)], axis=0)
    sums = [jnp.sum(p, axis=0, keepdims=True) for p in ptot]
    return jnp.transpose(every)[0:16], sums


def target_side(block, sub):
    cut = pieces(block)
    zero = jnp.zeros((16, LANES), F32)
    order = (0, 1, 2, 0, 1, 0)
    lead = (True, False, False, True, False, True)
    quad, along = [], []
    for p, flag in zip(order, lead):
        mark = 1.0 if flag else 0.0
        quad.append(jnp.where(sub < 3, -2.0 * cut[p], jnp.where(sub == 6, mark, 0.0)))
        turned = pltpu.roll(cut[p], 3, 0)
        along.append(
            jnp.where((sub >= 3) & (sub < 6), turned, jnp.where(sub == 7, -mark, 0.0))
        )
    quad.append(
        jnp.where(sub == 6, cut[0], jnp.where(sub == 7, pltpu.roll(cut[1], 1, 0), 0.0))
    )
    quad.append(jnp.where(sub == 6, cut[2], jnp.where(sub == 7, 1.0, 0.0)))
    along.append(zero)
    return jnp.concatenate(
        [jnp.concatenate(quad, axis=0), jnp.concatenate(along, axis=0)], axis=1
    ).astype(BF16)


def near_product(side, block):
    cut = pieces(block)
    source = jnp.concatenate(
        [cut[0], cut[0], cut[0], cut[1], cut[1], cut[2], jnp.ones((16, LANES), F32)], axis=0
    ).astype(BF16)
    return lax.dot_general(
        source, side, (((0,), (0,)), ((), ())), preferred_element_type=F32
    )


def near_sums(both, block, sub):
    parts = [[], [], [], []]
    for c in range(LANES // 16):
        quad = both[16 * c : 16 * c + 16, 0:LANES]
        along = both[16 * c : 16 * c + 16, LANES:]
        inv = lax.rsqrt(quad)
        inv2 = inv * inv
        inv3 = inv2 * inv
        coef = along * (inv3 * inv2)
        for i, weight in enumerate((coef, inv3)):
            high = weight.astype(BF16)
            parts[i].append(high)
            parts[2 + i].append((weight - high.astype(F32)).astype(BF16))
    high = jnp.concatenate(parts[0] + parts[1], axis=0)
    low = jnp.concatenate(parts[2] + parts[3], axis=0)

    def sums(part, one):
        c_side = jnp.where(sub < 3, part, jnp.where(sub == 6, one, 0.0))
        w_side = jnp.where((sub >= 3) & (sub < 6), part, 0.0)
        return jnp.concatenate([c_side, w_side], axis=1)

    cut = pieces(block)
    left = jnp.concatenate([sums(cut[0], 1.0), sums(cut[1], 0.0)], axis=0).astype(BF16)
    got = jnp.dot(left, high, preferred_element_type=F32)
    more = jnp.dot(left, low, preferred_element_type=F32)
    return (got[0:8] + got[8:16]) + more[0:8]


def near_pass(steps, width, first, last, store, buf_a, buf_b):
    def both(then, now, write, read):
        parts = []
        for i in range(width + LEAD):
            if i < width:
                first(then, i, write)
            if i >= LEAD:
                parts.append(last(now, i - LEAD, read))
        store(now, parts)

    for i in range(width):
        first(0, i, buf_a)

    def body(i, carry):
        both(2 * i + 1, 2 * i, buf_b, buf_a)
        both(jnp.minimum(2 * i + 2, steps - 1), 2 * i + 1, buf_a, buf_b)
        return carry

    lax.fori_loop(0, steps // 2, body, 0)


def exchange_kernel(
    pos_in, mom_in, fl_in, fn_in, fc_in, llist_in, llen_in, clist_in, clen_in, lens_in,
    pool_ref, sides, near, far_ref, parts_ref, list_out,
    pos_ref, mom_ref, fl_ref, fn_ref, fc_ref, llist_ref, llen_ref, clist_ref, clen_ref, in_sem,
    list_vec, lens_vec, key_rows, list_ref, list_sem,
    split, feats, index, cindex, gath, fsides, buf_a, buf_b, far_a, far_b, pick_a, pick_b, kept_a, kept_b,
    send_l, recv_l, send_c, recv_c, sl_sem, rl_sem, sc_sem, rc_sem,
):
    loads = [
        pltpu.make_async_copy(src, dst, in_sem.at[i])
        for i, (src, dst) in enumerate(
            (
                (pos_in, pos_ref), (mom_in, mom_ref), (fl_in, fl_ref), (fn_in, fn_ref),
                (fc_in, fc_ref), (llist_in, llist_ref), (llen_in, llen_ref),
                (clist_in, clist_ref), (clen_in, clen_ref),
                (llist_in, list_vec), (lens_in, lens_vec),
            )
        )
    ]
    for load in loads:
        load.start()
    me = lax.axis_index("dom")
    core = lax.rem(me, 2)
    base = EARLY_DONE * (1 - core)
    partners = []
    for b in range(SECTIONS):
        stride = 1 << b
        partners.append(me + (1 - 2 * lax.rem(me // stride, 2)) * stride)
    barrier = pltpu.get_barrier_semaphore()
    for other in partners:
        pl.semaphore_signal(
            barrier, inc=1, device_id=(other,), device_id_type=pl.DeviceIdType.MESH
        )
    for load in loads:
        load.wait()
    for d in range(3):
        pool_ref[0:LEAVES, d, :] = pos_ref[d]
        pool_ref[0:LEAVES, 3 + d, :] = mom_ref[d]

    lane = iota((8, LANES), 1)
    sub = iota((8, LANES), 0)
    index[...] = jnp.full((16, LANES), -1, jnp.int32)
    for b in range(SECTIONS):
        index[b : b + 1, 0:CELL_SENDS] = fc_ref[b]
    raw = index[...]
    index[...] = jnp.where(raw < OWN, raw, raw + (LANES - OWN))
    for half in range(2):
        rows = clist_ref[half * 32 : half * 32 + 32, :]
        cindex[:, half * 64 : half * 64 + 64] = jnp.where(
            rows < OWN, rows, rows + (LANES - OWN)
        )

    def leaf_copy(b):
        return pltpu.make_async_remote_copy(
            src_ref=send_l.at[b], dst_ref=recv_l.at[b],
            send_sem=sl_sem.at[b], recv_sem=rl_sem.at[b],
            device_id=(partners[b],), device_id_type=pl.DeviceIdType.MESH,
        )

    def cell_copy(b):
        return pltpu.make_async_remote_copy(
            src_ref=send_c.at[b], dst_ref=recv_c.at[b],
            send_sem=sc_sem.at[b], recv_sem=rc_sem.at[b],
            device_id=(partners[b],), device_id_type=pl.DeviceIdType.MESH,
        )

    def send_leaves(b):
        live = fn_ref[0, 1, b]
        for s in range(LEAF_SENDS):
            block = pool_ref[fl_ref[b, 0, s]][0:6]
            send_l[b, 6 * s : 6 * s + 6, :] = jnp.where(s < live, block, 0.0)
        leaf_copy(b).start()

    def take_tile(tile, at, ref, rows):
        if at % 2:
            kept = ref[:, at // 2 * LANES : at // 2 * LANES + LANES]
            turned = pltpu.roll(rows.astype(F32), CELL_SENDS, 1).astype(BF16)
            wide = iota(rows.shape, 1)
            rows = jnp.where(wide < CELL_SENDS, kept.astype(F32), turned.astype(F32)).astype(BF16)
        ref[:, at // 2 * LANES : at // 2 * LANES + LANES] = rows

    def take_split(tile, at):
        take_tile(tile, at, split, jnp.concatenate(pieces(tile), axis=0).astype(BF16))

    def take_features(tile, at):
        take_tile(tile, at, feats, cell_features(tile))

    def send_cells(b, msum):
        depth = LANES * ((b + 3) // 2)
        wanted = jnp.where(lane[0:1] < fn_ref[0, 0, b], index[b : b + 1, :], -1)
        hot = jnp.where(iota((depth, LANES), 0) == wanted, 1.0, 0.0).astype(BF16)
        got = jnp.dot(split[:, 0:depth], hot, preferred_element_type=F32)
        got = (got[0:16] + got[16:32]) + got[32:48]
        low = jnp.where(sub == 7, msum, got[8:16])
        send_c[b] = jnp.where(lane < CELL_SENDS, got[0:8], pltpu.roll(low, CELL_SENDS, 1))
        cell_copy(b).start()

    def finish_leaves(first, count):
        part = [pool_ref[first : first + count, i, :] for i in range(6)]
        pool_ref[first : first + count, 6, :] = (
            part[0] * part[0] + part[1] * part[1] + part[2] * part[2]
        )
        pool_ref[first : first + count, 7, :] = (
            part[0] * part[3] + part[1] * part[4] + part[2] * part[5]
        )

    def prepare_near(g, carry):
        for i in range(2):
            t = 2 * g + i
            sides[t] = target_side(pool_ref[t], sub)
        return carry

    def prepare_far(g, carry):
        for i in range(2):
            t = 2 * g + i
            fsides[t] = far_side(pool_ref[t])
        return carry

    def sort_list():
        slots = list_vec[...]
        place = iota((8, LEAVES), 0)
        leaf = iota((8, LEAVES), 1)
        live = (place >= 2) & (lens_vec[...] > place)
        section = jnp.zeros((8, LEAVES), jnp.int32)
        for b in range(SECTIONS):
            section = section + jnp.where(slots >= held(b), 1, 0)
        key = jnp.where(live, section, 16) * 512 + place * LEAVES + leaf
        key = key.astype(F32)
        for i in range(3):
            key_rows[i : i + 1, 0:LEAVES] = key[2 + i : 3 + i]
            key_rows[i : i + 1, LEAVES:] = key[5 + i : 6 + i]
        source = jnp.where(live, slots + 1, 0).astype(F32)
        both = jnp.concatenate([key, source], axis=0)
        both = jnp.concatenate([both, jnp.zeros((16, LANES - LEAVES), F32)], axis=1)
        turned = jnp.transpose(jnp.concatenate([both, jnp.zeros((LANES - 16, LANES), F32)], axis=0))
        own = iota((LEAVES, LANES), 0).astype(F32)
        spot = iota((LEAVES, LANES), 1).astype(F32)
        got_t = [jnp.zeros((LEAVES, LANES), F32) for _ in range(3)]
        got_s = [jnp.zeros((LEAVES, LANES), F32) for _ in range(3)]
        for k in range(2, 8):
            mine = jnp.broadcast_to(turned[0:LEAVES, k : k + 1], (LEAVES, LANES))
            src = jnp.broadcast_to(turned[0:LEAVES, 8 + k : 9 + k], (LEAVES, LANES))
            below = jnp.zeros((LEAVES, LANES), F32)
            for i in range(3):
                below = below + jnp.where(key_rows[i : i + 1, :] < mine, 1.0, 0.0)
            rank = jnp.sum(below, axis=1, keepdims=True)
            for m in range(3):
                here = rank == spot + float(LANES * m)
                got_t[m] = got_t[m] + jnp.where(here, own, 0.0)
                got_s[m] = got_s[m] + jnp.where(here, src, 0.0)
        counts = jnp.zeros((1, LANES), F32)
        for i, b in enumerate([stage[2] for stage in EARLY + STAGES] + [SECTIONS]):
            ready = jnp.where(live & (slots < held(b)), 1.0, 0.0)
            number = jnp.sum(jnp.sum(ready, axis=1, keepdims=True), axis=0, keepdims=True)
            counts = jnp.where(lane[0:1] == i, number, counts)
        counts = jnp.where(lane[0:1] == 6, jnp.where(core == 0, float(EARLY_DONE), 0.0), counts)
        list_out[...] = jnp.zeros((8, ENTRIES), jnp.int32)
        for m in range(3):
            cols = slice(LANES * m, LANES * m + LANES)
            list_out[0:1, cols] = jnp.sum(got_t[m], axis=0, keepdims=True).astype(jnp.int32)
            list_out[1:2, cols] = jnp.sum(got_s[m], axis=0, keepdims=True).astype(jnp.int32)
        list_out[2:3, 0:LANES] = counts.astype(jnp.int32)

    list_copy = pltpu.make_async_copy(list_out, list_ref, list_sem)

    def near_source(t, k):
        if k == 0:
            return pool_ref[t]
        return jnp.where(llen_ref[t] > 1, pool_ref[llist_ref[1, t]], 0.0)

    def near_steps(t0, leaves):
        def spot(g, i):
            return t0 + 4 * g + i // 2, i % 2

        def first(g, i, buf):
            t, k = spot(g, i)
            buf[i] = near_product(sides[t], near_source(t, k))

        def last(g, i, buf):
            return near_sums(buf.at[i], near_source(*spot(g, i)), sub)

        def store(g, parts):
            for i in range(4):
                near[t0 + 4 * g + i] = parts[2 * i] + parts[2 * i + 1]

        near_pass(leaves // 4, 8, first, last, store, buf_a, buf_b)

    def near_listed(n0, count, b):
        def block(g, i):
            src = list_ref[1, n0 + 8 * g + i]
            use = (src > 0) & (src <= held(b))
            return jnp.where(use, pool_ref[jnp.clip(src - 1, 0, LEAF_POOL - 1)], 0.0)

        def first(g, i, buf):
            t = jnp.clip(list_ref[0, n0 + 8 * g + i], 0, LEAVES - 1)
            buf[i] = near_product(sides[t], block(g, i))

        def last(g, i, buf):
            return near_sums(buf.at[i], block(g, i), sub)

        def store(g, parts):
            for i in range(8):
                parts_ref[n0 + 8 * g + i] = parts[i]

        near_pass(count // 8, 8, first, last, store, buf_a, buf_b)

    def wanted_cells(i):
        row = cindex[pl.ds(i, 1), :]
        k = jnp.where(lane[0:1] < 64, lane[0:1], lane[0:1] - 64)
        most = jnp.where(lane[0:1] < 64, clen_ref[i], clen_ref[i + 32])
        return jnp.where(k < most, row, -1)

    old = LANES + (SECTIONS - 1) * CELL_SENDS

    def gather(low, high):
        def body(g, carry):
            for j in range(4):
                i = 4 * g + j
                spot = iota((high - low, LANES), 0) + low
                hot = jnp.where(spot == wanted_cells(i), 1.0, 0.0).astype(BF16)
                got = jnp.dot(feats[:, low:high], hot, preferred_element_type=F32)
                gath[i] = got if low == 0 else gath[i] + got
            return carry

        lax.fori_loop(0, 8, body, 0)

    def far_pick(g, j, buf):
        i = FAR_UNROLL * g + j
        hot = jnp.where(iota((64, LANES), 0) + old == wanted_cells(i), 1.0, 0.0).astype(BF16)
        picked = gath[i] + jnp.dot(feats[:, old : old + 64], hot, preferred_element_type=F32)
        buf[2 * j] = picked
        buf[2 * j + 1] = pltpu.roll(picked, 64, 1)

    def far_middle(g, j, read, buf):
        both, kept = buf
        for h in range(2):
            part = read[2 * j + h]
            kept[2 * j + h] = part[0:32]
            both[2 * j + h] = far_product(fsides[FAR_UNROLL * g + j + 32 * h], part[:, 0:64])

    def far_last(g, j, buf):
        i = FAR_UNROLL * g + j
        both, kept = buf
        return [
            far_sums(both.at[2 * j + h], kept[2 * j + h][:, 0:64], pool_ref[i + 32 * h])
            for h in range(2)
        ]

    def far_store(g, parts, unif):
        for j in range(FAR_UNROLL):
            for half in range(2):
                t = FAR_UNROLL * g + j + 32 * half
                for d in range(3):
                    far_ref[d, pl.ds(t, 1), :] = parts[j][half][d] + unif[d]

    def beside(b):
        if b == 0:
            sort_list()
            list_copy.start()
            lax.fori_loop(0, LEAVES // 2 * core, prepare_near, 0)
            list_copy.wait()
        elif b < 3:

            @pl.when(core == 0)
            def _():
                near_listed(EARLY[b - 1][0], EARLY[b - 1][1], b)

            @pl.when(core == 1)
            def _():
                near_steps(16 * (b - 1), 16)

        elif b == 3:
            near_steps(32, 32)
        elif b == 4:
            lax.fori_loop(0, LEAVES // 2, prepare_far, 0)
        elif b == 5:
            gather(0, 384)
        for n0, count, when in STAGES:
            if b == when:
                near_listed(base + n0, count, b)
        if b == SECTIONS - 1:
            gather(384, old)

    @pl.when(core == 0)
    def _():
        finish_leaves(0, LEAVES)
        lax.fori_loop(0, LEAVES // 2, prepare_near, 0)
        near_steps(0, 32)

    pl.semaphore_wait(barrier, SECTIONS)
    send_leaves(0)
    tile, sums = own_tile(pos_ref, mom_ref)
    msum = jnp.zeros((8, LANES), F32)
    for j in range(3):
        msum = jnp.where((sub == 7) & (lane == j), sums[j], msum)
    take_split(tile, 0)
    send_cells(0, msum)
    finish_leaves(0, LEAVES)
    take_features(tile, 0)
    beside(0)
    for b in range(SECTIONS):
        first = LEAVES + b * LEAF_SENDS
        leaf_copy(b).wait_recv()
        for s in range(LEAF_SENDS):
            pool_ref[first + s, 0:6, :] = recv_l[b, 6 * s : 6 * s + 6, :]
        if b + 1 < SECTIONS:
            send_leaves(b + 1)
        cell_copy(b).wait_recv()
        got = recv_c[b]
        low = jnp.where(lane < CELL_SENDS, pltpu.roll(got, CELL_SENDS, 1), 0.0)
        high = jnp.where(lane < CELL_SENDS, got, 0.0)
        tile = jnp.concatenate([high, low], axis=0)
        msum = msum + jnp.where(sub == 7, low, 0.0)
        if b + 1 < SECTIONS:
            take_split(tile, b + 2)
            send_cells(b + 1, msum)
        take_features(tile, b + 2)
        finish_leaves(first, LEAF_SENDS)
        if b + 1 < SECTIONS:
            beside(b + 1)
    scaled = msum * (-DEMAG / (N_DOM * LEAVES))
    unif = [jnp.broadcast_to(scaled[7:8, j : j + 1], (1, LANES)) for j in range(3)]
    steps = 32 // FAR_UNROLL
    capped = lambda g: jnp.minimum(g, steps - 1)

    def far_round(g, pick_w, pick_r, far_w, far_r):
        parts = []
        for j in range(FAR_UNROLL):
            far_pick(capped(g + 2), j, pick_w)
            far_middle(capped(g + 1), j, pick_r, far_w)
            parts.append(far_last(g, j, far_r))
        far_store(g, parts, unif)

    for j in range(FAR_UNROLL):
        far_pick(0, j, pick_a)
        far_pick(1, j, pick_b)
    for j in range(FAR_UNROLL):
        far_middle(0, j, pick_a, (far_a, kept_a))

    def far_body(i, carry):
        far_round(2 * i, pick_a, pick_b, (far_b, kept_b), (far_a, kept_a))
        far_round(2 * i + 1, pick_b, pick_a, (far_a, kept_a), (far_b, kept_b))
        return carry

    lax.fori_loop(0, steps // 2, far_body, 0)
    for b in range(SECTIONS):
        leaf_copy(b).wait_send()
        cell_copy(b).wait_send()


def exchange(
    positions, moments, fwd_leaves, fwd_counts, fwd_cells, leaf_list, leaf_len, cell_list, cell_len
):
    vmem = pl.BlockSpec(memory_space=pltpu.VMEM)
    hbm = pl.BlockSpec(memory_space=pltpu.MemorySpace.HBM)
    dma = pltpu.SemaphoreType.DMA((SECTIONS,))
    return pl.pallas_call(
        exchange_kernel,
        out_shape=(
            jax.ShapeDtypeStruct((LEAF_POOL, 8, LANES), F32),
            jax.ShapeDtypeStruct((LEAVES, 64, 2 * LANES), BF16),
            jax.ShapeDtypeStruct((LEAVES, 8, LANES), F32),
            jax.ShapeDtypeStruct((3, LEAVES, LANES), F32),
            jax.ShapeDtypeStruct((DONE, 8, LANES), F32),
            jax.ShapeDtypeStruct((8, ENTRIES), jnp.int32),
        ),
        in_specs=[hbm] * 10,
        out_specs=(vmem,) * 6,
        scratch_shapes=[
            pltpu.VMEM((3, LEAVES, LANES), F32),
            pltpu.VMEM((3, LEAVES, LANES), F32),
            pltpu.SMEM((SECTIONS, 1, LEAF_SENDS), jnp.int32),
            pltpu.SMEM((1, 2, SECTIONS), jnp.int32),
            pltpu.VMEM((SECTIONS, 1, CELL_SENDS), jnp.int32),
            pltpu.SMEM((8, LEAVES), jnp.int32),
            pltpu.SMEM((LEAVES,), jnp.int32),
            pltpu.VMEM((LEAVES, 64), jnp.int32),
            pltpu.SMEM((LEAVES,), jnp.int32),
            pltpu.SemaphoreType.DMA((11,)),
            pltpu.VMEM((8, LEAVES), jnp.int32),
            pltpu.VMEM((1, LEAVES), jnp.int32),
            pltpu.VMEM((8, LANES), F32),
            pltpu.SMEM((8, ENTRIES), jnp.int32),
            pltpu.SemaphoreType.DMA,
            pltpu.VMEM((48, WIDE + 64), BF16),
            pltpu.VMEM((64, WIDE + 64), BF16),
            pltpu.VMEM((16, LANES), jnp.int32),
            pltpu.VMEM((32, LANES), jnp.int32),
            pltpu.VMEM((32, 64, LANES), F32),
            pltpu.VMEM((LEAVES, 112, 3 * LANES), BF16),
            pltpu.VMEM((8, LANES, 2 * LANES), F32),
            pltpu.VMEM((8, LANES, 2 * LANES), F32),
            pltpu.VMEM((2 * FAR_UNROLL, 64, 3 * LANES), F32),
            pltpu.VMEM((2 * FAR_UNROLL, 64, 3 * LANES), F32),
            pltpu.VMEM((2 * FAR_UNROLL, 64, LANES), F32),
            pltpu.VMEM((2 * FAR_UNROLL, 64, LANES), F32),
            pltpu.VMEM((2 * FAR_UNROLL, 32, LANES), F32),
            pltpu.VMEM((2 * FAR_UNROLL, 32, LANES), F32),
            pltpu.VMEM((SECTIONS, 6 * LEAF_SENDS, LANES), F32),
            pltpu.VMEM((SECTIONS, 6 * LEAF_SENDS, LANES), F32),
            pltpu.VMEM((SECTIONS, 8, LANES), F32),
            pltpu.VMEM((SECTIONS, 8, LANES), F32),
            dma, dma, dma, dma,
        ],
        compiler_params=pltpu.CompilerParams(
            collective_id=0, has_side_effects=True, vmem_limit_bytes=40 * 1024 * 1024
        ),
        name="exchange",
    )(
        *(
            pltpu.with_memory_space_constraint(x, pltpu.MemorySpace.HBM)
            for x in (
                positions, moments, fwd_leaves, fwd_counts, fwd_cells,
                leaf_list, leaf_len, cell_list, cell_len, leaf_len.reshape(1, LEAVES),
            )
        )
    )


def field_kernel(
    pool_ref, sides, near0, far_ref, parts_ref, list_ref, out_ref, near, more, buf_a, buf_b
):
    sub = iota((8, LANES), 0)
    total = list_ref[2, 5]
    base = jnp.clip(list_ref[2, 6], 0, EARLY_DONE)
    more[...] = jnp.zeros_like(more)

    def add_parts(g, carry):
        for i in range(4):
            more[i, jnp.clip(list_ref[0, 4 * g + i], 0, LEAVES - 1)] += parts_ref[4 * g + i]
        return carry

    lax.fori_loop(0, (jnp.clip(total, 0, DONE - EARLY_DONE + base) + 3) // 4, add_parts, 0)
    near[0:LEAVES] = near0[...] + ((more[0] + more[1]) + (more[2] + more[3]))

    def settle(n):
        for i, (n0, count, _) in enumerate(EARLY + STAGES):
            if i < len(EARLY):
                count = jnp.where(base > 0, count, 0)
            else:
                n0 = n0 + base
            ready = jnp.clip(list_ref[2, i] - n0, 0, count)
            n = jnp.where(n == n0, n0 + ready, n)
        return n

    def near_items(n):
        todo = []
        for _ in range(NEAR_UNROLL):
            here = jnp.clip(n, 0, ENTRIES - 1)
            t = jnp.clip(list_ref[0, here], 0, LEAVES - 1)
            live = n < total
            src = jnp.clip(list_ref[1, here] - 1, 0, LEAF_POOL - 1)
            todo += [jnp.where(live, t, LEAVES), t, src]
            n = settle(n + 1)
        return n, tuple(todo)

    def near_both(then, now, write, read):
        parts = []
        for i in range(NEAR_UNROLL):
            write[i] = near_product(sides[then[3 * i + 1]], pool_ref[then[3 * i + 2]])
            parts.append(near_sums(read.at[i], pool_ref[now[3 * i + 2]], sub))
        for i in range(NEAR_UNROLL):
            near[now[3 * i]] += parts[i]

    def near_body(carry):
        n, now, then = carry
        n, later = near_items(n)
        near_both(then, now, buf_b, buf_a)
        n, last = near_items(n)
        near_both(later, then, buf_a, buf_b)
        return n, later, last

    n, now = near_items(settle(jnp.int32(0)))
    n, then = near_items(n)

    @pl.when(now[0] < LEAVES)
    def _():
        for i in range(NEAR_UNROLL):
            buf_a[i] = near_product(sides[now[3 * i + 1]], pool_ref[now[3 * i + 2]])
        lax.while_loop(lambda carry: carry[1][0] < LEAVES, near_body, (n, now, then))

    for d in range(3):
        close = pool_ref[0:LEAVES, d, :] * near[0:LEAVES, 6, :] - near[0:LEAVES, d, :]
        out_ref[d] = 3.0 * close - near[0:LEAVES, 3 + d, :] + far_ref[d]


def field(pool, sides, near, far, parts, lists):
    vmem = pl.BlockSpec(memory_space=pltpu.VMEM)
    smem = pl.BlockSpec(memory_space=pltpu.SMEM)
    return pl.pallas_call(
        field_kernel,
        out_shape=jax.ShapeDtypeStruct((3, LEAVES, LANES), F32),
        in_specs=[vmem, vmem, vmem, vmem, vmem, smem],
        out_specs=vmem,
        scratch_shapes=[
            pltpu.VMEM((LEAVES + 1, 8, LANES), F32),
            pltpu.VMEM((4, LEAVES, 8, LANES), F32),
            pltpu.VMEM((NEAR_UNROLL, LANES, 2 * LANES), F32),
            pltpu.VMEM((NEAR_UNROLL, LANES, 2 * LANES), F32),
        ],
        compiler_params=pltpu.CompilerParams(vmem_limit_bytes=16 * 1024 * 1024),
        name="field",
    )(pool, sides, near, far, parts, lists)


def per_device(
    positions, moments, fwd_cells, fwd_leaves, fwd_counts, cell_list, cell_len, leaf_list, leaf_len
):
    swap = lambda x: jnp.transpose(x, (1, 0, 2))
    pool, sides, near, far, parts, lists = exchange(
        swap(positions), swap(moments), swap(fwd_leaves), jnp.transpose(fwd_counts, (0, 2, 1)),
        swap(fwd_cells), leaf_list.T, leaf_len, cell_list, cell_len,
    )
    return swap(field(pool, sides, near, far, parts, lists))


def solution(mesh):
    row = P("dom", None)
    cube = P("dom", None, None)
    return jax.shard_map(
        per_device,
        mesh=mesh,
        in_specs=(cube, cube, cube, cube, cube, row, P("dom"), row, P("dom")),
        out_specs=cube,
        check_vma=False,
    )
```
